128 devices in a mesh: gx: 16 (over z, x), gy: 8 (over y, core).
Axes of the slice: x: 4, y: 4, z: 4, core: 2. Of those that a mesh axis runs over, the one named last changes fastest.
Arguments:
- coarse_state: float32 [5, 256, 128, 128], P(None, 'gx', 'gy'), may hold values from -0.64 to 4.4, as said below
- patch_state: float32 [16, 8, 4, 5, 32, 1024], P('gx', 'gy'), may hold values from -0.64 to 4.4, as said below
- patch_anchor: int32 [16, 8, 4, 3], P(None, 'gy'), may hold values from 0 to 240, as said below
- patch_count: int32 [16, 8], P(None, 'gy'), may hold values from 1 to 4, as said below
Outputs:
- coarse_next: float32 [5, 256, 128, 128], P(None, 'gx', 'gy')
- patch_next: float32 [16, 8, 4, 5, 32, 1024], P('gx', 'gy')
The draws below stay inside these ranges and needn't reach their ends.
Inputs may be any that keep to these rules, and one draw needn't show every extreme that they name: `coarse_state`: density and pressure of every cell lie in [0.625, 1.6] and each velocity component in [-0.4, 0.4]. `patch_state`: density and pressure of every cell lie in [0.625, 1.6] and each velocity component in [-0.4, 0.4]. `patch_anchor`: entry [o, r, s] is 0 for s >= patch_count[o, r]. A live patch of device (o, r) has its second component r * 16 and its first and third multiples of 16; its z block index (third component / 16) has the parity of the sum of its pencil's two indices, so no two patches share a face. Every pencil of 16 x 16 coarse columns holds exactly 2 patches, owned by devices of its own gy index, no two by the same device. `patch_count`: each gy index's counts sum to 2 * 16.
All inputs are finite; a program needn't handle non-finite values.
Results may differ from the reference program's by a relative error of at most 0.0003.
Values sent between devices are 32-bit elements; how exact they have to be, the bound alone decides.
A program may use at most 192 MiB of HBM per device.

```python
import jax
import jax.numpy as jnp
from jax import lax

FINE = 32
HALF = 16
DEPTH = 128
PER_PENCIL = 2
SLOTS = 4
RIEMANN = 2
NX = 256
NY = 128
N_GX = 16
N_GY = 8


def make_state(key, shape, axis):

    def rough_field(index):
        normal_part = jnp.clip(jax.random.normal(jax.random.fold_in(key, index), shape, jnp.float32), -1.8, 1.8) / 1.8
        return normal_part
    density = jnp.exp(0.47 * rough_field(0))
    pressure = jnp.exp(0.47 * rough_field(1))
    velocity = [0.4 * rough_field(2 + comp_index) for comp_index in range(3)]
    kinetic = 0.5 * density * (velocity[0] * velocity[0] + velocity[1] * velocity[1] + velocity[2] * velocity[2])
    energy = pressure / 0.4 + kinetic
    return jnp.stack([density, density * velocity[0], density * velocity[1], density * velocity[2], energy], axis=axis)


def draw_coarse_state(key, part):
    key = jax.random.fold_in(key, 11)
    return make_state(key, (NX, NY, DEPTH), 0)


def draw_patch_state(key, part):
    key = jax.random.fold_in(key, 12)
    shape = (NX // HALF, NY // HALF, SLOTS, FINE, FINE * FINE)
    return make_state(key, shape, 3)


def patch_lists(key):
    pencils = NX // HALF
    row_total = NY // HALF
    quarter = pencils // 4
    classes = DEPTH // HALF // 2
    owner_loads = jnp.concatenate([jnp.full((quarter,), 2 * PER_PENCIL, jnp.int32), jnp.full((quarter,), PER_PENCIL, jnp.int32), jnp.full((quarter,), PER_PENCIL - 1, jnp.int32), jnp.full((pencils - 3 * quarter,), 1, jnp.int32)])
    load_ends = jnp.cumsum(owner_loads)
    load_starts = load_ends - owner_loads
    entries = jnp.arange(PER_PENCIL * pencils, dtype=jnp.int32)
    entry_rank = jnp.sum((entries[:, None] >= load_ends[None, :]).astype(jnp.int32), axis=1)

    def class_order(pencil_key):
        return jax.random.permutation(pencil_key, classes - 1).astype(jnp.int32)

    def one_row(row_key, row_index):
        key_owner, key_pencil, key_depth = jax.random.split(row_key, 3)
        owner_of_rank = jax.random.permutation(key_owner, pencils).astype(jnp.int32)
        pencil_order = jax.random.permutation(key_pencil, pencils).astype(jnp.int32)
        owner_index = owner_of_rank[entry_rank]
        slot_place = entries - load_starts[entry_rank]
        pencil = pencil_order[entries % pencils]
        within = entries // pencils
        extras = jax.vmap(class_order)(jax.random.split(key_depth, pencils))
        chosen = jnp.concatenate([jnp.full((pencils, 1), classes - 1, jnp.int32), extras[:, :PER_PENCIL - 1]], axis=1)
        depth_class = chosen[pencil, within]
        parity = (pencil + row_index) % 2
        z_anchor = (2 * depth_class + parity) * HALF
        triple = jnp.stack([pencil * HALF, jnp.full_like(pencil, row_index * HALF), z_anchor], axis=1)
        anchor = jnp.zeros((pencils, SLOTS, 3), jnp.int32).at[owner_index, slot_place].set(triple)
        owner_count = jnp.zeros((pencils,), jnp.int32).at[owner_of_rank].set(owner_loads)
        return (anchor, owner_count)
    row_keys = jax.random.split(key, row_total)
    anchor, owner_count = jax.vmap(one_row)(row_keys, jnp.arange(row_total, dtype=jnp.int32))
    return (jnp.transpose(anchor, (1, 0, 2, 3)), jnp.transpose(owner_count))


def draw_patch_anchor(key, part):
    shared = patch_lists(key)
    return shared[0]


def draw_patch_count(key, part):
    shared = patch_lists(key)
    return shared[1]


def setup_inputs(seed: int = 0) -> dict:
    key_list = jax.random.split(jax.random.key(seed), 5)
    return {
        "coarse_state": draw_coarse_state(jax.random.fold_in(key_list[4], 71), 0),
        "patch_state": draw_patch_state(jax.random.fold_in(key_list[4], 71), 0),
        "patch_anchor": draw_patch_anchor(jax.random.fold_in(key_list[4], 71), 0),
        "patch_count": draw_patch_count(jax.random.fold_in(key_list[4], 71), 0),
    }


gamma_ratio = 1.4
courant = 0.12

def primitives(conserved):
    density = conserved[0]
    velocity = conserved[1:4] / density
    pressure = (gamma_ratio - 1.0) * (conserved[4] - 0.5 * density * lax.optimization_barrier(jnp.sum(velocity * velocity, axis=0)))
    return (density, velocity, pressure)

def physical_flux(conserved, velocity, pressure, normal):
    normal_speed = velocity[normal]
    pieces = [conserved[0] * normal_speed]
    for component in range(3):
        momentum_term = conserved[1 + component] * normal_speed
        if component == normal:
            momentum_term = momentum_term + pressure
        pieces.append(momentum_term)
    pieces.append((conserved[4] + pressure) * normal_speed)
    return jnp.stack(pieces)

def branch_terms(star_press, side_press, side_dens, side_sound):
    exponent = (gamma_ratio - 1.0) / (2.0 * gamma_ratio)
    coef_a = 2.0 / ((gamma_ratio + 1.0) * side_dens)
    coef_b = (gamma_ratio - 1.0) / (gamma_ratio + 1.0) * side_press
    root_term = jnp.sqrt(coef_a / (star_press + coef_b))
    shock_term = (star_press - side_press) * root_term
    shock_slope = root_term * (1.0 - 0.5 * (star_press - side_press) / (star_press + coef_b))
    press_ratio = star_press / side_press
    rarefy_term = 2.0 * side_sound / (gamma_ratio - 1.0) * (press_ratio ** exponent - 1.0)
    rarefy_slope = press_ratio ** (-(gamma_ratio + 1.0) / (2.0 * gamma_ratio)) / (side_dens * side_sound)
    compressed = star_press > side_press
    return (jnp.where(compressed, shock_term, rarefy_term), jnp.where(compressed, shock_slope, rarefy_slope))

def face_flux(lower_state, upper_state, normal):
    dens_left, vel_left, press_left = primitives(lower_state)
    dens_right, vel_right, press_right = primitives(upper_state)
    speed_left = vel_left[normal]
    speed_right = vel_right[normal]
    sound_left = jnp.sqrt(gamma_ratio * press_left / dens_left)
    sound_right = jnp.sqrt(gamma_ratio * press_right / dens_right)
    exponent = (gamma_ratio - 1.0) / (2.0 * gamma_ratio)
    star_press = ((sound_left + sound_right - 0.5 * (gamma_ratio - 1.0) * (speed_right - speed_left)) / (sound_left * press_left ** (-exponent) + sound_right * press_right ** (-exponent))) ** (1.0 / exponent)
    for newton_step in range(RIEMANN):
        value_left, slope_left = branch_terms(star_press, press_left, dens_left, sound_left)
        value_right, slope_right = branch_terms(star_press, press_right, dens_right, sound_right)
        star_press = star_press - (value_left + value_right + speed_right - speed_left) / (slope_left + slope_right)
    factor = (gamma_ratio + 1.0) / (2.0 * gamma_ratio)
    lift_left = jnp.where(star_press > press_left, jnp.sqrt(1.0 + factor * (star_press / press_left - 1.0)), 1.0)
    lift_right = jnp.where(star_press > press_right, jnp.sqrt(1.0 + factor * (star_press / press_right - 1.0)), 1.0)
    wave_low = speed_left - sound_left * lift_left
    wave_high = speed_right + sound_right * lift_right
    flux_left = physical_flux(lower_state, vel_left, press_left, normal)
    flux_right = physical_flux(upper_state, vel_right, press_right, normal)
    blended = (wave_high * flux_left - wave_low * flux_right + wave_low * wave_high * (upper_state - lower_state)) / (wave_high - wave_low)
    return jnp.where(wave_low >= 0.0, flux_left, jnp.where(wave_high <= 0.0, flux_right, blended))

def coarsen(fine_faces):
    fine_cells = fine_faces.shape[-1]
    half_cells = fine_cells // 2
    shaped = fine_faces.reshape(fine_faces.shape[:-2] + (half_cells, 2, half_cells, 2))
    return lax.optimization_barrier(jnp.sum(shaped, axis=(-3, -1)))

def advance(one_patch, one_shell):
    fine_cells = one_patch.shape[1]
    half_cells = fine_cells // 2
    padded_side = fine_cells + 2
    plane_size = padded_side * padded_side
    block_cells = one_patch.reshape(5, fine_cells, fine_cells, fine_cells)
    shell_faces = one_shell.reshape(5, 6, half_cells, half_cells)
    refined = jnp.repeat(jnp.repeat(shell_faces, 2, axis=2), 2, axis=3)
    padded = jnp.pad(block_cells, ((0, 0), (1, 1), (1, 1), (1, 1)), mode='edge')
    padded = padded.at[:, 0, 1:-1, 1:-1].set(refined[:, 0])
    padded = padded.at[:, -1, 1:-1, 1:-1].set(refined[:, 1])
    padded = padded.at[:, 1:-1, 0, 1:-1].set(refined[:, 2])
    padded = padded.at[:, 1:-1, -1, 1:-1].set(refined[:, 3])
    padded = padded.at[:, 1:-1, 1:-1, 0].set(refined[:, 4])
    padded = padded.at[:, 1:-1, 1:-1, -1].set(refined[:, 5])
    flattened = padded.reshape(5, padded_side, plane_size)
    flux_x = face_flux(flattened[:, :-1], flattened[:, 1:], 0)
    flux_y = face_flux(flattened[:, :, :-padded_side], flattened[:, :, padded_side:], 1)
    flux_z = face_flux(flattened[:, :, :-1], flattened[:, :, 1:], 2)
    full_x = jnp.concatenate([flux_x, jnp.zeros((5, 1, plane_size), flux_x.dtype)], axis=1)
    full_y = jnp.concatenate([flux_y, jnp.zeros((5, padded_side, padded_side), flux_y.dtype)], axis=2)
    full_z = jnp.concatenate([flux_z, jnp.zeros((5, padded_side, 1), flux_z.dtype)], axis=2)
    change = full_x - jnp.roll(full_x, 1, axis=1) + (full_y - jnp.roll(full_y, padded_side, axis=2)) + (full_z - jnp.roll(full_z, 1, axis=2))
    change_cells = change.reshape(5, padded_side, padded_side, padded_side)[:, 1:-1, 1:-1, 1:-1]
    updated = block_cells - courant * change_cells
    cube_x = full_x.reshape(5, padded_side, padded_side, padded_side)
    cube_y = full_y.reshape(5, padded_side, padded_side, padded_side)
    cube_z = full_z.reshape(5, padded_side, padded_side, padded_side)
    boundary = jnp.stack([cube_x[:, 0, 1:-1, 1:-1], cube_x[:, fine_cells, 1:-1, 1:-1], cube_y[:, 1:-1, 0, 1:-1], cube_y[:, 1:-1, fine_cells, 1:-1], cube_z[:, 1:-1, 1:-1, 0], cube_z[:, 1:-1, 1:-1, fine_cells]], axis=1)
    return (updated.reshape(5, fine_cells, fine_cells * fine_cells), boundary)

def coarse_fluxes(field):
    flux_x = face_flux(field, jnp.roll(field, -1, axis=1), 0)
    flux_y = face_flux(field, jnp.roll(field, -1, axis=2), 1)
    flux_z = face_flux(field, jnp.roll(field, -1, axis=3), 2)
    change = flux_x - jnp.roll(flux_x, 1, axis=1) + (flux_y - jnp.roll(flux_y, 1, axis=2)) + (flux_z - jnp.roll(flux_z, 1, axis=3))
    return (flux_x, flux_y, flux_z, field - courant * change)

def six_faces(field_x, field_y, field_z, anchor, upper):
    x_first = anchor[0]
    y_first = anchor[1]
    z_first = anchor[2]
    span = jnp.arange(HALF, dtype=jnp.int32)
    x_cells = (x_first + span) % NX
    y_cells = (y_first + span) % NY
    z_cells = (z_first + span) % DEPTH

    def x_face(position):
        return field_x[:, position % NX][:, y_cells][:, :, z_cells]

    def y_face(position):
        return field_y[:, :, position % NY][:, x_cells][:, :, z_cells]

    def z_face(position):
        return field_z[:, :, :, position % DEPTH][:, x_cells][:, :, y_cells]
    return jnp.stack([x_face(x_first - 1), x_face(x_first + upper), y_face(y_first - 1), y_face(y_first + upper), z_face(z_first - 1), z_face(z_first + upper)], axis=1)

def add_faces(field, anchor, delta):
    x_first = anchor[0]
    y_first = anchor[1]
    z_first = anchor[2]
    span = jnp.arange(HALF, dtype=jnp.int32)
    first_grid = jnp.broadcast_to(span[:, None], (HALF, HALF))
    second_grid = jnp.broadcast_to(span[None, :], (HALF, HALF))
    x_tan = (x_first + first_grid) % NX
    y_tan_first = (y_first + first_grid) % NY
    y_tan_second = (y_first + second_grid) % NY
    z_tan = (z_first + second_grid) % DEPTH
    field = field.at[:, jnp.full_like(first_grid, (x_first - 1) % NX), y_tan_first, z_tan].add(delta[:, 0])
    field = field.at[:, jnp.full_like(first_grid, (x_first + HALF) % NX), y_tan_first, z_tan].add(delta[:, 1])
    field = field.at[:, x_tan, jnp.full_like(first_grid, (y_first - 1) % NY), z_tan].add(delta[:, 2])
    field = field.at[:, x_tan, jnp.full_like(first_grid, (y_first + HALF) % NY), z_tan].add(delta[:, 3])
    field = field.at[:, x_tan, y_tan_second, jnp.full_like(first_grid, (z_first - 1) % DEPTH)].add(delta[:, 4])
    field = field.at[:, x_tan, y_tan_second, jnp.full_like(first_grid, (z_first + HALF) % DEPTH)].add(delta[:, 5])
    return field

def reference(coarse_state, patch_state, patch_anchor, patch_count):
    flux_x, flux_y, flux_z, advanced = coarse_fluxes(coarse_state)
    slot_count = N_GX * N_GY * SLOTS
    patches = patch_state.reshape(slot_count, 5, FINE, FINE * FINE)
    anchors = patch_anchor.reshape(slot_count, 3)
    active_slots = (jnp.arange(SLOTS, dtype=jnp.int32)[None, None, :] < patch_count[:, :, None]).reshape(slot_count)
    signs = jnp.array([1.0, -1.0, 1.0, -1.0, 1.0, -1.0], dtype=jnp.float32)[None, :, None, None]

    def advance_one(inputs):
        one_patch, anchor, active = inputs

        def work(operand):
            old_shell = six_faces(coarse_state, coarse_state, coarse_state, anchor, HALF).reshape(5, 6 * HALF * HALF)
            new_shell = six_faces(advanced, advanced, advanced, anchor, HALF).reshape(5, 6 * HALF * HALF)
            first_step, faces_one = advance(one_patch, old_shell)
            second, faces_two = advance(first_step, 0.5 * (old_shell + new_shell))
            fine_mean = 0.125 * (coarsen(faces_one) + coarsen(faces_two))
            coarse_faces = six_faces(flux_x, flux_y, flux_z, anchor, HALF - 1)
            return (second, courant * signs * (coarse_faces - fine_mean))

        def unchanged(operand):
            return (one_patch, jnp.zeros((5, 6, HALF, HALF), one_patch.dtype))
        return lax.cond(active, work, unchanged, 0)
    results, deltas = lax.map(advance_one, (patches, anchors, active_slots))

    def add_one(slot_index, field):
        return add_faces(field, anchors[slot_index], deltas[slot_index])
    coarse_next = lax.fori_loop(0, slot_count, add_one, advanced)
    return (coarse_next, results.reshape(patch_state.shape))
```

```python
import jax
import jax.numpy as jnp
from jax import lax
from jax.experimental import pallas as pl
from jax.experimental.pallas import tpu as pltpu
from jax.sharding import PartitionSpec as P

COURANT = 0.12
VMEM_LIMIT = 56 * 1024 * 1024
F32 = jnp.float32


def rcp(x):
    return pl.reciprocal(x, approx=True)


def root(x):
    return x * lax.rsqrt(x)


def primitives(U):
    r = rcp(U[0])
    u, v, w = U[1] * r, U[2] * r, U[3] * r
    p = 0.4 * (U[4] - 0.5 * (U[1] * u + U[2] * v + U[3] * w))
    c5 = root((35.0 * p) * r)
    cg5 = c5 * jnp.exp2(jnp.log2(p) * (-1.0 / 7.0))
    sa = root(r * (1.0 / 1.2))
    return [u, v, w, p, c5, cg5, sa]


def newton(s, z, scaled, L, R, du):
    value, slope = du, None
    for p6, p7, c5, cg5, sa in (L, R):
        t = s + p6
        q = lax.rsqrt(t)
        rt = sa * q
        d = t - p7
        shock = d * rt
        shock_slope = rt * (1.0 + p7 * (q * q))
        rare = cg5 * z - c5
        rare_slope = cg5 * scaled
        up = d > 0.0
        value = value + jnp.where(up, shock, rare)
        term = jnp.where(up, shock_slope, rare_slope)
        slope = term if slope is None else slope + term
    return s - (value + value) * rcp(slope)


def face_flux(UL, QL, UR, QR, n, keep=None):
    uL, pL, c5L, cg5L, saL = QL[n], QL[3], QL[4], QL[5], QL[6]
    uR, pR, c5R, cg5R, saR = QR[n], QR[3], QR[4], QR[5], QR[6]
    du = uR - uL
    L = (pL * (1.0 / 6.0), pL * (7.0 / 6.0), c5L, cg5L, saL)
    R = (pR * (1.0 / 6.0), pR * (7.0 / 6.0), c5R, cg5R, saR)
    z = (c5L + c5R - du) * rcp(cg5L + cg5R)
    z2 = z * z
    z6 = z2 * z2 * z2
    s = newton(z6 * z, z, (2.0 / 7.0) * rcp(z6), L, R, du)
    z = jnp.exp2(jnp.log2(s) * (1.0 / 7.0))
    s = newton(s, z, (2.0 / 7.0) * z * rcp(s), L, R, du)
    waves = []
    for c5, sa in ((c5L, saL), (c5R, saR)):
        cc = c5 * c5
        waves.append(0.2 * root(jnp.maximum(cc, (cc + (252.0 * s) * (sa * sa)) * (1.0 / 7.0))))
    low = jnp.minimum(uL - waves[0], 0.0)
    high = jnp.maximum(uR + waves[1], 0.0)
    inv = rcp(high - low)
    if keep is not None:
        inv = jnp.where(keep, inv, 0.0)
    wL, wR = high * inv, low * inv
    a, b = wL * (uL - low), wR * (high - uR)
    eL, eR = wL * pL, wR * pR
    F = [a * UL[i] + b * UR[i] for i in range(5)]
    F[1 + n] = F[1 + n] + (eL - eR)
    F[4] = F[4] + (eL * uL - eR * uR)
    return F


def roll(x, by, axis):
    by = by % x.shape[axis]
    return x if by == 0 else pltpu.roll(x, by, axis)


def lanes(shape):
    return lax.broadcasted_iota(jnp.int32, shape, len(shape) - 1)


def block_transpose(vs, width):
    n = len(vs)
    block = lanes(vs[0].shape) // width
    vs = list(vs)
    d = n // 2
    while d:
        low = (block & d) == 0
        for i in range(n):
            if i & d == 0:
                a, b = vs[i], vs[i + d]
                vs[i] = jnp.where(low, a, roll(b, d * width, 1))
                vs[i + d] = jnp.where(low, roll(a, -d * width, 1), b)
        d //= 2
    return vs


def pick(x, index):
    return jnp.take_along_axis(x, index, axis=1)


NORMAL = (2, 2, 0, 0, 1, 1)


def fine_load(patch, W, Q):
    def body(yg, _):
        at = pl.ds(pl.multiple_of(yg * 128, 128), 128)
        U = [[None] * 5 for _ in range(4)]
        for c in range(5):
            vs = block_transpose([patch[s, c, :, at] for s in range(4)], 32)
            for j in range(4):
                W[c, 4 * yg + j] = vs[j]
                U[j][c] = vs[j]
        for j in range(4):
            for k, q in enumerate(primitives(U[j])):
                Q[k, 4 * yg + j] = q
        return 0

    lax.fori_loop(0, 8, body, 0)


def fine_interior(W, Q, FY, B):
    shape = (32, 128)
    row = lax.broadcasted_iota(jnp.int32, shape, 0)
    lane = lanes(shape) % 32
    keep_x, keep_z = row < 31, lane < 31
    for c in range(5):
        FY[c] = jnp.zeros(shape, F32)
        B[2, c] = W[c, :, 0, :]
        B[3, c] = W[c, :, 31, :]
        B[4, c] = W[c, 0]
        B[5, c] = W[c, 31]
        B[0, c] = W[c, 0]
        B[1, c] = W[c, 0]

    def body(y, _):
        up = jnp.minimum(y + 1, 31)
        U = [W[c, y] for c in range(5)]
        S = [Q[k, y] for k in range(7)]
        here = lane == y
        for c in range(5):
            B[0, c] = jnp.where(here, pltpu.roll(U[c], y, 1), B[0, c])
            B[1, c] = jnp.where(here, pltpu.roll(U[c], y + 97, 1), B[1, c])
        total = []
        F = face_flux(U, S, [roll(a, -1, 1) for a in U], [roll(a, -1, 1) for a in S], 2, keep_z)
        for c in range(5):
            total.append(F[c] - roll(F[c], 1, 1))
        F = face_flux(U, S, [roll(a, -1, 0) for a in U], [roll(a, -1, 0) for a in S], 0, keep_x)
        for c in range(5):
            total[c] = total[c] + (F[c] - roll(F[c], 1, 0))
        keep = jnp.broadcast_to(y, shape) < 31
        F = face_flux(
            U, S, [W[c, up] for c in range(5)], [Q[k, up] for k in range(7)], 1, keep
        )
        for c in range(5):
            total[c] = total[c] + (F[c] - FY[c])
            FY[c] = F[c]
            W[c, y] = U[c] - COURANT * total[c]
        return 0

    lax.fori_loop(0, 32, body, 0)


def fine_shells(got, sources, S, mix=None):
    shape = (16, 128)
    lane = lanes(shape)
    slot = lane // 32
    column = (lane % 32) // 2
    for g in range(4):
        blocks = []
        for s in range(4):
            at = pl.ds(16 * g, 16)
            block = got[sources[s], at, :]
            if mix is not None:
                block = 0.5 * (block + mix[sources[s], at, :])
            blocks.append(block)
        for k in range(8):
            q = 8 * g + k
            if q < 30:
                out = None
                for s in range(4):
                    piece = pick(blocks[s], 16 * k + column)
                    out = piece if out is None else jnp.where(slot == s, piece, out)
                S[q // 5, q % 5, pl.ds(0, 16, 2), :] = out
                S[q // 5, q % 5, pl.ds(1, 16, 2), :] = out


def fine_boundary(B, S, FB, FS, W, first):
    def body(e2, _):
        for side in range(2):
            face = 2 * e2 + side
            inner = [B[face, c] for c in range(5)]
            outer = [S[face, c] for c in range(5)]
            for n in range(3):
                axis = (2, 0, 1)[n]

                @pl.when(e2 == n)
                def _():
                    qi, qo = primitives(inner), primitives(outer)
                    if side == 0:
                        F = face_flux(outer, qo, inner, qi, axis)
                    else:
                        F = face_flux(inner, qi, outer, qo, axis)
                    for c in range(5):
                        FB[face, c] = F[c]
                        FS[face, c] = F[c] if first else FS[face, c] + F[c]

        return 0

    lax.fori_loop(0, 3, body, 0)
    for c in range(5):
        W[c, :, 0, :] = W[c, :, 0, :] + COURANT * FB[2, c]
        W[c, :, 31, :] = W[c, :, 31, :] - COURANT * FB[3, c]
        W[c, 0] = W[c, 0] + COURANT * FB[4, c]
        W[c, 31] = W[c, 31] - COURANT * FB[5, c]


def z_boundary(value, FB, c, y, lane):
    value = value + jnp.where(lane == 0, COURANT * pltpu.roll(FB[0, c], 128 - y, 1), 0.0)
    return value - jnp.where(lane == 31, COURANT * pltpu.roll(FB[1, c], 159 - y, 1), 0.0)


def fine_again(W, FB, Q):
    lane = lanes((32, 128)) % 32

    def body(y, _):
        U = []
        for c in range(5):
            U.append(z_boundary(W[c, y], FB, c, y, lane))
            W[c, y] = U[c]
        for k, q in enumerate(primitives(U)):
            Q[k, y] = q
        return 0

    lax.fori_loop(0, 32, body, 0)


def fine_store(W, FB, patch, count, out):
    lane = lanes((32, 128)) % 32

    def body(yg, _):
        at = pl.ds(pl.multiple_of(yg * 128, 128), 128)
        for c in range(5):
            vs = []
            for j in range(4):
                y = 4 * yg + j
                vs.append(z_boundary(W[c, y], FB, c, y, lane))
            vs = block_transpose(vs, 32)
            for s in range(4):
                out[s, c, :, at] = jnp.where(s < count, vs[s], patch[s, c, :, at])
        return 0

    lax.fori_loop(0, 8, body, 0)


def fine_pack(FS, PS):
    shape = (16, 128)
    lane = lanes(shape)
    for g in range(4):
        outs = [jnp.zeros(shape, F32) for _ in range(4)]
        for k in range(8):
            q = 8 * g + k
            if q < 30:
                m = FS[q // 5, q % 5, pl.ds(0, 16, 2), :] + FS[q // 5, q % 5, pl.ds(1, 16, 2), :]
                m = m + roll(m, -1, 1)
                for s in range(4):
                    piece = pick(m, 32 * s + 2 * (lane % 16))
                    outs[s] = jnp.where(lane // 16 == k, piece, outs[s])
        for s in range(4):
            PS[s, pl.ds(16 * g, 16), :] = outs[s]


def build_shells(field, sides, planes, PZ):
    shape = (16, 128)
    lane = lanes(shape)
    zeros = jnp.zeros(shape, F32)
    T = [zeros] * 10
    for x in range(16):
        here = lane % 16 == x
        for c in range(5):
            U = field[c, x, 0:16, :]
            T[c] = jnp.where(here, roll(U, x + 1, 1), T[c])
            T[5 + c] = jnp.where(here, roll(U, x - 16, 1), T[5 + c])
    z0 = jnp.concatenate(T[:8], axis=0).T
    z1 = jnp.concatenate(T[8:] + [zeros] * 6, axis=0).T
    for zb in range(8):
        PZ[zb, 0:16] = z0[16 * zb : 16 * zb + 16]
    for g in range(1, 4):
        vs = []
        for k in range(8):
            q = 8 * g + k
            vs.append(zeros if q < 10 or q >= 30 else sides[q // 5 - 2][q % 5])
        vs = block_transpose(vs, 16)
        for zb in range(8):
            value = vs[zb]
            if g == 1:
                value = jnp.where(lane < 32, z1[16 * zb : 16 * zb + 16], value)
            PZ[zb, 16 * g : 16 * g + 16] = value


def coarse_kernel(me_ref, anchors, counts, field, xlo, xhi, ylo, yhi, adv, FP, dense, C, Q, FX, PZ):
    owners = dense.shape[0]
    for c in range(5):
        for x in range(16):
            C[c, x, 0:16] = field[c, x]
            C[c, x, 16:24] = jnp.broadcast_to(yhi[c, x : x + 1], (8, 128))
        C[c, 16, 0:16] = xhi[c]
        C[c, 16, 16:24] = xhi[c, 8:16]

    def cells(x, _):
        for k, q in enumerate(primitives([C[c, x] for c in range(5)])):
            Q[k, x] = q
        return 0

    lax.fori_loop(0, 17, cells, 0)
    R = [field[c, 0] for c in range(5)]
    L = [xlo[c] for c in range(5)]
    F = face_flux(L, primitives(L), R, primitives(R), 0)
    for c in range(5):
        FP[2, c] = F[c]
        FX[c] = F[c]
    R = [field[c, :, 0, :] for c in range(5)]
    L = [ylo[c] for c in range(5)]
    F = face_flux(L, primitives(L), R, primitives(R), 1)
    for c in range(5):
        FP[4, c] = F[c]
        FP[0, c] = jnp.zeros((16, 128), F32)
    lane = lanes((16, 128)) % 16
    row = lax.broadcasted_iota(jnp.int32, (16, 128), 0)

    def body(x, _):
        U24 = [C[c, x] for c in range(5)]
        S24 = [Q[k, x] for k in range(7)]
        U, S = [a[0:16] for a in U24], [a[0:16] for a in S24]
        F = face_flux(U, S, [roll(a, -1, 1) for a in U], [roll(a, -1, 1) for a in S], 2)
        total = []
        for c in range(5):
            FP[0, c] = jnp.where(lane == x, pltpu.roll(F[c], x + 1, 1), FP[0, c])
            total.append(F[c] - roll(F[c], 1, 1))
        F = face_flux(U, S, [roll(a, -1, 0)[0:16] for a in U24], [roll(a, -1, 0)[0:16] for a in S24], 1)
        for c in range(5):
            before = jnp.where(row == 0, FP[4, c, pl.ds(x, 1), :], roll(F[c], 1, 0))
            total[c] = total[c] + (F[c] - before)
            FP[5, c, pl.ds(x, 1), :] = F[c][15:16]
        F = face_flux(
            U, S, [C[c, x + 1, 0:16] for c in range(5)], [Q[k, x + 1, 0:16] for k in range(7)], 0
        )
        for c in range(5):
            adv[c, x] = U[c] - COURANT * (total[c] + (F[c] - FX[c]))
            FX[c] = F[c]
        return 0

    lax.fori_loop(0, 16, body, 0)
    for c in range(5):
        FP[3, c] = FX[c]
        FP[1, c] = roll(FP[0, c], -16, 1)
    shell_kernel(me_ref, anchors, counts, field, xlo, xhi, ylo, yhi, dense, PZ)


def shell_kernel(me_ref, anchors, counts, field, xlo, xhi, ylo, yhi, dense, PZ):
    owners = dense.shape[0]
    me = me_ref[0]
    build_shells(field, (xlo, xhi, ylo, yhi), None, PZ)
    for o in range(owners):
        block = jnp.int32(0)
        for s in range(4):
            at = 12 * o + 3 * s
            mine = jnp.logical_and(s < counts[o], anchors[at] == 16 * me)
            block = block + jnp.where(mine, anchors[at + 2] // 16, 0)
        dense[o] = PZ[block]


def interior_kernel(patch, W, B, Q, FY):
    fine_load(patch, W, Q)
    fine_interior(W, Q, FY, B)


def fine_kernel(
    me_ref, anchors, counts, patch, W_in, B, old, new, out, outgoing, W, Q, FY, S, FB, FS, PS, B2
):
    owners = outgoing.shape[0]
    me = me_ref[0]
    count = counts[me]
    sources = [anchors[12 * me + 3 * s] // 16 for s in range(4)]

    def copy(y, _):
        for c in range(5):
            W[c, y] = W_in[c, y]
        return 0

    lax.fori_loop(0, 32, copy, 0)
    fine_shells(old, sources, S)
    fine_boundary(B, S, FB, FS, W, True)
    fine_again(W, FB, Q)
    fine_interior(W, Q, FY, B2)
    fine_shells(old, sources, S, new)
    fine_boundary(B2, S, FB, FS, W, False)
    fine_pack(FS, PS)
    for i in range(owners):
        slot = jnp.int32(0)
        for s in range(1, 4):
            slot = jnp.where(jnp.logical_and(s < count, sources[s] == i), s, slot)
        outgoing[i] = PS[slot]
    fine_store(W, FB, patch, count, out)


def reflux_kernel(me_ref, anchors, counts, adv, FP, got, out, D):
    owners = got.shape[0]
    me = me_ref[0]
    shape = (16, 128)
    lane = lanes(shape)
    owner = [jnp.int32(0)] * 8
    present = [jnp.int32(0)] * 8
    for o in range(owners):
        for s in range(4):
            at = 12 * o + 3 * s
            mine = jnp.logical_and(s < counts[o], anchors[at] == 16 * me)
            block = anchors[at + 2] // 16
            for zb in range(8):
                hit = jnp.logical_and(mine, block == zb)
                owner[zb] = jnp.where(hit, o, owner[zb])
                present[zb] = jnp.where(hit, 1, present[zb])
    live = jnp.zeros(shape, jnp.int32)
    for zb in range(8):
        live = jnp.where(lane // 16 == zb, present[zb], live)
    live = live > 0
    delta = {}
    for g in range(4):
        vs = [got[owner[zb], pl.ds(16 * g, 16), :] for zb in range(8)]
        if g < 2:
            turned = jnp.concatenate(vs, axis=0).T
        if g > 0:
            vs = block_transpose(vs, 16)
        for k in range(8):
            q = 8 * g + k
            if q < 30:
                e, c = q // 5, q % 5
                mean = 0.125 * (turned[16 * k : 16 * k + 16] if q < 10 else vs[k])
                value = COURANT * (FP[e, c] - mean) if e % 2 == 0 else COURANT * (mean - FP[e, c])
                value = jnp.where(live, value, 0.0)
                if e < 2:
                    delta[e, c] = value
                else:
                    D[e - 2, c] = value
    for c in range(5):
        for x in range(16):
            value = adv[c, x]
            value = value + jnp.where(lane % 16 == 15, roll(delta[0, c], -(x + 1), 1), 0.0)
            value = value + jnp.where(lane % 16 == 0, roll(delta[1, c], 16 - x, 1), 0.0)
            out[c, x] = value


def rim_kernel(field, x_up, x_down, y_up, y_down, out):
    out[...] = field[...]
    for c in range(5):
        out[c, 15] = out[c, 15] + x_up[c]
        out[c, 0] = out[c, 0] + x_down[c]
        out[c, :, 15, :] = out[c, :, 15, :] + y_up[c]
        out[c, :, 0, :] = out[c, :, 0, :] + y_down[c]


def call(kernel, outs, n_scalar, n_vector, scratch=(), flops=1000000):
    return pl.pallas_call(
        kernel,
        out_shape=[jax.ShapeDtypeStruct(shape, F32) for shape in outs],
        in_specs=[pl.BlockSpec(memory_space=pltpu.SMEM)] * n_scalar
        + [pl.BlockSpec(memory_space=pltpu.VMEM)] * n_vector,
        out_specs=[pl.BlockSpec(memory_space=pltpu.VMEM)] * len(outs),
        scratch_shapes=[pltpu.VMEM(shape, F32) for shape in scratch],
        compiler_params=pltpu.CompilerParams(vmem_limit_bytes=VMEM_LIMIT),
        cost_estimate=pl.CostEstimate(flops=flops, bytes_accessed=4000000, transcendentals=0),
    )


def shift(x, axis, up):
    count = lax.axis_size(axis)
    pairs = [(i, (i + 1) % count) for i in range(count)]
    if not up:
        pairs = [(b, a) for a, b in pairs]
    return lax.ppermute(x, axis, pairs)


def halos(field):
    return (
        shift(field[:, 15], "gx", True),
        shift(field[:, 0], "gx", False),
        shift(field[:, :, 15], "gy", True),
        shift(field[:, :, 0], "gy", False),
    )


def exchange(x):
    return lax.all_to_all(x, "gx", split_axis=0, concat_axis=0, tiled=True)


def shards(coarse_state, patch_state, patch_anchor, patch_count):
    owners = lax.axis_size("gx")
    me = lax.axis_index("gx").astype(jnp.int32).reshape(1)
    anchors = patch_anchor.reshape(-1)
    counts = patch_count.reshape(-1)
    meta = (me, anchors, counts)
    patch = patch_state.reshape(4, 5, 32, 1024)
    cube = (5, 32, 32, 128)
    prim = (7, 32, 32, 128)
    planes = (6, 5, 32, 128)
    field = (5, 16, 16, 128)
    dense = (owners, 64, 128)

    W, B = call(interior_kernel, [cube, planes], 0, 1, [prim, (5, 32, 128)], 50000000)(patch)
    sides = halos(coarse_state)
    advanced, FP, dense_old = call(
        coarse_kernel,
        [field, (6, 5, 16, 128), dense],
        3,
        5,
        [(5, 17, 24, 128), (7, 17, 24, 128), (5, 16, 128), (8, 64, 128)],
        10000000,
    )(*meta, coarse_state, *sides)
    old = exchange(dense_old)
    sides = halos(advanced)
    (dense_new,) = call(shell_kernel, [dense], 3, 5, [(8, 64, 128)])(*meta, advanced, *sides)
    new = exchange(dense_new)
    out, outgoing = call(
        fine_kernel,
        [(4, 5, 32, 1024), dense],
        3,
        5,
        [cube, prim, (5, 32, 128), planes, planes, planes, (4, 64, 128), planes],
        50000000,
    )(*meta, patch, W, B, old, new)
    arrived = exchange(outgoing)
    field_next, D = call(reflux_kernel, [field, (4, 5, 16, 128)], 3, 3)(
        *meta, advanced, FP, arrived
    )
    (coarse_next,) = call(rim_kernel, [field], 0, 5)(
        field_next,
        shift(D[0], "gx", False),
        shift(D[1], "gx", True),
        shift(D[2], "gy", False),
        shift(D[3], "gy", True),
    )
    return (coarse_next, out.reshape(patch_state.shape))


def solution(mesh):
    in_specs = (
        P(None, "gx", "gy", None),
        P("gx", "gy", None, None, None, None),
        P(None, "gy", None, None),
        P(None, "gy"),
    )
    out_specs = (P(None, "gx", "gy", None), P("gx", "gy", None, None, None, None))
    return jax.shard_map(shards, mesh=mesh, in_specs=in_specs, out_specs=out_specs, check_vma=False)
```

```python
import jax
import jax.numpy as jnp
from jax import lax
from jax.experimental import pallas as pl
from jax.experimental.pallas import tpu as pltpu
from jax.sharding import PartitionSpec as P

COURANT = 0.12
VMEM_LIMIT = 56 * 1024 * 1024
F32 = jnp.float32
MESH = pl.DeviceIdType.MESH


def rcp(x):
    return pl.reciprocal(x, approx=True)


def root(x):
    return x * lax.rsqrt(x)


def primitives(U):
    r = rcp(U[0])
    u, v, w = U[1] * r, U[2] * r, U[3] * r
    p = 0.4 * (U[4] - 0.5 * (U[1] * u + U[2] * v + U[3] * w))
    c5 = root((35.0 * p) * r)
    cg5 = c5 * jnp.exp2(jnp.log2(p) * (-1.0 / 7.0))
    sa = root(r * (1.0 / 1.2))
    return [u, v, w, p, c5, cg5, sa]


def newton(s, z, scaled, L, R, du):
    value, slope = du, None
    for p6, p7, c5, cg5, sa in (L, R):
        t = s + p6
        q = lax.rsqrt(t)
        rt = sa * q
        d = t - p7
        shock = d * rt
        shock_slope = rt * (1.0 + p7 * (q * q))
        rare = cg5 * z - c5
        rare_slope = cg5 * scaled
        up = d > 0.0
        value = value + jnp.where(up, shock, rare)
        term = jnp.where(up, shock_slope, rare_slope)
        slope = term if slope is None else slope + term
    return s - (value + value) * rcp(slope)


def face_flux(UL, QL, UR, QR, n, keep=None):
    uL, pL, c5L, cg5L, saL = QL[n], QL[3], QL[4], QL[5], QL[6]
    uR, pR, c5R, cg5R, saR = QR[n], QR[3], QR[4], QR[5], QR[6]
    du = uR - uL
    L = (pL * (1.0 / 6.0), pL * (7.0 / 6.0), c5L, cg5L, saL)
    R = (pR * (1.0 / 6.0), pR * (7.0 / 6.0), c5R, cg5R, saR)
    z = (c5L + c5R - du) * rcp(cg5L + cg5R)
    z2 = z * z
    z6 = z2 * z2 * z2
    s = newton(z6 * z, z, (2.0 / 7.0) * rcp(z6), L, R, du)
    z = jnp.exp2(jnp.log2(s) * (1.0 / 7.0))
    s = newton(s, z, (2.0 / 7.0) * z * rcp(s), L, R, du)
    waves = []
    for c5, sa in ((c5L, saL), (c5R, saR)):
        cc = c5 * c5
        waves.append(0.2 * root(jnp.maximum(cc, (cc + (252.0 * s) * (sa * sa)) * (1.0 / 7.0))))
    low = jnp.minimum(uL - waves[0], 0.0)
    high = jnp.maximum(uR + waves[1], 0.0)
    inv = rcp(high - low)
    if keep is not None:
        inv = jnp.where(keep, inv, 0.0)
    wL, wR = high * inv, low * inv
    a, b = wL * (uL - low), wR * (high - uR)
    eL, eR = wL * pL, wR * pR
    F = [a * UL[i] + b * UR[i] for i in range(5)]
    F[1 + n] = F[1 + n] + (eL - eR)
    F[4] = F[4] + (eL * uL - eR * uR)
    return F


def roll(x, by, axis):
    by = by % x.shape[axis]
    return x if by == 0 else pltpu.roll(x, by, axis)


def lanes(shape):
    return lax.broadcasted_iota(jnp.int32, shape, len(shape) - 1)


def block_transpose(vs, width):
    n = len(vs)
    block = lanes(vs[0].shape) // width
    vs = list(vs)
    d = n // 2
    while d:
        low = (block & d) == 0
        for i in range(n):
            if i & d == 0:
                a, b = vs[i], vs[i + d]
                vs[i] = jnp.where(low, a, roll(b, d * width, 1))
                vs[i + d] = jnp.where(low, roll(a, -d * width, 1), b)
        d //= 2
    return vs


def pick(x, index):
    return jnp.take_along_axis(x, index, axis=1)


NORMAL = (2, 2, 0, 0, 1, 1)


def fine_load(patch, W, Q):
    def body(yg, _):
        at = pl.ds(pl.multiple_of(yg * 128, 128), 128)
        U = [[None] * 5 for _ in range(4)]
        for c in range(5):
            vs = block_transpose([patch[s, c, :, at] for s in range(4)], 32)
            for j in range(4):
                W[c, 4 * yg + j] = vs[j]
                U[j][c] = vs[j]
        for j in range(4):
            for k, q in enumerate(primitives(U[j])):
                Q[k, 4 * yg + j] = q
        return 0

    lax.fori_loop(0, 8, body, 0)


def fine_edges(W, FY, B):
    shape = (32, 128)
    for c in range(5):
        FY[c] = jnp.zeros(shape, F32)
        B[2, c] = W[c, :, 0, :]
        B[3, c] = W[c, :, 31, :]
        B[4, c] = W[c, 0]
        B[5, c] = W[c, 31]
        B[0, c] = W[c, 0]
        B[1, c] = W[c, 0]


def fine_interior(W, Q, FY, B, first, last):
    shape = (32, 128)
    row = lax.broadcasted_iota(jnp.int32, shape, 0)
    lane = lanes(shape) % 32
    keep_x, keep_z = row < 31, lane < 31

    def body(y, _):
        up = jnp.minimum(y + 1, 31)
        U = [W[c, y] for c in range(5)]
        S = [Q[k, y] for k in range(7)]
        here = lane == y
        for c in range(5):
            B[0, c] = jnp.where(here, pltpu.roll(U[c], y, 1), B[0, c])
            B[1, c] = jnp.where(here, pltpu.roll(U[c], y + 97, 1), B[1, c])
        total = []
        F = face_flux(U, S, [roll(a, -1, 1) for a in U], [roll(a, -1, 1) for a in S], 2, keep_z)
        for c in range(5):
            total.append(F[c] - roll(F[c], 1, 1))
        F = face_flux(U, S, [roll(a, -1, 0) for a in U], [roll(a, -1, 0) for a in S], 0, keep_x)
        for c in range(5):
            total[c] = total[c] + (F[c] - roll(F[c], 1, 0))
        keep = jnp.broadcast_to(y, shape) < 31
        F = face_flux(
            U, S, [W[c, up] for c in range(5)], [Q[k, up] for k in range(7)], 1, keep
        )
        for c in range(5):
            total[c] = total[c] + (F[c] - FY[c])
            FY[c] = F[c]
            W[c, y] = U[c] - COURANT * total[c]
        return 0

    lax.fori_loop(first, last, body, 0)


def fine_shells(got, sources, S, mix=None):
    shape = (16, 128)
    lane = lanes(shape)
    slot = lane // 32
    column = (lane % 32) // 2
    for g in range(4):
        blocks = []
        for s in range(4):
            at = pl.ds(16 * g, 16)
            block = got[sources[s], at, :]
            if mix is not None:
                block = 0.5 * (block + mix[sources[s], at, :])
            blocks.append(block)
        for k in range(8):
            q = 8 * g + k
            if q < 30:
                out = None
                for s in range(4):
                    piece = pick(blocks[s], 16 * k + column)
                    out = piece if out is None else jnp.where(slot == s, piece, out)
                S[q // 5, q % 5, pl.ds(0, 16, 2), :] = out
                S[q // 5, q % 5, pl.ds(1, 16, 2), :] = out


def fine_boundary(B, S, FB, FS, W, first):
    def body(e2, _):
        for side in range(2):
            face = 2 * e2 + side
            inner = [B[face, c] for c in range(5)]
            outer = [S[face, c] for c in range(5)]
            for n in range(3):
                axis = (2, 0, 1)[n]

                @pl.when(e2 == n)
                def _():
                    qi, qo = primitives(inner), primitives(outer)
                    if side == 0:
                        F = face_flux(outer, qo, inner, qi, axis)
                    else:
                        F = face_flux(inner, qi, outer, qo, axis)
                    for c in range(5):
                        FB[face, c] = F[c]
                        FS[face, c] = F[c] if first else FS[face, c] + F[c]

        return 0

    lax.fori_loop(0, 3, body, 0)
    for c in range(5):
        W[c, :, 0, :] = W[c, :, 0, :] + COURANT * FB[2, c]
        W[c, :, 31, :] = W[c, :, 31, :] - COURANT * FB[3, c]
        W[c, 0] = W[c, 0] + COURANT * FB[4, c]
        W[c, 31] = W[c, 31] - COURANT * FB[5, c]


def z_boundary(value, FB, c, y, lane):
    value = value + jnp.where(lane == 0, COURANT * pltpu.roll(FB[0, c], 128 - y, 1), 0.0)
    return value - jnp.where(lane == 31, COURANT * pltpu.roll(FB[1, c], 159 - y, 1), 0.0)


def fine_again(W, FB, Q):
    lane = lanes((32, 128)) % 32

    def body(y, _):
        U = []
        for c in range(5):
            U.append(z_boundary(W[c, y], FB, c, y, lane))
            W[c, y] = U[c]
        for k, q in enumerate(primitives(U)):
            Q[k, y] = q
        return 0

    lax.fori_loop(0, 32, body, 0)


def fine_store(W, FB, patch, count, out):
    lane = lanes((32, 128)) % 32

    def body(yg, _):
        at = pl.ds(pl.multiple_of(yg * 128, 128), 128)
        for c in range(5):
            vs = []
            for j in range(4):
                y = 4 * yg + j
                vs.append(z_boundary(W[c, y], FB, c, y, lane))
            vs = block_transpose(vs, 32)
            for s in range(4):
                out[s, c, :, at] = jnp.where(s < count, vs[s], patch[s, c, :, at])
        return 0

    lax.fori_loop(0, 8, body, 0)


def fine_pack(FS, PS):
    shape = (16, 128)
    lane = lanes(shape)
    for g in range(4):
        outs = [jnp.zeros(shape, F32) for _ in range(4)]
        for k in range(8):
            q = 8 * g + k
            if q < 30:
                m = FS[q // 5, q % 5, pl.ds(0, 16, 2), :] + FS[q // 5, q % 5, pl.ds(1, 16, 2), :]
                m = m + roll(m, -1, 1)
                for s in range(4):
                    piece = pick(m, 32 * s + 2 * (lane % 16))
                    outs[s] = jnp.where(lane // 16 == k, piece, outs[s])
        for s in range(4):
            PS[s, pl.ds(16 * g, 16), :] = outs[s]


def build_shells(field, sides, planes, PZ):
    shape = (16, 128)
    lane = lanes(shape)
    zeros = jnp.zeros(shape, F32)
    T = [zeros] * 10
    for x in range(16):
        here = lane % 16 == x
        for c in range(5):
            U = field[c, x, 0:16, :]
            T[c] = jnp.where(here, roll(U, x + 1, 1), T[c])
            T[5 + c] = jnp.where(here, roll(U, x - 16, 1), T[5 + c])
    z0 = jnp.concatenate(T[:8], axis=0).T
    z1 = jnp.concatenate(T[8:] + [zeros] * 6, axis=0).T
    for zb in range(8):
        PZ[zb, 0:16] = z0[16 * zb : 16 * zb + 16]
    for g in range(1, 4):
        vs = []
        for k in range(8):
            q = 8 * g + k
            vs.append(zeros if q < 10 or q >= 30 else sides[q // 5 - 2][q % 5])
        vs = block_transpose(vs, 16)
        for zb in range(8):
            value = vs[zb]
            if g == 1:
                value = jnp.where(lane < 32, z1[16 * zb : 16 * zb + 16], value)
            PZ[zb, 16 * g : 16 * g + 16] = value


def coarse_step(field, xlo, xhi, ylo, yhi, adv, FP, C, Q, FX):
    for c in range(5):
        for x in range(16):
            C[c, x, 0:16] = field[c, x]
            C[c, x, 16:24] = jnp.broadcast_to(yhi[c, x : x + 1], (8, 128))
        C[c, 16, 0:16] = xhi[c]
        C[c, 16, 16:24] = xhi[c, 8:16]

    def cells(x, _):
        for k, q in enumerate(primitives([C[c, x] for c in range(5)])):
            Q[k, x] = q
        return 0

    lax.fori_loop(0, 17, cells, 0)
    R = [field[c, 0] for c in range(5)]
    L = [xlo[c] for c in range(5)]
    F = face_flux(L, primitives(L), R, primitives(R), 0)
    for c in range(5):
        FP[2, c] = F[c]
        FX[c] = F[c]
    R = [field[c, :, 0, :] for c in range(5)]
    L = [ylo[c] for c in range(5)]
    F = face_flux(L, primitives(L), R, primitives(R), 1)
    for c in range(5):
        FP[4, c] = F[c]
        FP[0, c] = jnp.zeros((16, 128), F32)
    lane = lanes((16, 128)) % 16
    row = lax.broadcasted_iota(jnp.int32, (16, 128), 0)

    def body(x, _):
        U24 = [C[c, x] for c in range(5)]
        S24 = [Q[k, x] for k in range(7)]
        U, S = [a[0:16] for a in U24], [a[0:16] for a in S24]
        F = face_flux(U, S, [roll(a, -1, 1) for a in U], [roll(a, -1, 1) for a in S], 2)
        total = []
        for c in range(5):
            FP[0, c] = jnp.where(lane == x, pltpu.roll(F[c], x + 1, 1), FP[0, c])
            total.append(F[c] - roll(F[c], 1, 1))
        F = face_flux(U, S, [roll(a, -1, 0)[0:16] for a in U24], [roll(a, -1, 0)[0:16] for a in S24], 1)
        for c in range(5):
            before = jnp.where(row == 0, FP[4, c, pl.ds(x, 1), :], roll(F[c], 1, 0))
            total[c] = total[c] + (F[c] - before)
            FP[5, c, pl.ds(x, 1), :] = F[c][15:16]
        F = face_flux(
            U, S, [C[c, x + 1, 0:16] for c in range(5)], [Q[k, x + 1, 0:16] for k in range(7)], 0
        )
        for c in range(5):
            adv[c, x] = U[c] - COURANT * (total[c] + (F[c] - FX[c]))
            FX[c] = F[c]
        return 0

    lax.fori_loop(0, 16, body, 0)
    for c in range(5):
        FP[3, c] = FX[c]
        FP[1, c] = roll(FP[0, c], -16, 1)


def in_pencil(anchors, counts, me, o, s):
    at = 12 * o + 3 * s
    return jnp.logical_and(s < counts[o], anchors[at] == 16 * me), anchors[at + 2] // 16


def pack_shells(anchors, counts, me, owners, field, sides, PZ, dense):
    build_shells(field, sides, None, PZ)
    for o in range(owners):
        block = jnp.int32(0)
        for s in range(4):
            mine, zb = in_pencil(anchors, counts, me, o, s)
            block = block + jnp.where(mine, zb, 0)
        dense[o] = PZ[block]


class Place:
    def __init__(self):
        self.i, self.j = lax.axis_index("gx"), lax.axis_index("gy")
        self.ni, self.nj = lax.axis_size("gx"), lax.axis_size("gy")

    def along_x(self, d):
        return (lax.rem(self.i + (d + self.ni), self.ni), self.j)

    def along_y(self, d):
        return (self.i, lax.rem(self.j + (d + self.nj), self.nj))

    def greet(self):
        barrier = pltpu.get_barrier_semaphore()
        for d in range(1, self.ni):
            pl.semaphore_signal(barrier, inc=1, device_id=self.along_x(d), device_id_type=MESH)
        for d in (1, -1):
            pl.semaphore_signal(barrier, inc=1, device_id=self.along_y(d), device_id_type=MESH)

    def greeted(self):
        pl.semaphore_wait(pltpu.get_barrier_semaphore(), self.ni + 1)

    def send(self, src, dst, send_sem, recv_sem, to):
        copy = pltpu.make_async_remote_copy(
            src_ref=src,
            dst_ref=dst,
            send_sem=send_sem,
            recv_sem=recv_sem,
            device_id=to,
            device_id_type=MESH,
        )
        copy.start()
        return copy

    def neighbours(self, planes, sides, sems):
        to = (self.along_x(1), self.along_x(-1), self.along_y(1), self.along_y(-1))
        return [
            self.send(planes[k], sides[k], sems.at[0, k], sems.at[1, k], to[k]) for k in range(4)
        ]

    def exchange(self, dense, got, sems):
        got[self.i] = dense[self.i]
        copies = []
        for d in range(1, self.ni):
            to = self.along_x(d)
            copies.append(
                self.send(dense.at[to[0]], got.at[self.i], sems.at[0, d], sems.at[1, d], to)
            )
        return copies


def wait(copies):
    for copy in copies:
        copy.wait()


def edge_planes(field, edges):
    for c in range(5):
        edges[0, c] = field[c, :, 15, :]
        edges[1, c] = field[c, :, 0, :]
    return (field.at[:, 15], field.at[:, 0], edges.at[0], edges.at[1])


def first_kernel(
    anchors, counts, patch, field, W, B, S1, S2, adv, FP,
    Q, FY, C, CQ, FX, PZ, dense_old, dense_new, got_old, got_new, edges, sides, near_sems, far_sems,
):
    place = Place()
    me = place.i
    sources = [anchors[12 * me + 3 * s] // 16 for s in range(4)]
    place.greet()
    fine_load(patch, W, Q)
    fine_edges(W, FY, B)
    planes = edge_planes(field, edges.at[0])
    old = [sides.at[0, k] for k in range(4)]
    new = [sides.at[1, k] for k in range(4)]
    place.greeted()
    near = place.neighbours(planes, old, near_sems.at[0])
    fine_interior(W, Q, FY, B, 0, 6)
    wait(near)
    pack_shells(anchors, counts, me, place.ni, field, old, PZ, dense_old)
    far_old = place.exchange(dense_old, got_old, far_sems.at[0])
    coarse_step(field, *old, adv, FP, C, CQ, FX)
    planes = edge_planes(adv, edges.at[1])
    near = place.neighbours(planes, new, near_sems.at[1])
    fine_interior(W, Q, FY, B, 6, 14)
    wait(near)
    pack_shells(anchors, counts, me, place.ni, adv, new, PZ, dense_new)
    far_new = place.exchange(dense_new, got_new, far_sems.at[1])
    fine_interior(W, Q, FY, B, 14, 32)
    wait(far_old)
    fine_shells(got_old, sources, S1)
    wait(far_new)
    fine_shells(got_old, sources, S2, got_new)


def fine_kernel(anchors, counts, me_ref, patch, W_in, B, S1, S2, out, outgoing, W, Q, FY, FB, FS, PS, B2):
    owners = outgoing.shape[0]
    me = me_ref[0]
    count = counts[me]
    sources = [anchors[12 * me + 3 * s] // 16 for s in range(4)]

    def copy(y, _):
        for c in range(5):
            W[c, y] = W_in[c, y]
        return 0

    lax.fori_loop(0, 32, copy, 0)
    fine_boundary(B, S1, FB, FS, W, True)
    fine_again(W, FB, Q)
    fine_edges(W, FY, B2)
    fine_interior(W, Q, FY, B2, 0, 32)
    fine_boundary(B2, S2, FB, FS, W, False)
    fine_pack(FS, PS)
    for i in range(owners):
        slot = jnp.int32(0)
        for s in range(1, 4):
            slot = jnp.where(jnp.logical_and(s < count, sources[s] == i), s, slot)
        outgoing[i] = PS[slot]
    fine_store(W, FB, patch, count, out)


def reflux(anchors, counts, me, owners, adv, FP, got, out, D):
    shape = (16, 128)
    lane = lanes(shape)
    owner = [jnp.int32(0)] * 8
    present = [jnp.int32(0)] * 8
    for o in range(owners):
        for s in range(4):
            mine, block = in_pencil(anchors, counts, me, o, s)
            for zb in range(8):
                hit = jnp.logical_and(mine, block == zb)
                owner[zb] = jnp.where(hit, o, owner[zb])
                present[zb] = jnp.where(hit, 1, present[zb])
    live = jnp.zeros(shape, jnp.int32)
    for zb in range(8):
        live = jnp.where(lane // 16 == zb, present[zb], live)
    live = live > 0
    delta = {}
    for g in range(4):
        vs = [got[owner[zb], pl.ds(16 * g, 16), :] for zb in range(8)]
        if g < 2:
            turned = jnp.concatenate(vs, axis=0).T
        if g > 0:
            vs = block_transpose(vs, 16)
        for k in range(8):
            q = 8 * g + k
            if q < 30:
                e, c = q // 5, q % 5
                mean = 0.125 * (turned[16 * k : 16 * k + 16] if q < 10 else vs[k])
                value = COURANT * (FP[e, c] - mean) if e % 2 == 0 else COURANT * (mean - FP[e, c])
                value = jnp.where(live, value, 0.0)
                if e < 2:
                    delta[e, c] = value
                else:
                    D[e - 2, c] = value
    for c in range(5):
        for x in range(16):
            value = adv[c, x]
            value = value + jnp.where(lane % 16 == 15, roll(delta[0, c], -(x + 1), 1), 0.0)
            value = value + jnp.where(lane % 16 == 0, roll(delta[1, c], 16 - x, 1), 0.0)
            out[c, x] = value


def last_kernel(
    anchors, counts, outgoing, adv, FP, out, got, D, rims, near_sems, far_sems
):
    place = Place()
    place.greet()
    place.greeted()
    wait(place.exchange(outgoing, got, far_sems))
    reflux(anchors, counts, place.i, place.ni, adv, FP, got, out, D)
    planes = [D.at[1], D.at[0], D.at[3], D.at[2]]
    wait(place.neighbours(planes, [rims.at[k] for k in range(4)], near_sems))
    for c in range(5):
        out[c, 0] = out[c, 0] + rims[0, c]
        out[c, 15] = out[c, 15] + rims[1, c]
        out[c, :, 0, :] = out[c, :, 0, :] + rims[2, c]
        out[c, :, 15, :] = out[c, :, 15, :] + rims[3, c]


def call(kernel, outs, n_scalar, n_vector, scratch=(), collective=None):
    more = {}
    if collective is not None:
        more = {"collective_id": collective, "has_side_effects": True}
    return pl.pallas_call(
        kernel,
        out_shape=[jax.ShapeDtypeStruct(shape, F32) for shape in outs],
        in_specs=[pl.BlockSpec(memory_space=pltpu.SMEM)] * n_scalar
        + [pl.BlockSpec(memory_space=pltpu.VMEM)] * n_vector,
        out_specs=[pl.BlockSpec(memory_space=pltpu.VMEM)] * len(outs),
        scratch_shapes=[pltpu.VMEM(s, F32) if isinstance(s, tuple) else s for s in scratch],
        compiler_params=pltpu.CompilerParams(vmem_limit_bytes=VMEM_LIMIT, **more),
        cost_estimate=pl.CostEstimate(flops=10000000, bytes_accessed=4000000, transcendentals=0),
    )


def shards(coarse_state, patch_state, patch_anchor, patch_count):
    owners = lax.axis_size("gx")
    me = lax.axis_index("gx").astype(jnp.int32).reshape(1)
    anchors = patch_anchor.reshape(-1)
    counts = patch_count.reshape(-1)
    patch = patch_state.reshape(4, 5, 32, 1024)
    cube = (5, 32, 32, 128)
    prim = (7, 32, 32, 128)
    planes = (6, 5, 32, 128)
    field = (5, 16, 16, 128)
    side = (5, 16, 128)
    dense = (owners, 64, 128)
    dma = pltpu.SemaphoreType.DMA

    W, B, S1, S2, advanced, FP = call(
        first_kernel,
        [cube, planes, planes, planes, field, (6,) + side],
        2,
        2,
        [prim, (5, 32, 128), (5, 17, 24, 128), (7, 17, 24, 128), side, (8, 64, 128)]
        + [dense] * 4
        + [(2, 2) + side, (2, 4) + side, dma((2, 2, 4)), dma((2, 2, owners))],
        0,
    )(anchors, counts, patch, coarse_state)
    out, outgoing = call(
        fine_kernel,
        [(4, 5, 32, 1024), dense],
        3,
        5,
        [cube, prim, (5, 32, 128), planes, planes, (4, 64, 128), planes],
    )(anchors, counts, me, patch, W, B, S1, S2)
    (coarse_next,) = call(
        last_kernel,
        [field],
        2,
        3,
        [dense, (4,) + side, (4,) + side, dma((2, 4)), dma((2, owners))],
        1,
    )(anchors, counts, outgoing, advanced, FP)
    return (coarse_next, out.reshape(patch_state.shape))


def solution(mesh):
    in_specs = (
        P(None, "gx", "gy", None),
        P("gx", "gy", None, None, None, None),
        P(None, "gy", None, None),
        P(None, "gy"),
    )
    out_specs = (P(None, "gx", "gy", None), P("gx", "gy", None, None, None, None))
    return jax.shard_map(shards, mesh=mesh, in_specs=in_specs, out_specs=out_specs, check_vma=False)
```

```python
import jax
import jax.numpy as jnp
from jax import lax
from jax.experimental import pallas as pl
from jax.experimental.pallas import tpu as pltpu
from jax.sharding import PartitionSpec as P

COURANT = 0.12
VMEM_LIMIT = 56 * 1024 * 1024
F32 = jnp.float32
MESH = pl.DeviceIdType.MESH


def rcp(x):
    return pl.reciprocal(x, approx=True)


def root(x):
    return x * lax.rsqrt(x)


def primitives(U):
    r = rcp(U[0])
    u, v, w = U[1] * r, U[2] * r, U[3] * r
    p = 0.4 * (U[4] - 0.5 * (U[1] * u + U[2] * v + U[3] * w))
    c5 = root((35.0 * p) * r)
    cg5 = c5 * jnp.exp2(jnp.log2(p) * (-1.0 / 7.0))
    sa = root(r * (1.0 / 1.2))
    return [u, v, w, p, c5, cg5, sa]


def newton(s, z, scaled, L, R, du):
    value, slope = du, None
    for p6, p7, c5, cg5, sa in (L, R):
        t = s + p6
        q = lax.rsqrt(t)
        rt = sa * q
        d = t - p7
        shock = d * rt
        shock_slope = rt * (1.0 + p7 * (q * q))
        rare = cg5 * z - c5
        rare_slope = cg5 * scaled
        up = d > 0.0
        value = value + jnp.where(up, shock, rare)
        term = jnp.where(up, shock_slope, rare_slope)
        slope = term if slope is None else slope + term
    return s - (value + value) * rcp(slope)


def face_flux(UL, QL, UR, QR, n, keep=None):
    uL, pL, c5L, cg5L, saL = QL[n], QL[3], QL[4], QL[5], QL[6]
    uR, pR, c5R, cg5R, saR = QR[n], QR[3], QR[4], QR[5], QR[6]
    du = uR - uL
    L = (pL * (1.0 / 6.0), pL * (7.0 / 6.0), c5L, cg5L, saL)
    R = (pR * (1.0 / 6.0), pR * (7.0 / 6.0), c5R, cg5R, saR)
    z = (c5L + c5R - du) * rcp(cg5L + cg5R)
    z2 = z * z
    z6 = z2 * z2 * z2
    s = newton(z6 * z, z, (2.0 / 7.0) * rcp(z6), L, R, du)
    z = jnp.exp2(jnp.log2(s) * (1.0 / 7.0))
    s = newton(s, z, (2.0 / 7.0) * z * rcp(s), L, R, du)
    waves = []
    for c5, sa in ((c5L, saL), (c5R, saR)):
        cc = c5 * c5
        waves.append(0.2 * root(jnp.maximum(cc, (cc + (252.0 * s) * (sa * sa)) * (1.0 / 7.0))))
    low = jnp.minimum(uL - waves[0], 0.0)
    high = jnp.maximum(uR + waves[1], 0.0)
    inv = rcp(high - low)
    if keep is not None:
        inv = jnp.where(keep, inv, 0.0)
    wL, wR = high * inv, low * inv
    a, b = wL * (uL - low), wR * (high - uR)
    eL, eR = wL * pL, wR * pR
    F = [a * UL[i] + b * UR[i] for i in range(5)]
    F[1 + n] = F[1 + n] + (eL - eR)
    F[4] = F[4] + (eL * uL - eR * uR)
    return F


def roll(x, by, axis):
    by = by % x.shape[axis]
    return x if by == 0 else pltpu.roll(x, by, axis)


def lanes(shape):
    return lax.broadcasted_iota(jnp.int32, shape, len(shape) - 1)


def block_transpose(vs, width):
    n = len(vs)
    block = lanes(vs[0].shape) // width
    vs = list(vs)
    d = n // 2
    while d:
        low = (block & d) == 0
        for i in range(n):
            if i & d == 0:
                a, b = vs[i], vs[i + d]
                vs[i] = jnp.where(low, a, roll(b, d * width, 1))
                vs[i + d] = jnp.where(low, roll(a, -d * width, 1), b)
        d //= 2
    return vs


def pick(x, index):
    return jnp.take_along_axis(x, index, axis=1)


NORMAL = (2, 2, 0, 0, 1, 1)


def collect(U, y, lane, B):
    here = lane == y
    for c in range(5):
        B[0, c] = jnp.where(here, pltpu.roll(U[c], y, 1), B[0, c])
        B[1, c] = jnp.where(here, pltpu.roll(U[c], y + 97, 1), B[1, c])


def fine_load(patch, W, Q, B):
    lane = lanes((32, 128)) % 32
    for c in range(5):
        B[0, c] = jnp.zeros((32, 128), F32)
        B[1, c] = jnp.zeros((32, 128), F32)

    def body(yg, _):
        at = pl.ds(pl.multiple_of(yg * 128, 128), 128)
        U = [[None] * 5 for _ in range(4)]
        for c in range(5):
            vs = block_transpose([patch[s, c, :, at] for s in range(4)], 32)
            for j in range(4):
                W[c, 4 * yg + j] = vs[j]
                U[j][c] = vs[j]
        for j in range(4):
            collect(U[j], 4 * yg + j, lane, B)
            for k, q in enumerate(primitives(U[j])):
                Q[k, 4 * yg + j] = q
        return 0

    lax.fori_loop(0, 8, body, 0)


def fine_edges(W, FY, B):
    shape = (32, 128)
    for c in range(5):
        FY[c] = jnp.zeros(shape, F32)
        B[2, c] = W[c, :, 0, :]
        B[3, c] = W[c, :, 31, :]
        B[4, c] = W[c, 0]
        B[5, c] = W[c, 31]


def fine_interior(W, Q, FY, first, last):
    shape = (32, 128)
    row = lax.broadcasted_iota(jnp.int32, shape, 0)
    lane = lanes(shape) % 32
    keep_x, keep_z = row < 31, lane < 31

    def body(y, _):
        up = jnp.minimum(y + 1, 31)
        U = [W[c, y] for c in range(5)]
        S = [Q[k, y] for k in range(7)]
        total = []
        F = face_flux(U, S, [roll(a, -1, 1) for a in U], [roll(a, -1, 1) for a in S], 2, keep_z)
        for c in range(5):
            total.append(F[c] - roll(F[c], 1, 1))
        F = face_flux(U, S, [roll(a, -1, 0) for a in U], [roll(a, -1, 0) for a in S], 0, keep_x)
        for c in range(5):
            total[c] = total[c] + (F[c] - roll(F[c], 1, 0))
        keep = jnp.broadcast_to(y, shape) < 31
        F = face_flux(
            U, S, [W[c, up] for c in range(5)], [Q[k, up] for k in range(7)], 1, keep
        )
        for c in range(5):
            total[c] = total[c] + (F[c] - FY[c])
            FY[c] = F[c]
            W[c, y] = U[c] - COURANT * total[c]
        return 0

    lax.fori_loop(first, last, body, 0)


def fine_shells(got, sources, S, mix=None):
    shape = (16, 128)
    lane = lanes(shape)
    slot = lane // 32
    column = (lane % 32) // 2
    for g in range(4):
        blocks = []
        for s in range(4):
            at = pl.ds(16 * g, 16)
            block = got[sources[s], at, :]
            if mix is not None:
                block = 0.5 * (block + mix[sources[s], at, :])
            blocks.append(block)
        for k in range(8):
            q = 8 * g + k
            if q < 30:
                out = None
                for s in range(4):
                    piece = pick(blocks[s], 16 * k + column)
                    out = piece if out is None else jnp.where(slot == s, piece, out)
                S[q // 5, q % 5, pl.ds(0, 16, 2), :] = out
                S[q // 5, q % 5, pl.ds(1, 16, 2), :] = out


def fine_boundary(B, S, FB, FS, first):
    def body(e2, _):
        for side in range(2):
            face = 2 * e2 + side
            inner = [B[face, c] for c in range(5)]
            outer = [S[face, c] for c in range(5)]
            for n in range(3):
                axis = (2, 0, 1)[n]

                @pl.when(e2 == n)
                def _():
                    qi, qo = primitives(inner), primitives(outer)
                    if side == 0:
                        F = face_flux(outer, qo, inner, qi, axis)
                    else:
                        F = face_flux(inner, qi, outer, qo, axis)
                    for c in range(5):
                        FB[face, c] = F[c]
                        FS[face, c] = F[c] if first else FS[face, c] + F[c]

        return 0

    lax.fori_loop(0, 3, body, 0)


def add_boundary(W, FB):
    for c in range(5):
        W[c, :, 0, :] = W[c, :, 0, :] + COURANT * FB[2, c]
        W[c, :, 31, :] = W[c, :, 31, :] - COURANT * FB[3, c]
        W[c, 0] = W[c, 0] + COURANT * FB[4, c]
        W[c, 31] = W[c, 31] - COURANT * FB[5, c]


def z_boundary(value, FB, c, y, lane):
    value = value + jnp.where(lane == 0, COURANT * pltpu.roll(FB[0, c], 128 - y, 1), 0.0)
    return value - jnp.where(lane == 31, COURANT * pltpu.roll(FB[1, c], 159 - y, 1), 0.0)


def fine_again(W, FB, Q, B):
    lane = lanes((32, 128)) % 32

    def body(y, _):
        U = []
        for c in range(5):
            U.append(z_boundary(W[c, y], FB, c, y, lane))
            W[c, y] = U[c]
        collect(U, y, lane, B)
        for k, q in enumerate(primitives(U)):
            Q[k, y] = q
        return 0

    lax.fori_loop(0, 32, body, 0)


def fine_store(W, FB, patch, count, out):
    lane = lanes((32, 128)) % 32

    def body(yg, _):
        at = pl.ds(pl.multiple_of(yg * 128, 128), 128)
        for c in range(5):
            vs = []
            for j in range(4):
                y = 4 * yg + j
                vs.append(z_boundary(W[c, y], FB, c, y, lane))
            vs = block_transpose(vs, 32)
            for s in range(4):
                out[s, c, :, at] = jnp.where(s < count, vs[s], patch[s, c, :, at])
        return 0

    lax.fori_loop(0, 8, body, 0)


def fine_pack(FS, PS):
    shape = (16, 128)
    lane = lanes(shape)
    for g in range(4):
        outs = [jnp.zeros(shape, F32) for _ in range(4)]
        for k in range(8):
            q = 8 * g + k
            if q < 30:
                m = FS[q // 5, q % 5, pl.ds(0, 16, 2), :] + FS[q // 5, q % 5, pl.ds(1, 16, 2), :]
                m = m + roll(m, -1, 1)
                for s in range(4):
                    piece = pick(m, 32 * s + 2 * (lane % 16))
                    outs[s] = jnp.where(lane // 16 == k, piece, outs[s])
        for s in range(4):
            PS[s, pl.ds(16 * g, 16), :] = outs[s]


def build_shells(field, sides, planes, PZ):
    shape = (16, 128)
    lane = lanes(shape)
    zeros = jnp.zeros(shape, F32)
    T = [zeros] * 10
    for x in range(16):
        here = lane % 16 == x
        for c in range(5):
            U = field[c, x, 0:16, :]
            T[c] = jnp.where(here, roll(U, x + 1, 1), T[c])
            T[5 + c] = jnp.where(here, roll(U, x - 16, 1), T[5 + c])
    z0 = jnp.concatenate(T[:8], axis=0).T
    z1 = jnp.concatenate(T[8:] + [zeros] * 6, axis=0).T
    for zb in range(8):
        PZ[zb, 0:16] = z0[16 * zb : 16 * zb + 16]
    for g in range(1, 4):
        vs = []
        for k in range(8):
            q = 8 * g + k
            vs.append(zeros if q < 10 or q >= 30 else sides[q // 5 - 2][q % 5])
        vs = block_transpose(vs, 16)
        for zb in range(8):
            value = vs[zb]
            if g == 1:
                value = jnp.where(lane < 32, z1[16 * zb : 16 * zb + 16], value)
            PZ[zb, 16 * g : 16 * g + 16] = value


def coarse_step(field, xlo, xhi, ylo, yhi, adv, FP, C, Q, FX):
    for c in range(5):
        for x in range(16):
            C[c, x, 0:16] = field[c, x]
            C[c, x, 16:24] = jnp.broadcast_to(yhi[c, x : x + 1], (8, 128))
        C[c, 16, 0:16] = xhi[c]
        C[c, 16, 16:24] = xhi[c, 8:16]

    def cells(x, _):
        for k, q in enumerate(primitives([C[c, x] for c in range(5)])):
            Q[k, x] = q
        return 0

    lax.fori_loop(0, 17, cells, 0)
    R = [field[c, 0] for c in range(5)]
    L = [xlo[c] for c in range(5)]
    F = face_flux(L, primitives(L), R, primitives(R), 0)
    for c in range(5):
        FP[2, c] = F[c]
        FX[c] = F[c]
    R = [field[c, :, 0, :] for c in range(5)]
    L = [ylo[c] for c in range(5)]
    F = face_flux(L, primitives(L), R, primitives(R), 1)
    for c in range(5):
        FP[4, c] = F[c]
        FP[0, c] = jnp.zeros((16, 128), F32)
    lane = lanes((16, 128)) % 16
    row = lax.broadcasted_iota(jnp.int32, (16, 128), 0)

    def body(x, _):
        U24 = [C[c, x] for c in range(5)]
        S24 = [Q[k, x] for k in range(7)]
        U, S = [a[0:16] for a in U24], [a[0:16] for a in S24]
        F = face_flux(U, S, [roll(a, -1, 1) for a in U], [roll(a, -1, 1) for a in S], 2)
        total = []
        for c in range(5):
            FP[0, c] = jnp.where(lane == x, pltpu.roll(F[c], x + 1, 1), FP[0, c])
            total.append(F[c] - roll(F[c], 1, 1))
        F = face_flux(U, S, [roll(a, -1, 0)[0:16] for a in U24], [roll(a, -1, 0)[0:16] for a in S24], 1)
        for c in range(5):
            before = jnp.where(row == 0, FP[4, c, pl.ds(x, 1), :], roll(F[c], 1, 0))
            total[c] = total[c] + (F[c] - before)
            FP[5, c, pl.ds(x, 1), :] = F[c][15:16]
        F = face_flux(
            U, S, [C[c, x + 1, 0:16] for c in range(5)], [Q[k, x + 1, 0:16] for k in range(7)], 0
        )
        for c in range(5):
            adv[c, x] = U[c] - COURANT * (total[c] + (F[c] - FX[c]))
            FX[c] = F[c]
        return 0

    lax.fori_loop(0, 16, body, 0)
    for c in range(5):
        FP[3, c] = FX[c]
        FP[1, c] = roll(FP[0, c], -16, 1)


def owned_blocks(anchors, counts, me, owners):
    blocks = []
    for o in range(owners):
        block = jnp.int32(-1)
        for s in range(4):
            at = 12 * o + 3 * s
            mine = jnp.logical_and(s < counts[o], anchors[at] == 16 * me)
            block = jnp.where(mine, anchors[at + 2] // 16, block)
        blocks.append(block)
    return blocks


def pack_shells(blocks, field, sides, PZ, dense):
    build_shells(field, sides, None, PZ)
    for o, block in enumerate(blocks):
        dense[o] = PZ[jnp.maximum(block, 0)]


class Place:
    def __init__(self):
        self.i, self.j = lax.axis_index("gx"), lax.axis_index("gy")
        self.ni, self.nj = lax.axis_size("gx"), lax.axis_size("gy")

    def along_x(self, d):
        return (lax.rem(self.i + (d + self.ni), self.ni), self.j)

    def along_y(self, d):
        return (self.i, lax.rem(self.j + (d + self.nj), self.nj))

    def greet(self):
        barrier = pltpu.get_barrier_semaphore()
        for d in range(1, self.ni):
            pl.semaphore_signal(barrier, inc=1, device_id=self.along_x(d), device_id_type=MESH)
        for d in (1, -1):
            pl.semaphore_signal(barrier, inc=1, device_id=self.along_y(d), device_id_type=MESH)

    def greeted(self):
        pl.semaphore_wait(pltpu.get_barrier_semaphore(), self.ni + 1)

    def send(self, src, dst, send_sem, recv_sem, to):
        copy = pltpu.make_async_remote_copy(
            src_ref=src,
            dst_ref=dst,
            send_sem=send_sem,
            recv_sem=recv_sem,
            device_id=to,
            device_id_type=MESH,
        )
        copy.start()
        return copy

    def neighbours(self, planes, sides, sems):
        to = (self.along_x(1), self.along_x(-1), self.along_y(1), self.along_y(-1))
        return [
            self.send(planes[k], sides[k], sems.at[0, k], sems.at[1, k], to[k]) for k in range(4)
        ]

    def exchange(self, dense, got, sems):
        got[self.i] = dense[self.i]
        copies = []
        for d in range(1, self.ni):
            to = self.along_x(d)
            copies.append(
                self.send(dense.at[to[0]], got.at[self.i], sems.at[0, d], sems.at[1, d], to)
            )
        return copies


def wait(copies):
    for copy in copies:
        copy.wait()


def edge_planes(field, edges):
    for c in range(5):
        edges[0, c] = field[c, :, 15, :]
        edges[1, c] = field[c, :, 0, :]
    return (field.at[:, 15], field.at[:, 0], edges.at[0], edges.at[1])


def step_kernel(
    anchors, counts, patch, field, out_field, out,
    W, Q, B, S1, S2, FB, FS, FY, PS, C, CQ, FX, adv, FP, PZ,
    dense_old, dense_new, dense_back, got_old, got_new, got_back, edges, D, sides, near_sems, far_sems,
):
    place = Place()
    me = place.i
    count = counts[me]
    sources = [anchors[12 * me + 3 * s] // 16 for s in range(4)]
    old, new, rims = ([sides.at[n, k] for k in range(4)] for n in range(3))
    place.greet()
    planes = edge_planes(field, edges.at[0])
    blocks = owned_blocks(anchors, counts, me, place.ni)
    fine_load(patch, W, Q, B)
    fine_edges(W, FY, B)
    place.greeted()
    near = place.neighbours(planes, old, near_sems.at[0])
    fine_interior(W, Q, FY, 0, 6)
    wait(near)
    pack_shells(blocks, field, old, PZ, dense_old)
    far_old = place.exchange(dense_old, got_old, far_sems.at[0])
    coarse_step(field, *old, adv, FP, C, CQ, FX)
    planes = edge_planes(adv, edges.at[1])
    near = place.neighbours(planes, new, near_sems.at[1])
    fine_interior(W, Q, FY, 6, 14)
    wait(near)
    pack_shells(blocks, adv, new, PZ, dense_new)
    far_new = place.exchange(dense_new, got_new, far_sems.at[1])
    fine_interior(W, Q, FY, 14, 32)
    wait(far_old)
    fine_shells(got_old, sources, S1)
    fine_boundary(B, S1, FB, FS, True)
    add_boundary(W, FB)
    fine_again(W, FB, Q, B)
    fine_edges(W, FY, B)
    wait(far_new)
    fine_shells(got_old, sources, S2, got_new)
    fine_boundary(B, S2, FB, FS, False)
    fine_pack(FS, PS)
    for i in range(place.ni):
        slot = jnp.int32(0)
        for s in range(1, 4):
            slot = jnp.where(jnp.logical_and(s < count, sources[s] == i), s, slot)
        dense_back[i] = PS[slot]
    back = place.exchange(dense_back, got_back, far_sems.at[2])
    fine_interior(W, Q, FY, 0, 22)
    wait(back)
    reflux(blocks, adv, FP, got_back, out_field, D)
    near = place.neighbours([D.at[1], D.at[0], D.at[3], D.at[2]], rims, near_sems.at[2])
    fine_interior(W, Q, FY, 22, 32)
    add_boundary(W, FB)
    fine_store(W, FB, patch, count, out)
    wait(near)
    for c in range(5):
        out_field[c, 0] = out_field[c, 0] + sides[2, 0, c]
        out_field[c, 15] = out_field[c, 15] + sides[2, 1, c]
        out_field[c, :, 0, :] = out_field[c, :, 0, :] + sides[2, 2, c]
        out_field[c, :, 15, :] = out_field[c, :, 15, :] + sides[2, 3, c]


def reflux(blocks, adv, FP, got, out, D):
    shape = (16, 128)
    lane = lanes(shape)
    owner = [jnp.int32(0)] * 8
    present = [jnp.int32(0)] * 8
    for o, block in enumerate(blocks):
        for zb in range(8):
            owner[zb] = jnp.where(block == zb, o, owner[zb])
            present[zb] = jnp.where(block == zb, 1, present[zb])
    live = jnp.zeros(shape, jnp.int32)
    for zb in range(8):
        live = jnp.where(lane // 16 == zb, present[zb], live)
    live = live > 0
    delta = {}
    for g in range(4):
        vs = [got[owner[zb], pl.ds(16 * g, 16), :] for zb in range(8)]
        if g < 2:
            turned = jnp.concatenate(vs, axis=0).T
        if g > 0:
            vs = block_transpose(vs, 16)
        for k in range(8):
            q = 8 * g + k
            if q < 30:
                e, c = q // 5, q % 5
                mean = 0.125 * (turned[16 * k : 16 * k + 16] if q < 10 else vs[k])
                value = COURANT * (FP[e, c] - mean) if e % 2 == 0 else COURANT * (mean - FP[e, c])
                value = jnp.where(live, value, 0.0)
                if e < 2:
                    delta[e, c] = value
                else:
                    D[e - 2, c] = value
    for c in range(5):
        for x in range(16):
            value = adv[c, x]
            value = value + jnp.where(lane % 16 == 15, roll(delta[0, c], -(x + 1), 1), 0.0)
            value = value + jnp.where(lane % 16 == 0, roll(delta[1, c], 16 - x, 1), 0.0)
            out[c, x] = value


def call(kernel, outs, n_scalar, n_vector, scratch=(), collective=None):
    more = {}
    if collective is not None:
        more = {"collective_id": collective, "has_side_effects": True}
    return pl.pallas_call(
        kernel,
        out_shape=[jax.ShapeDtypeStruct(shape, F32) for shape in outs],
        in_specs=[pl.BlockSpec(memory_space=pltpu.SMEM)] * n_scalar
        + [pl.BlockSpec(memory_space=pltpu.VMEM)] * n_vector,
        out_specs=[pl.BlockSpec(memory_space=pltpu.VMEM)] * len(outs),
        scratch_shapes=[pltpu.VMEM(s, F32) if isinstance(s, tuple) else s for s in scratch],
        compiler_params=pltpu.CompilerParams(vmem_limit_bytes=VMEM_LIMIT, **more),
        cost_estimate=pl.CostEstimate(flops=10000000, bytes_accessed=4000000, transcendentals=0),
    )


def shards(coarse_state, patch_state, patch_anchor, patch_count):
    owners = lax.axis_size("gx")
    anchors = patch_anchor.reshape(-1)
    counts = patch_count.reshape(-1)
    patch = patch_state.reshape(4, 5, 32, 1024)
    cube = (5, 32, 32, 128)
    prim = (7, 32, 32, 128)
    planes = (6, 5, 32, 128)
    field = (5, 16, 16, 128)
    side = (5, 16, 128)
    dense = (owners, 64, 128)
    dma = pltpu.SemaphoreType.DMA

    coarse_next, out = call(
        step_kernel,
        [field, (4, 5, 32, 1024)],
        2,
        2,
        [cube, prim] + [planes] * 5 + [(5, 32, 128), (4, 64, 128)]
        + [(5, 17, 24, 128), (7, 17, 24, 128), side, field, (6,) + side, (8, 64, 128)]
        + [dense] * 6
        + [(2, 2) + side, (4,) + side, (3, 4) + side, dma((3, 2, 4)), dma((3, 2, owners))],
        0,
    )(anchors, counts, patch, coarse_state)
    return (coarse_next, out.reshape(patch_state.shape))


def solution(mesh):
    in_specs = (
        P(None, "gx", "gy", None),
        P("gx", "gy", None, None, None, None),
        P(None, "gy", None, None),
        P(None, "gy"),
    )
    out_specs = (P(None, "gx", "gy", None), P("gx", "gy", None, None, None, None))
    return jax.shard_map(shards, mesh=mesh, in_specs=in_specs, out_specs=out_specs, check_vma=False)
```

```python
import jax
import jax.numpy as jnp
from jax import lax
from jax.experimental import pallas as pl
from jax.experimental.pallas import tpu as pltpu
from jax.sharding import PartitionSpec as P

COURANT = 0.12
VMEM_LIMIT = 36 * 1024 * 1024
F32 = jnp.float32
MESH = pl.DeviceIdType.MESH


def rcp(x):
    return pl.reciprocal(x, approx=True)


def root(x):
    return x * lax.rsqrt(x)


def primitives(U):
    r = rcp(U[0])
    u, v, w = U[1] * r, U[2] * r, U[3] * r
    p = 0.4 * (U[4] - 0.5 * (U[1] * u + U[2] * v + U[3] * w))
    cc = 1.4 * (p * r)
    c5 = 5.0 * root(cc)
    cg5 = c5 * jnp.exp2(jnp.log2(p) * (-1.0 / 7.0))
    sa = root(r * (1.0 / 1.2))
    return [u, v, w, p, c5, cg5, sa, cc, 1.2 * r]


PRIMS = 9


def newton(s, z, scaled, L, R, du):
    value, slope = du, None
    for p, p7, c5, cg5, sa in (L, R):
        d = s - p
        q = lax.rsqrt(d + p7)
        rt = sa * q
        shock = d * rt
        shock_slope = rt * (1.0 + p7 * (q * q))
        rare = cg5 * z - c5
        rare_slope = cg5 * scaled
        up = d > 0.0
        value = value + jnp.where(up, shock, rare)
        term = jnp.where(up, shock_slope, rare_slope)
        slope = term if slope is None else slope + term
    return s - (value + value) * rcp(slope)


def face_flux(UL, QL, UR, QR, n, scale=COURANT):
    uL, pL, c5L, cg5L, saL = QL[n], QL[3], QL[4], QL[5], QL[6]
    uR, pR, c5R, cg5R, saR = QR[n], QR[3], QR[4], QR[5], QR[6]
    du = uR - uL
    L = (pL, pL * (7.0 / 6.0), c5L, cg5L, saL)
    R = (pR, pR * (7.0 / 6.0), c5R, cg5R, saR)
    z = (c5L + c5R - du) * rcp(cg5L + cg5R)
    z2 = z * z
    z6 = z2 * z2 * z2
    s = newton(z6 * z, z, (2.0 / 7.0) * rcp(z6), L, R, du)
    z = jnp.exp2(jnp.log2(s) * (1.0 / 7.0))
    s = newton(s, z, (2.0 / 7.0) * z * rcp(s), L, R, du)
    low, high = (
        root(jnp.maximum(q[7], q[7] * (1.0 / 7.0) + s * q[8])) for q in (QL, QR)
    )
    low = jnp.minimum(uL - low, 0.0)
    high = jnp.maximum(uR + high, 0.0)
    inv = rcp(high - low) * scale
    wL, wR = high * inv, low * inv
    a, b = wL * (uL - low), wR * (high - uR)
    eL, eR = wL * pL, wR * pR
    F = [a * UL[i] + b * UR[i] for i in range(5)]
    F[1 + n] = F[1 + n] + (eL - eR)
    F[4] = F[4] + (eL * uL - eR * uR)
    return F


def roll(x, by, axis):
    by = by % x.shape[axis]
    return x if by == 0 else pltpu.roll(x, by, axis)


def lanes(shape):
    return lax.broadcasted_iota(jnp.int32, shape, len(shape) - 1)


def block_transpose(vs, width):
    n = len(vs)
    block = lanes(vs[0].shape) // width
    vs = list(vs)
    d = n // 2
    while d:
        low = (block & d) == 0
        for i in range(n):
            if i & d == 0:
                a, b = vs[i], vs[i + d]
                vs[i] = jnp.where(low, a, roll(b, d * width, 1))
                vs[i + d] = jnp.where(low, roll(a, -d * width, 1), b)
        d //= 2
    return vs


def pick(x, index):
    return jnp.take_along_axis(x, index, axis=1)


NORMAL = (2, 2, 0, 0, 1, 1)


def next_x(a):
    return jnp.concatenate([a[8:32], roll(a[0:8], -1, 0)], axis=0)


def last_x(a):
    return jnp.concatenate([roll(a[24:32], 1, 0), a[0:24]], axis=0)


def collect(U, y, lane, B):
    here = lane == y
    for c in range(5):
        B[0, c] = jnp.where(here, pltpu.roll(U[c], y, 1), B[0, c])
        B[1, c] = jnp.where(here, pltpu.roll(U[c], y + 97, 1), B[1, c])


def fine_load(patch, W, Q, B, T):
    lane = lanes((32, 128)) % 32
    for c in range(5):
        B[0, c] = jnp.zeros((32, 128), F32)
        B[1, c] = jnp.zeros((32, 128), F32)

    def body(yg, _):
        at = pl.ds(pl.multiple_of(yg * 128, 128), 128)
        U = [[None] * 5 for _ in range(4)]
        for c in range(5):
            vs = block_transpose([patch[s, c, :, at] for s in range(4)], 32)
            for j in range(4):
                T[c, j] = vs[j]
        for c in range(5):
            for j in range(4):
                U[j][c] = jnp.concatenate([T[c, j, pl.ds(v, 8, 4), :] for v in range(4)], axis=0)
                W[c, 4 * yg + j] = U[j][c]
        for j in range(4):
            collect(U[j], 4 * yg + j, lane, B)
            for k, q in enumerate(primitives(U[j])):
                Q[k, 4 * yg + j] = q
        return 0

    lax.fori_loop(0, 8, body, 0)


def fine_edges(W, FY, B):
    for c in range(5):
        FY[c] = jnp.zeros((32, 128), F32)
        B[2, c] = W[c, :, 0, :]
        B[3, c] = W[c, :, 31, :]
        B[4, c] = W[c, 0]
        B[5, c] = W[c, 31]


def fine_interior(W, Q, FY, first, last):
    shape = (32, 128)
    row = lax.broadcasted_iota(jnp.int32, shape, 0)
    scale_x = jnp.where(row < 31, COURANT, 0.0)
    scale_z = jnp.where(lanes(shape) % 32 < 31, COURANT, 0.0)

    def body(pair, _):
        ys = (2 * pair, 2 * pair + 1, jnp.minimum(2 * pair + 2, 31))
        U = [[W[c, y] for c in range(5)] for y in ys]
        S = [[Q[k, y] for k in range(PRIMS)] for y in ys]
        before = [FY[c] for c in range(5)]
        results = []
        for n in range(2):
            scale = COURANT if n == 0 else jnp.where(jnp.broadcast_to(pair, shape) < 15, COURANT, 0.0)
            F = face_flux(U[n], S[n], U[n + 1], S[n + 1], 1, scale)
            total = [F[c] - before[c] for c in range(5)]
            before = F
            F = face_flux(
                U[n], S[n], [roll(a, -1, 1) for a in U[n]], [roll(a, -1, 1) for a in S[n]], 2, scale_z
            )
            total = [total[c] + (F[c] - roll(F[c], 1, 1)) for c in range(5)]
            F = face_flux(
                U[n], S[n], [next_x(a) for a in U[n]], [next_x(a) for a in S[n]], 0, scale_x
            )
            results.append([U[n][c] - (total[c] + (F[c] - last_x(F[c]))) for c in range(5)])
        for c in range(5):
            W[c, ys[0]] = results[0][c]
            W[c, ys[1]] = results[1][c]
            FY[c] = before[c]
        return 0

    lax.fori_loop(first // 2, last // 2, body, 0)


def fine_shells(got, sources, S, T16, mix=None):
    zeros = jnp.zeros((16, 128), F32)
    twice = lanes((16, 128)) // 2
    for g in range(4):
        blocks = []
        for s in range(4):
            at = pl.ds(16 * g, 16)
            block = got[sources[s], at, :]
            if mix is not None:
                block = 0.5 * (block + mix[sources[s], at, :])
            blocks.append(block)
        pieces = block_transpose(blocks + [zeros] * 4, 16)
        for k in range(8):
            q = 8 * g + k
            if q < 30:
                e, c = q // 5, q % 5
                out = pick(pieces[k], twice)
                if e in (2, 3):
                    S[e, c, pl.ds(0, 16, 2), :] = out
                    S[e, c, pl.ds(1, 16, 2), :] = out
                else:
                    T16[q] = out
                    even, odd = T16[q, pl.ds(0, 8, 2), :], T16[q, pl.ds(1, 8, 2), :]
                    S[e, c] = jnp.concatenate([even, even, odd, odd], axis=0)


def fine_boundary(B, S, FB, FS, first):
    for n in range(3):
        for face in (2 * n, 2 * n + 1):
            inner = [B[face, c] for c in range(5)]
            outer = [S[face, c] for c in range(5)]
            qi, qo = primitives(inner), primitives(outer)
            if face % 2 == 0:
                F = face_flux(outer, qo, inner, qi, NORMAL[face])
            else:
                F = face_flux(inner, qi, outer, qo, NORMAL[face])
            for c in range(5):
                FB[face, c] = F[c]
                FS[face, c] = F[c] if first else FS[face, c] + F[c]


def add_boundary(W, FB):
    for c in range(5):
        W[c, :, 0, :] = W[c, :, 0, :] + FB[2, c]
        W[c, :, 31, :] = W[c, :, 31, :] - FB[3, c]
        W[c, 0] = W[c, 0] + FB[4, c]
        W[c, 31] = W[c, 31] - FB[5, c]


def z_boundary(value, FB, c, y, lane):
    value = value + jnp.where(lane == 0, pltpu.roll(FB[0, c], 128 - y, 1), 0.0)
    return value - jnp.where(lane == 31, pltpu.roll(FB[1, c], 159 - y, 1), 0.0)


def fine_again(W, FB, Q, B):
    lane = lanes((32, 128)) % 32

    def body(pair, _):
        for y in (2 * pair, 2 * pair + 1):
            U = []
            for c in range(5):
                U.append(z_boundary(W[c, y], FB, c, y, lane))
                W[c, y] = U[c]
            collect(U, y, lane, B)
            for k, q in enumerate(primitives(U)):
                Q[k, y] = q
        return 0

    lax.fori_loop(0, 16, body, 0)


def fine_store(W, FB, patch, count, out, T):
    lane = lanes((32, 128)) % 32

    def body(yg, _):
        at = pl.ds(pl.multiple_of(yg * 128, 128), 128)
        for c in range(5):
            for j in range(4):
                y = 4 * yg + j
                value = z_boundary(W[c, y], FB, c, y, lane)
                for v in range(4):
                    T[c, j, pl.ds(v, 8, 4), :] = value[8 * v : 8 * v + 8]
        for c in range(5):
            vs = block_transpose([T[c, j] for j in range(4)], 32)
            for s in range(4):
                out[s, c, :, at] = jnp.where(s < count, vs[s], patch[s, c, :, at])
        return 0

    lax.fori_loop(0, 8, body, 0)


def fine_pack(FS, PS, T16):
    half = (lanes((16, 128)) * 2) % 128
    for g in range(4):
        pieces = []
        for k in range(8):
            q = 8 * g + k
            if q >= 30:
                pieces.append(jnp.zeros((16, 128), F32))
                continue
            e, c = q // 5, q % 5
            if e in (2, 3):
                m = FS[e, c, pl.ds(0, 16, 2), :] + FS[e, c, pl.ds(1, 16, 2), :]
            else:
                T16[q, pl.ds(0, 8, 2), :] = FS[e, c, 0:8] + FS[e, c, 8:16]
                T16[q, pl.ds(1, 8, 2), :] = FS[e, c, 16:24] + FS[e, c, 24:32]
                m = T16[q]
            pieces.append(pick(m + roll(m, -1, 1), half))
        outs = block_transpose(pieces, 16)
        for s in range(4):
            PS[s, pl.ds(16 * g, 16), :] = outs[s]


def build_shells(field, sides, planes, PZ):
    shape = (16, 128)
    lane = lanes(shape)
    zeros = jnp.zeros(shape, F32)
    T = [zeros] * 10
    for x in range(16):
        here = lane % 16 == x
        for c in range(5):
            U = field[c, x, 0:16, :]
            T[c] = jnp.where(here, roll(U, x + 1, 1), T[c])
            T[5 + c] = jnp.where(here, roll(U, x - 16, 1), T[5 + c])
    z0 = jnp.concatenate(T[:8], axis=0).T
    z1 = jnp.concatenate(T[8:] + [zeros] * 6, axis=0).T
    for zb in range(8):
        PZ[zb, 0:16] = z0[16 * zb : 16 * zb + 16]
    for g in range(1, 4):
        vs = []
        for k in range(8):
            q = 8 * g + k
            vs.append(zeros if q < 10 or q >= 30 else sides[q // 5 - 2][q % 5])
        vs = block_transpose(vs, 16)
        for zb in range(8):
            value = vs[zb]
            if g == 1:
                value = jnp.where(lane < 32, z1[16 * zb : 16 * zb + 16], value)
            PZ[zb, 16 * g : 16 * g + 16] = value


def coarse_step(field, xlo, xhi, ylo, yhi, adv, FP, C, Q, FX):
    for c in range(5):
        for x in range(16):
            C[c, x, 0:16] = field[c, x]
            C[c, x, 16:24] = jnp.broadcast_to(yhi[c, x : x + 1], (8, 128))
        C[c, 16, 0:16] = xhi[c]
        C[c, 16, 16:24] = xhi[c, 8:16]

    def cells(x4, _):
        for x in range(4):
            for k, q in enumerate(primitives([C[c, 4 * x4 + x] for c in range(5)])):
                Q[k, 4 * x4 + x] = q
        return 0

    lax.fori_loop(0, 4, cells, 0)
    for k, q in enumerate(primitives([C[c, 16] for c in range(5)])):
        Q[k, 16] = q
    R = [field[c, 0] for c in range(5)]
    L = [xlo[c] for c in range(5)]
    F = face_flux(L, primitives(L), R, primitives(R), 0)
    for c in range(5):
        FP[2, c] = F[c]
        FX[c] = F[c]
    R = [field[c, :, 0, :] for c in range(5)]
    L = [ylo[c] for c in range(5)]
    F = face_flux(L, primitives(L), R, primitives(R), 1)
    for c in range(5):
        FP[4, c] = F[c]
        FP[0, c] = jnp.zeros((16, 128), F32)
    lane = lanes((16, 128)) % 16
    row = lax.broadcasted_iota(jnp.int32, (16, 128), 0)

    def body(pair, _):
        xs = (2 * pair, 2 * pair + 1, 2 * pair + 2)
        U24 = [[C[c, x] for c in range(5)] for x in xs]
        S24 = [[Q[k, x] for k in range(PRIMS)] for x in xs]
        U = [[a[0:16] for a in As] for As in U24]
        S = [[a[0:16] for a in As] for As in S24]
        below = [FX[c] for c in range(5)]
        corner = [[FP[4, c, pl.ds(x, 1), :] for c in range(5)] for x in xs[:2]]
        zs = [FP[0, c] for c in range(5)]
        results, tops = [], []
        for n in range(2):
            F = face_flux(U[n], S[n], U[n + 1], S[n + 1], 0)
            total = [F[c] - below[c] for c in range(5)]
            below = F
            F = face_flux(
                U[n], S[n], [roll(a, -1, 1) for a in U[n]], [roll(a, -1, 1) for a in S[n]], 2
            )
            for c in range(5):
                zs[c] = jnp.where(lane == xs[n], pltpu.roll(F[c], xs[n] + 1, 1), zs[c])
                total[c] = total[c] + (F[c] - roll(F[c], 1, 1))
            up = [[roll(a, -1, 0)[0:16] for a in As] for As in (U24[n], S24[n])]
            F = face_flux(U[n], S[n], up[0], up[1], 1)
            tops.append([a[15:16] for a in F])
            for c in range(5):
                before = jnp.where(row == 0, corner[n][c], roll(F[c], 1, 0))
                total[c] = total[c] + (F[c] - before)
            results.append([U[n][c] - total[c] for c in range(5)])
        for c in range(5):
            for n in range(2):
                adv[c, xs[n]] = results[n][c]
                FP[5, c, pl.ds(xs[n], 1), :] = tops[n][c]
            FP[0, c] = zs[c]
            FX[c] = below[c]
        return 0

    lax.fori_loop(0, 8, body, 0)
    for c in range(5):
        FP[3, c] = FX[c]
        FP[1, c] = roll(FP[0, c], -16, 1)


def owned_blocks(anchors, counts, me, owners):
    blocks = []
    for o in range(owners):
        block = jnp.int32(-1)
        for s in range(4):
            mine = jnp.logical_and(s < counts[o], anchors[0, s, o] == 16 * me)
            block = jnp.where(mine, anchors[2, s, o] // 16, block)
        blocks.append(block)
    return blocks


def pack_shells(blocks, field, sides, PZ, dense):
    build_shells(field, sides, None, PZ)
    for o, block in enumerate(blocks):
        dense[o] = PZ[jnp.maximum(block, 0)]


class Place:
    def __init__(self):
        self.i, self.j = lax.axis_index("gx"), lax.axis_index("gy")
        self.ni, self.nj = lax.axis_size("gx"), lax.axis_size("gy")

    def along_x(self, d):
        return (lax.rem(self.i + (d + self.ni), self.ni), self.j)

    def along_y(self, d):
        return (self.i, lax.rem(self.j + (d + self.nj), self.nj))

    def greet(self):
        barrier = pltpu.get_barrier_semaphore()
        for d in range(1, self.ni):
            pl.semaphore_signal(barrier, inc=1, device_id=self.along_x(d), device_id_type=MESH)
        for d in (1, -1):
            pl.semaphore_signal(barrier, inc=1, device_id=self.along_y(d), device_id_type=MESH)

    def greeted(self):
        pl.semaphore_wait(pltpu.get_barrier_semaphore(), self.ni + 1)

    def send(self, src, dst, send_sem, recv_sem, to):
        copy = pltpu.make_async_remote_copy(
            src_ref=src,
            dst_ref=dst,
            send_sem=send_sem,
            recv_sem=recv_sem,
            device_id=to,
            device_id_type=MESH,
        )
        copy.start()
        return copy

    def neighbours(self, planes, sides, sems):
        to = (self.along_x(1), self.along_x(-1), self.along_y(1), self.along_y(-1))
        return [
            self.send(planes[k], sides[k], sems.at[0, k], sems.at[1, k], to[k]) for k in range(4)
        ]

    def exchange(self, dense, got, sems):
        got[self.i] = dense[self.i]
        copies = []
        for d in range(1, self.ni):
            to = self.along_x(d)
            copies.append(
                self.send(dense.at[to[0]], got.at[self.i], sems.at[0, d], sems.at[1, d], to)
            )
        return copies


def wait(copies):
    for copy in copies:
        copy.wait()


def edge_planes(field, edges):
    for c in range(5):
        edges[0, c] = field[c, :, 15, :]
        edges[1, c] = field[c, :, 0, :]
    return (field.at[:, 15], field.at[:, 0], edges.at[0], edges.at[1])


def step_kernel(
    anchors, counts, patch, field, out_field, out,
    W, Q, B, S1, S2, FB, FS, FY, PS, C, CQ, FX, adv, FP, PZ,
    dense_old, dense_new, dense_back, got_old, got_new, got_back, edges, D, sides, near_sems, far_sems, T, T16,
):
    place = Place()
    me = place.i
    count = counts[me]
    sources = [anchors[0, s, me] // 16 for s in range(4)]
    old, new, rims = ([sides.at[n, k] for k in range(4)] for n in range(3))
    place.greet()
    planes = edge_planes(field, edges.at[0])
    blocks = owned_blocks(anchors, counts, me, place.ni)
    fine_load(patch, W, Q, B, T)
    fine_edges(W, FY, B)
    place.greeted()
    near = place.neighbours(planes, old, near_sems.at[0])
    fine_interior(W, Q, FY, 0, 6)
    wait(near)
    pack_shells(blocks, field, old, PZ, dense_old)
    far_old = place.exchange(dense_old, got_old, far_sems.at[0])
    coarse_step(field, *old, adv, FP, C, CQ, FX)
    planes = edge_planes(adv, edges.at[1])
    near = place.neighbours(planes, new, near_sems.at[1])
    fine_interior(W, Q, FY, 6, 14)
    wait(near)
    pack_shells(blocks, adv, new, PZ, dense_new)
    far_new = place.exchange(dense_new, got_new, far_sems.at[1])
    fine_interior(W, Q, FY, 14, 32)
    wait(far_old)
    fine_shells(got_old, sources, S1, T16)
    fine_boundary(B, S1, FB, FS, True)
    add_boundary(W, FB)
    fine_again(W, FB, Q, B)
    fine_edges(W, FY, B)
    wait(far_new)
    fine_shells(got_old, sources, S2, T16, got_new)
    fine_boundary(B, S2, FB, FS, False)
    fine_pack(FS, PS, T16)
    for i in range(place.ni):
        slot = jnp.int32(0)
        for s in range(1, 4):
            slot = jnp.where(jnp.logical_and(s < count, sources[s] == i), s, slot)
        dense_back[i] = PS[slot]
    back = place.exchange(dense_back, got_back, far_sems.at[2])
    fine_interior(W, Q, FY, 0, 22)
    wait(back)
    reflux(blocks, adv, FP, got_back, out_field, D)
    near = place.neighbours([D.at[1], D.at[0], D.at[3], D.at[2]], rims, near_sems.at[2])
    fine_interior(W, Q, FY, 22, 32)
    add_boundary(W, FB)
    fine_store(W, FB, patch, count, out, T)
    wait(near)
    for c in range(5):
        out_field[c, 0] = out_field[c, 0] + sides[2, 0, c]
        out_field[c, 15] = out_field[c, 15] + sides[2, 1, c]
        out_field[c, :, 0, :] = out_field[c, :, 0, :] + sides[2, 2, c]
        out_field[c, :, 15, :] = out_field[c, :, 15, :] + sides[2, 3, c]


def reflux(blocks, adv, FP, got, out, D):
    shape = (16, 128)
    lane = lanes(shape)
    owner = [jnp.int32(0)] * 8
    present = [jnp.int32(0)] * 8
    for o, block in enumerate(blocks):
        for zb in range(8):
            owner[zb] = jnp.where(block == zb, o, owner[zb])
            present[zb] = jnp.where(block == zb, 1, present[zb])
    live = jnp.zeros(shape, jnp.int32)
    for zb in range(8):
        live = jnp.where(lane // 16 == zb, present[zb], live)
    live = live > 0
    delta = {}
    for g in range(4):
        vs = [got[owner[zb], pl.ds(16 * g, 16), :] for zb in range(8)]
        if g < 2:
            turned = jnp.concatenate(vs, axis=0).T
        if g > 0:
            vs = block_transpose(vs, 16)
        for k in range(8):
            q = 8 * g + k
            if q < 30:
                e, c = q // 5, q % 5
                mean = 0.125 * (turned[16 * k : 16 * k + 16] if q < 10 else vs[k])
                value = FP[e, c] - mean if e % 2 == 0 else mean - FP[e, c]
                value = jnp.where(live, value, 0.0)
                if e < 2:
                    delta[e, c] = value
                else:
                    D[e - 2, c] = value
    for c in range(5):
        for x in range(16):
            value = adv[c, x]
            value = value + jnp.where(lane % 16 == 15, roll(delta[0, c], -(x + 1), 1), 0.0)
            value = value + jnp.where(lane % 16 == 0, roll(delta[1, c], 16 - x, 1), 0.0)
            out[c, x] = value


def call(kernel, outs, n_scalar, n_vector, scratch=(), collective=None):
    more = {}
    if collective is not None:
        more = {"collective_id": collective, "has_side_effects": True}
    return pl.pallas_call(
        kernel,
        out_shape=[jax.ShapeDtypeStruct(shape, F32) for shape in outs],
        in_specs=[pl.BlockSpec(memory_space=pltpu.SMEM)] * n_scalar
        + [pl.BlockSpec(memory_space=pltpu.VMEM)] * n_vector,
        out_specs=[pl.BlockSpec(memory_space=pltpu.VMEM)] * len(outs),
        scratch_shapes=[pltpu.VMEM(s, F32) if isinstance(s, tuple) else s for s in scratch],
        compiler_params=pltpu.CompilerParams(vmem_limit_bytes=VMEM_LIMIT, **more),
        cost_estimate=pl.CostEstimate(flops=10000000, bytes_accessed=4000000, transcendentals=0),
    )


def shards(coarse_state, patch_state, patch_anchor, patch_count):
    owners = lax.axis_size("gx")
    anchors = jnp.transpose(patch_anchor[:, 0], (2, 1, 0))
    counts = patch_count.reshape(-1)
    patch = patch_state.reshape(4, 5, 32, 1024)
    cube = (5, 32, 32, 128)
    prim = (PRIMS, 32, 32, 128)
    planes = (6, 5, 32, 128)
    field = (5, 16, 16, 128)
    side = (5, 16, 128)
    dense = (owners, 64, 128)
    dma = pltpu.SemaphoreType.DMA

    coarse_next, out = call(
        step_kernel,
        [field, (4, 5, 32, 1024)],
        2,
        2,
        [cube, prim] + [planes] * 5 + [(5, 32, 128), (4, 64, 128)]
        + [(5, 17, 24, 128), (PRIMS, 17, 24, 128), side, field, (6,) + side, (8, 64, 128)]
        + [dense] * 6
        + [(2, 2) + side, (4,) + side, (3, 4) + side, dma((3, 2, 4)), dma((3, 2, owners)), (5, 4, 32, 128), (30, 16, 128)],
        0,
    )(anchors, counts, patch, coarse_state)
    return (coarse_next, out.reshape(patch_state.shape))


def solution(mesh):
    in_specs = (
        P(None, "gx", "gy", None),
        P("gx", "gy", None, None, None, None),
        P(None, "gy", None, None),
        P(None, "gy"),
    )
    out_specs = (P(None, "gx", "gy", None), P("gx", "gy", None, None, None, None))
    return jax.shard_map(shards, mesh=mesh, in_specs=in_specs, out_specs=out_specs, check_vma=False)
```

```python
import jax
import jax.numpy as jnp
from jax import lax
from jax.experimental import pallas as pl
from jax.experimental.pallas import tpu as pltpu
from jax.sharding import PartitionSpec as P

COURANT = 0.12
VMEM_LIMIT = 50 * 1024 * 1024
F32 = jnp.float32
BF16 = jnp.bfloat16
MESH = pl.DeviceIdType.MESH


def rcp(x):
    return pl.reciprocal(x, approx=True)


def root(x):
    return x * lax.rsqrt(x)


def primitives(U):
    r = rcp(U[0])
    u, v, w = U[1] * r, U[2] * r, U[3] * r
    p = 0.4 * (U[4] - 0.5 * (U[1] * u + U[2] * v + U[3] * w))
    cc = 1.4 * (p * r)
    c5 = 5.0 * root(cc)
    cg5 = c5 * jnp.exp2(jnp.log2(p) * (-1.0 / 7.0))
    sa = root(r * (1.0 / 1.2))
    return [u, v, w, p, c5, cg5, sa, cc, 1.2 * r]


PRIMS = 9


def newton(s, z, L, R, du):
    value, slope = du, None
    scaled = (2.0 / 7.0) * rcp(s)
    for p, c5, cg5, sa in (L, R):
        p7 = p * (7.0 / 6.0)
        d = s - p
        q = lax.rsqrt(d + p7)
        rt = sa * q
        shock = d * rt
        shock_slope = rt * (1.0 + p7 * (q * q))
        power = cg5 * z
        rare = power - c5
        rare_slope = power * scaled
        up = d > 0.0
        value = value + jnp.where(up, shock, rare)
        term = jnp.where(up, shock_slope, rare_slope)
        slope = term if slope is None else slope + term
    return s - (value + value) * rcp(slope)


def first_star(L, R, du):
    z = (L[1] + R[1] - du) * rcp(L[2] + R[2])
    z2 = z * z
    z3 = z2 * z
    return newton(z3 * z3 * z, z, L, R, du)


def face_flux(UL, QL, UR, QR, n, scale=COURANT):
    uL, pL, uR, pR = QL[n], QL[3], QR[n], QR[3]
    du = uR - uL
    s = first_star([q.astype(BF16) for q in QL[3:7]], [q.astype(BF16) for q in QR[3:7]], du.astype(BF16))
    s = s.astype(F32)
    z = jnp.exp2(jnp.log2(s) * (1.0 / 7.0))
    s = newton(s, z, QL[3:7], QR[3:7], du)
    low, high = (
        root(jnp.maximum(q[7], q[7] * (1.0 / 7.0) + s * q[8])) for q in (QL, QR)
    )
    low = jnp.minimum(uL - low, 0.0)
    high = jnp.maximum(uR + high, 0.0)
    inv = rcp(high - low) * scale
    wL, wR = high * inv, low * inv
    a, b = wL * (uL - low), wR * (high - uR)
    eL, eR = wL * pL, wR * pR
    F = [a * UL[i] + b * UR[i] for i in range(5)]
    F[1 + n] = F[1 + n] + (eL - eR)
    F[4] = F[4] + (eL * uL - eR * uR)
    return F


def roll(x, by, axis):
    by = by % x.shape[axis]
    return x if by == 0 else pltpu.roll(x, by, axis)


def lanes(shape):
    return lax.broadcasted_iota(jnp.int32, shape, len(shape) - 1)


def block_transpose(vs, width):
    n = len(vs)
    block = lanes(vs[0].shape) // width
    vs = list(vs)
    d = n // 2
    while d:
        low = (block & d) == 0
        for i in range(n):
            if i & d == 0:
                a, b = vs[i], vs[i + d]
                vs[i] = jnp.where(low, a, roll(b, d * width, 1))
                vs[i + d] = jnp.where(low, roll(a, -d * width, 1), b)
        d //= 2
    return vs


def pick(x, index):
    return jnp.take_along_axis(x, index, axis=1)


NORMAL = (2, 2, 0, 0, 1, 1)


def next_x(a):
    return jnp.concatenate([a[8:32], roll(a[0:8], -1, 0)], axis=0)


def last_x(a):
    return jnp.concatenate([roll(a[24:32], 1, 0), a[0:24]], axis=0)


def collect(U, y, lane, B):
    lower, upper = lane == y, (lane + 1) % 32 == y
    for c in range(5):
        turned = pltpu.roll(U[c], y, 1)
        B[0, c] = jnp.where(lower, turned, B[0, c])
        B[1, c] = jnp.where(upper, turned, B[1, c])


def fine_load(patch, W, Q, B, T, arrived):
    lane = lanes((32, 128)) % 32
    for c in range(5):
        B[0, c] = jnp.zeros((32, 128), F32)
        B[1, c] = jnp.zeros((32, 128), F32)

    def body(yg, _):
        at = pl.ds(pl.multiple_of(yg * 128, 128), 128)
        arrived(yg)
        U = [[None] * 5 for _ in range(4)]
        for c in range(5):
            vs = block_transpose([patch[s, c, :, at] for s in range(4)], 32)
            for j in range(4):
                T[c, j] = vs[j]
        for c in range(5):
            for j in range(4):
                U[j][c] = jnp.concatenate([T[c, j, pl.ds(v, 8, 4), :] for v in range(4)], axis=0)
                W[c, 4 * yg + j] = U[j][c]
        for j in range(4):
            collect(U[j], 4 * yg + j, lane, B)
            for k, q in enumerate(primitives(U[j])):
                Q[k, 4 * yg + j] = q
        return 0

    lax.fori_loop(0, 8, body, 0)


def fine_edges(W, FY, B):
    for c in range(5):
        FY[c] = jnp.zeros((32, 128), F32)
        B[1, c] = roll(B[1, c], -31, 1)
        B[2, c] = W[c, :, 0, :]
        B[3, c] = W[c, :, 31, :]
        B[4, c] = W[c, 0]
        B[5, c] = W[c, 31]


def fine_interior(W, Q, FY, first, last):
    shape = (32, 128)
    row = lax.broadcasted_iota(jnp.int32, shape, 0)
    scale_x = jnp.where(row < 31, COURANT, 0.0)
    scale_z = jnp.where(lanes(shape) % 32 < 31, COURANT, 0.0)

    def body(pair, _):
        ys = (2 * pair, 2 * pair + 1, jnp.minimum(2 * pair + 2, 31))
        U = [[W[c, y] for c in range(5)] for y in ys]
        S = [[Q[k, y] for k in range(PRIMS)] for y in ys]
        before = [FY[c] for c in range(5)]
        results = []
        for n in range(2):
            scale = COURANT if n == 0 else jnp.where(jnp.broadcast_to(pair, shape) < 15, COURANT, 0.0)
            F = face_flux(U[n], S[n], U[n + 1], S[n + 1], 1, scale)
            total = [F[c] - before[c] for c in range(5)]
            before = F
            F = face_flux(
                U[n], S[n], [roll(a, -1, 1) for a in U[n]], [roll(a, -1, 1) for a in S[n]], 2, scale_z
            )
            total = [total[c] + (F[c] - roll(F[c], 1, 1)) for c in range(5)]
            F = face_flux(
                U[n], S[n], [next_x(a) for a in U[n]], [next_x(a) for a in S[n]], 0, scale_x
            )
            results.append([U[n][c] - (total[c] + (F[c] - last_x(F[c]))) for c in range(5)])
        for c in range(5):
            W[c, ys[0]] = results[0][c]
            W[c, ys[1]] = results[1][c]
            FY[c] = before[c]
        return 0

    lax.fori_loop(first // 2, last // 2, body, 0)


def fine_shells(got, sources, S, T16, mix=None):
    zeros = jnp.zeros((16, 128), F32)
    twice = lanes((16, 128)) // 2
    for g in range(4):
        blocks = []
        for s in range(4):
            at = pl.ds(16 * g, 16)
            block = got[sources[s], at, :]
            if mix is not None:
                block = 0.5 * (block + mix[sources[s], at, :])
            blocks.append(block)
        pieces = block_transpose(blocks + [zeros] * 4, 16)
        for k in range(8):
            q = 8 * g + k
            if q < 30:
                e, c = q // 5, q % 5
                out = pick(pieces[k], twice)
                if e in (2, 3):
                    S[e, c, pl.ds(0, 16, 2), :] = out
                    S[e, c, pl.ds(1, 16, 2), :] = out
                else:
                    T16[q] = out
                    even, odd = T16[q, pl.ds(0, 8, 2), :], T16[q, pl.ds(1, 8, 2), :]
                    S[e, c] = jnp.concatenate([even, even, odd, odd], axis=0)


def fine_boundary(B, S, FB, FS, first):
    for n in range(3):
        for face in (2 * n, 2 * n + 1):
            inner = [B[face, c] for c in range(5)]
            outer = [S[face, c] for c in range(5)]
            qi, qo = primitives(inner), primitives(outer)
            if face % 2 == 0:
                F = face_flux(outer, qo, inner, qi, NORMAL[face])
            else:
                F = face_flux(inner, qi, outer, qo, NORMAL[face])
            for c in range(5):
                FB[face, c] = F[c]
                FS[face, c] = F[c] if first else FS[face, c] + F[c]


def add_boundary(W, FB):
    for c in range(5):
        FB[1, c] = roll(FB[1, c], 31, 1)
        W[c, :, 0, :] = W[c, :, 0, :] + FB[2, c]
        W[c, :, 31, :] = W[c, :, 31, :] - FB[3, c]
        W[c, 0] = W[c, 0] + FB[4, c]
        W[c, 31] = W[c, 31] - FB[5, c]


def z_boundary(value, FB, c, y, lane):
    upper = jnp.where((lane + 1) % 32 == y, -FB[1, c], 0.0)
    return value + pltpu.roll(jnp.where(lane == y, FB[0, c], upper), 128 - y, 1)


def fine_again(W, FB, Q, B):
    lane = lanes((32, 128)) % 32

    def body(pair, _):
        for y in (2 * pair, 2 * pair + 1):
            U = []
            for c in range(5):
                U.append(z_boundary(W[c, y], FB, c, y, lane))
                W[c, y] = U[c]
            collect(U, y, lane, B)
            for k, q in enumerate(primitives(U)):
                Q[k, y] = q
        return 0

    lax.fori_loop(0, 16, body, 0)


def fine_store(W, FB, patch, count, out, T):
    lane = lanes((32, 128)) % 32

    def body(yg, _):
        at = pl.ds(pl.multiple_of(yg * 128, 128), 128)
        for c in range(5):
            for j in range(4):
                y = 4 * yg + j
                value = z_boundary(W[c, y], FB, c, y, lane)
                for v in range(4):
                    T[c, j, pl.ds(v, 8, 4), :] = value[8 * v : 8 * v + 8]
        for c in range(5):
            vs = block_transpose([T[c, j] for j in range(4)], 32)
            for s in range(4):
                out[s, c, :, at] = jnp.where(s < count, vs[s], patch[s, c, :, at])
        return 0

    lax.fori_loop(0, 8, body, 0)


def fine_pack(FS, PS, T16):
    half = (lanes((16, 128)) * 2) % 128
    for g in range(4):
        pieces = []
        for k in range(8):
            q = 8 * g + k
            if q >= 30:
                pieces.append(jnp.zeros((16, 128), F32))
                continue
            e, c = q // 5, q % 5
            if e in (2, 3):
                m = FS[e, c, pl.ds(0, 16, 2), :] + FS[e, c, pl.ds(1, 16, 2), :]
            else:
                T16[q, pl.ds(0, 8, 2), :] = FS[e, c, 0:8] + FS[e, c, 8:16]
                T16[q, pl.ds(1, 8, 2), :] = FS[e, c, 16:24] + FS[e, c, 24:32]
                m = T16[q]
            pieces.append(pick(m + roll(m, -1, 1), half))
        outs = block_transpose(pieces, 16)
        for s in range(4):
            PS[s, pl.ds(16 * g, 16), :] = outs[s]


def build_shells(field, sides, planes, PZ):
    shape = (16, 128)
    lane = lanes(shape)
    zeros = jnp.zeros(shape, F32)
    T = [zeros] * 10
    for x in range(16):
        here = lane % 16 == x
        for c in range(5):
            U = field[c, x, 0:16, :]
            T[c] = jnp.where(here, roll(U, x + 1, 1), T[c])
            T[5 + c] = jnp.where(here, roll(U, x - 16, 1), T[5 + c])
    z0 = jnp.concatenate(T[:8], axis=0).T
    z1 = jnp.concatenate(T[8:] + [zeros] * 6, axis=0).T
    for zb in range(8):
        PZ[zb, 0:16] = z0[16 * zb : 16 * zb + 16]
    for g in range(1, 4):
        vs = []
        for k in range(8):
            q = 8 * g + k
            vs.append(zeros if q < 10 or q >= 30 else sides[q // 5 - 2][q % 5])
        vs = block_transpose(vs, 16)
        for zb in range(8):
            value = vs[zb]
            if g == 1:
                value = jnp.where(lane < 32, z1[16 * zb : 16 * zb + 16], value)
            PZ[zb, 16 * g : 16 * g + 16] = value


def coarse_step(field, xlo, xhi, ylo, yhi, adv, FP, C, Q, FX):
    for c in range(5):
        for x in range(16):
            C[c, x, 0:16] = field[c, x]
            C[c, x, 16:24] = jnp.broadcast_to(yhi[c, x : x + 1], (8, 128))
        C[c, 16, 0:16] = xhi[c]
        C[c, 16, 16:24] = xhi[c, 8:16]

    def cells(x4, _):
        for x in range(4):
            for k, q in enumerate(primitives([C[c, 4 * x4 + x] for c in range(5)])):
                Q[k, 4 * x4 + x] = q
        return 0

    lax.fori_loop(0, 4, cells, 0)
    for k, q in enumerate(primitives([C[c, 16] for c in range(5)])):
        Q[k, 16] = q
    R = [field[c, 0] for c in range(5)]
    L = [xlo[c] for c in range(5)]
    F = face_flux(L, primitives(L), R, primitives(R), 0)
    for c in range(5):
        FP[2, c] = F[c]
        FX[c] = F[c]
    R = [field[c, :, 0, :] for c in range(5)]
    L = [ylo[c] for c in range(5)]
    F = face_flux(L, primitives(L), R, primitives(R), 1)
    for c in range(5):
        FP[4, c] = F[c]
        FP[0, c] = jnp.zeros((16, 128), F32)
    lane = lanes((16, 128)) % 16
    row = lax.broadcasted_iota(jnp.int32, (16, 128), 0)

    def body(pair, _):
        xs = (2 * pair, 2 * pair + 1, 2 * pair + 2)
        U24 = [[C[c, x] for c in range(5)] for x in xs]
        S24 = [[Q[k, x] for k in range(PRIMS)] for x in xs]
        U = [[a[0:16] for a in As] for As in U24]
        S = [[a[0:16] for a in As] for As in S24]
        below = [FX[c] for c in range(5)]
        corner = [[FP[4, c, pl.ds(x, 1), :] for c in range(5)] for x in xs[:2]]
        zs = [FP[0, c] for c in range(5)]
        results, tops = [], []
        for n in range(2):
            F = face_flux(U[n], S[n], U[n + 1], S[n + 1], 0)
            total = [F[c] - below[c] for c in range(5)]
            below = F
            F = face_flux(
                U[n], S[n], [roll(a, -1, 1) for a in U[n]], [roll(a, -1, 1) for a in S[n]], 2
            )
            for c in range(5):
                zs[c] = jnp.where(lane == xs[n], pltpu.roll(F[c], xs[n] + 1, 1), zs[c])
                total[c] = total[c] + (F[c] - roll(F[c], 1, 1))
            up = [[roll(a, -1, 0)[0:16] for a in As] for As in (U24[n], S24[n])]
            F = face_flux(U[n], S[n], up[0], up[1], 1)
            tops.append([a[15:16] for a in F])
            for c in range(5):
                before = jnp.where(row == 0, corner[n][c], roll(F[c], 1, 0))
                total[c] = total[c] + (F[c] - before)
            results.append([U[n][c] - total[c] for c in range(5)])
        for c in range(5):
            for n in range(2):
                adv[c, xs[n]] = results[n][c]
                FP[5, c, pl.ds(xs[n], 1), :] = tops[n][c]
            FP[0, c] = zs[c]
            FX[c] = below[c]
        return 0

    lax.fori_loop(0, 8, body, 0)
    for c in range(5):
        FP[3, c] = FX[c]
        FP[1, c] = roll(FP[0, c], -16, 1)


def owned_blocks(anchors, counts, me, owners):
    blocks = []
    for o in range(owners):
        block = jnp.int32(-1)
        for s in range(4):
            mine = jnp.logical_and(s < counts[o], anchors[0, s, o] == 16 * me)
            block = jnp.where(mine, anchors[2, s, o] // 16, block)
        blocks.append(block)
    return blocks


def pack_shells(blocks, field, sides, PZ, dense):
    build_shells(field, sides, None, PZ)
    for o, block in enumerate(blocks):
        dense[o] = PZ[jnp.maximum(block, 0)]


class Place:
    def __init__(self):
        self.i, self.j = lax.axis_index("gx"), lax.axis_index("gy")
        self.ni, self.nj = lax.axis_size("gx"), lax.axis_size("gy")

    def along_x(self, d):
        return (lax.rem(self.i + (d + self.ni), self.ni), self.j)

    def along_y(self, d):
        return (self.i, lax.rem(self.j + (d + self.nj), self.nj))

    def greet(self):
        barrier = pltpu.get_barrier_semaphore()
        for d in range(1, self.ni):
            pl.semaphore_signal(barrier, inc=1, device_id=self.along_x(d), device_id_type=MESH)
        for d in (1, -1):
            pl.semaphore_signal(barrier, inc=1, device_id=self.along_y(d), device_id_type=MESH)

    def greeted(self):
        pl.semaphore_wait(pltpu.get_barrier_semaphore(), self.ni + 1)

    def send(self, src, dst, send_sem, recv_sem, to):
        copy = pltpu.make_async_remote_copy(
            src_ref=src,
            dst_ref=dst,
            send_sem=send_sem,
            recv_sem=recv_sem,
            device_id=to,
            device_id_type=MESH,
        )
        copy.start()
        return copy

    def neighbours(self, planes, sides, sems):
        to = (self.along_x(1), self.along_x(-1), self.along_y(1), self.along_y(-1))
        return [
            self.send(planes[k], sides[k], sems.at[0, k], sems.at[1, k], to[k]) for k in range(4)
        ]

    def exchange(self, dense, got, sems):
        got[self.i] = dense[self.i]
        copies = []
        for d in range(1, self.ni):
            to = self.along_x(d)
            copies.append(
                self.send(dense.at[to[0]], got.at[self.i], sems.at[0, d], sems.at[1, d], to)
            )
        return copies


def wait(copies):
    for copy in copies:
        copy.wait()


def edge_planes(field, edges):
    for c in range(5):
        edges[0, c] = field[c, :, 15, :]
        edges[1, c] = field[c, :, 0, :]
    return (field.at[:, 15], field.at[:, 0], edges.at[0], edges.at[1])


def step_kernel(
    anchors_hbm, counts_hbm, patch_hbm, field_hbm, out_field, out, anchors, counts, patch, field, load_sems,
    W, Q, B, S1, S2, FB, FS, FY, PS, C, CQ, FX, adv, FP, PZ,
    dense_old, dense_new, dense_back, got_old, got_new, got_back, edges, D, sides, near_sems, far_sems, T, T16,
):
    place = Place()
    me = place.i

    def chunk(yg):
        at = pl.ds(pl.multiple_of(yg * 128, 128), 128)
        return pltpu.make_async_copy(
            patch_hbm.at[:, :, :, at], patch.at[:, :, :, at], load_sems.at[yg]
        )

    small = [
        pltpu.make_async_copy(field_hbm, field, load_sems.at[8]),
        pltpu.make_async_copy(anchors_hbm, anchors, load_sems.at[9]),
        pltpu.make_async_copy(counts_hbm, counts, load_sems.at[10]),
    ]
    chunk(0).start()
    for copy in small:
        copy.start()
    for yg in range(1, 8):
        chunk(yg).start()
    old, new, rims = ([sides.at[n, k] for k in range(4)] for n in range(3))
    place.greet()
    fine_load(patch, W, Q, B, T, lambda yg: chunk(yg).wait())
    wait(small)
    planes = edge_planes(field, edges.at[0])
    count = counts[me]
    sources = [anchors[0, s, me] // 16 for s in range(4)]
    blocks = owned_blocks(anchors, counts, me, place.ni)
    fine_edges(W, FY, B)
    place.greeted()
    near = place.neighbours(planes, old, near_sems.at[0])
    fine_interior(W, Q, FY, 0, 6)
    wait(near)
    pack_shells(blocks, field, old, PZ, dense_old)
    far_old = place.exchange(dense_old, got_old, far_sems.at[0])
    coarse_step(field, *old, adv, FP, C, CQ, FX)
    planes = edge_planes(adv, edges.at[1])
    near = place.neighbours(planes, new, near_sems.at[1])
    fine_interior(W, Q, FY, 6, 14)
    wait(near)
    pack_shells(blocks, adv, new, PZ, dense_new)
    far_new = place.exchange(dense_new, got_new, far_sems.at[1])
    fine_interior(W, Q, FY, 14, 32)
    wait(far_old)
    fine_shells(got_old, sources, S1, T16)
    fine_boundary(B, S1, FB, FS, True)
    add_boundary(W, FB)
    fine_again(W, FB, Q, B)
    fine_edges(W, FY, B)
    wait(far_new)
    fine_shells(got_old, sources, S2, T16, got_new)
    fine_boundary(B, S2, FB, FS, False)
    fine_pack(FS, PS, T16)
    for i in range(place.ni):
        slot = jnp.int32(0)
        for s in range(1, 4):
            slot = jnp.where(jnp.logical_and(s < count, sources[s] == i), s, slot)
        dense_back[i] = PS[slot]
    back = place.exchange(dense_back, got_back, far_sems.at[2])
    fine_interior(W, Q, FY, 0, 26)
    wait(back)
    reflux(blocks, adv, FP, got_back, out_field, D)
    near = place.neighbours([D.at[1], D.at[0], D.at[3], D.at[2]], rims, near_sems.at[2])
    fine_interior(W, Q, FY, 26, 32)
    add_boundary(W, FB)
    fine_store(W, FB, patch, count, out, T)
    wait(near)
    for c in range(5):
        out_field[c, 0] = out_field[c, 0] + sides[2, 0, c]
        out_field[c, 15] = out_field[c, 15] + sides[2, 1, c]
        out_field[c, :, 0, :] = out_field[c, :, 0, :] + sides[2, 2, c]
        out_field[c, :, 15, :] = out_field[c, :, 15, :] + sides[2, 3, c]


def reflux(blocks, adv, FP, got, out, D):
    shape = (16, 128)
    lane = lanes(shape)
    owner = [jnp.int32(0)] * 8
    present = [jnp.int32(0)] * 8
    for o, block in enumerate(blocks):
        for zb in range(8):
            owner[zb] = jnp.where(block == zb, o, owner[zb])
            present[zb] = jnp.where(block == zb, 1, present[zb])
    live = jnp.zeros(shape, jnp.int32)
    for zb in range(8):
        live = jnp.where(lane // 16 == zb, present[zb], live)
    live = live > 0
    delta = {}
    for g in range(4):
        vs = [got[owner[zb], pl.ds(16 * g, 16), :] for zb in range(8)]
        if g < 2:
            turned = jnp.concatenate(vs, axis=0).T
        if g > 0:
            vs = block_transpose(vs, 16)
        for k in range(8):
            q = 8 * g + k
            if q < 30:
                e, c = q // 5, q % 5
                mean = 0.125 * (turned[16 * k : 16 * k + 16] if q < 10 else vs[k])
                value = FP[e, c] - mean if e % 2 == 0 else mean - FP[e, c]
                value = jnp.where(live, value, 0.0)
                if e < 2:
                    delta[e, c] = value
                else:
                    D[e - 2, c] = value
    for c in range(5):
        for x in range(16):
            value = adv[c, x]
            value = value + jnp.where(lane % 16 == 15, roll(delta[0, c], -(x + 1), 1), 0.0)
            value = value + jnp.where(lane % 16 == 0, roll(delta[1, c], 16 - x, 1), 0.0)
            out[c, x] = value


def call(kernel, outs, n_in, scratch=(), collective=None):
    more = {}
    if collective is not None:
        more = {"collective_id": collective, "has_side_effects": True}
    return pl.pallas_call(
        kernel,
        out_shape=[jax.ShapeDtypeStruct(shape, F32) for shape in outs],
        in_specs=[pl.BlockSpec(memory_space=pltpu.HBM)] * n_in,
        out_specs=[pl.BlockSpec(memory_space=pltpu.VMEM)] * len(outs),
        scratch_shapes=[pltpu.VMEM(s, F32) if isinstance(s, tuple) else s for s in scratch],
        compiler_params=pltpu.CompilerParams(vmem_limit_bytes=VMEM_LIMIT, **more),
        cost_estimate=pl.CostEstimate(flops=10000000, bytes_accessed=4000000, transcendentals=0),
    )


def shards(coarse_state, patch_state, patch_anchor, patch_count):
    owners = lax.axis_size("gx")
    anchors = jnp.transpose(patch_anchor[:, 0], (2, 1, 0))
    counts = patch_count.reshape(-1)
    patch = patch_state.reshape(4, 5, 32, 1024)
    cube = (5, 32, 32, 128)
    prim = (PRIMS, 32, 32, 128)
    planes = (6, 5, 32, 128)
    field = (5, 16, 16, 128)
    side = (5, 16, 128)
    dense = (owners, 64, 128)
    dma = pltpu.SemaphoreType.DMA

    coarse_next, out = call(
        step_kernel,
        [field, (4, 5, 32, 1024)],
        4,
        [pltpu.SMEM((3, 4, owners), jnp.int32), pltpu.SMEM((owners,), jnp.int32)]
        + [(4, 5, 32, 1024), field, dma((11,)), cube, prim] + [planes] * 5 + [(5, 32, 128), (4, 64, 128)]
        + [(5, 17, 24, 128), (PRIMS, 17, 24, 128), side, field, (6,) + side, (8, 64, 128)]
        + [dense] * 6
        + [(2, 2) + side, (4,) + side, (3, 4) + side, dma((3, 2, 4)), dma((3, 2, owners)), (5, 4, 32, 128), (30, 16, 128)],
        0,
    )(anchors, counts, patch, coarse_state)
    return (coarse_next, out.reshape(patch_state.shape))


def solution(mesh):
    in_specs = (
        P(None, "gx", "gy", None),
        P("gx", "gy", None, None, None, None),
        P(None, "gy", None, None),
        P(None, "gy"),
    )
    out_specs = (P(None, "gx", "gy", None), P("gx", "gy", None, None, None, None))
    return jax.shard_map(shards, mesh=mesh, in_specs=in_specs, out_specs=out_specs, check_vma=False)
```

```python
import jax
import jax.numpy as jnp
from jax import lax
from jax.experimental import pallas as pl
from jax.experimental.pallas import tpu as pltpu
from jax.sharding import PartitionSpec as P

COURANT = 0.12
VMEM_LIMIT = 50 * 1024 * 1024
F32 = jnp.float32
BF16 = jnp.bfloat16
MESH = pl.DeviceIdType.MESH


def rcp(x):
    return pl.reciprocal(x, approx=True)


def root(x):
    return x * lax.rsqrt(x)


def primitives(U):
    r = rcp(U[0])
    u, v, w = U[1] * r, U[2] * r, U[3] * r
    p = 0.4 * (U[4] - 0.5 * (U[1] * u + U[2] * v + U[3] * w))
    cc = 1.4 * (p * r)
    c5 = 5.0 * root(cc)
    cg5 = c5 * jnp.exp2(jnp.log2(p) * (-1.0 / 7.0))
    return [u, v, w, p, c5, cg5, 1.2 * U[0], p * (1.0 / 6.0), cc, 1.2 * r]


PRIMS = 10


def newton(s, z, L, R, du):
    value, slope = du, None
    scaled = (2.0 / 7.0) * rcp(s)
    for p, c5, cg5, r12, p6 in (L, R):
        d = s - p
        rt = lax.rsqrt((s + p6) * r12)
        shock = d * rt
        shock_slope = rt * (2.0 - (shock * rt) * r12)
        power = cg5 * z
        rare = power - c5
        rare_slope = power * scaled
        up = d > 0.0
        value = value + jnp.where(up, shock, rare)
        term = jnp.where(up, shock_slope, rare_slope)
        slope = term if slope is None else slope + term
    return s - (value + value) * rcp(slope)


def first_star(L, R, du):
    z = (L[1] + R[1] - du) * rcp(L[2] + R[2])
    z2 = z * z
    z3 = z2 * z
    return newton(z3 * z3 * z, z, L, R, du)


def face_flux(UL, QL, UR, QR, n, scale=COURANT):
    uL, pL, uR, pR = QL[n], QL[3], QR[n], QR[3]
    du = uR - uL
    s = first_star([q.astype(BF16) for q in QL[3:8]], [q.astype(BF16) for q in QR[3:8]], du.astype(BF16))
    s = s.astype(F32)
    z = jnp.exp2(jnp.log2(s) * (1.0 / 7.0))
    s = newton(s, z, QL[3:8], QR[3:8], du)
    low, high = (root(jnp.maximum(q[8], (s + q[7]) * q[9])) for q in (QL, QR))
    low = jnp.minimum(uL - low, 0.0)
    high = jnp.maximum(uR + high, 0.0)
    inv = rcp(high - low) * scale
    wL, wR = high * inv, low * inv
    a, b = wL * (uL - low), wR * (high - uR)
    eL, eR = wL * pL, wR * pR
    F = [a * UL[i] + b * UR[i] for i in range(5)]
    F[1 + n] = F[1 + n] + (eL - eR)
    F[4] = F[4] + (eL * uL - eR * uR)
    return F


def roll(x, by, axis):
    by = by % x.shape[axis]
    return x if by == 0 else pltpu.roll(x, by, axis)


def lanes(shape):
    return lax.broadcasted_iota(jnp.int32, shape, len(shape) - 1)


def block_transpose(vs, width):
    n = len(vs)
    block = lanes(vs[0].shape) // width
    vs = list(vs)
    d = n // 2
    while d:
        low = (block & d) == 0
        for i in range(n):
            if i & d == 0:
                a, b = vs[i], vs[i + d]
                vs[i] = jnp.where(low, a, roll(b, d * width, 1))
                vs[i + d] = jnp.where(low, roll(a, -d * width, 1), b)
        d //= 2
    return vs


def pick(x, index):
    return jnp.take_along_axis(x, index, axis=1)


NORMAL = (2, 2, 0, 0, 1, 1)


def next_x(a):
    return jnp.concatenate([a[8:32], roll(a[0:8], -1, 0)], axis=0)


def last_x(a):
    return jnp.concatenate([roll(a[24:32], 1, 0), a[0:24]], axis=0)


def collect(U, y, lane, B):
    lower, upper = lane == y, (lane + 1) % 32 == y
    for c in range(5):
        turned = pltpu.roll(U[c], y, 1)
        B[0, c] = jnp.where(lower, turned, B[0, c])
        B[1, c] = jnp.where(upper, turned, B[1, c])


def fine_load(patch, W, Q, B, T, arrived):
    lane = lanes((32, 128)) % 32
    for c in range(5):
        B[0, c] = jnp.zeros((32, 128), F32)
        B[1, c] = jnp.zeros((32, 128), F32)

    def body(yg, _):
        at = pl.ds(pl.multiple_of(yg * 128, 128), 128)
        arrived(yg)
        U = [[None] * 5 for _ in range(4)]
        for c in range(5):
            vs = block_transpose([patch[s, c, :, at] for s in range(4)], 32)
            for j in range(4):
                T[c, j] = vs[j]
        for c in range(5):
            for j in range(4):
                U[j][c] = jnp.concatenate([T[c, j, pl.ds(v, 8, 4), :] for v in range(4)], axis=0)
                W[c, 4 * yg + j] = U[j][c]
        for j in range(4):
            collect(U[j], 4 * yg + j, lane, B)
            for k, q in enumerate(primitives(U[j])):
                Q[k, 4 * yg + j] = q
        return 0

    lax.fori_loop(0, 8, body, 0)


def fine_edges(W, FY, B):
    for c in range(5):
        FY[c] = jnp.zeros((32, 128), F32)
        B[1, c] = roll(B[1, c], -31, 1)
        B[2, c] = W[c, :, 0, :]
        B[3, c] = W[c, :, 31, :]
        B[4, c] = W[c, 0]
        B[5, c] = W[c, 31]


def fine_interior(W, Q, FY, first, last):
    shape = (32, 128)
    row = lax.broadcasted_iota(jnp.int32, shape, 0)
    scale_x = jnp.where(row < 31, COURANT, 0.0)
    scale_z = jnp.where(lanes(shape) % 32 < 31, COURANT, 0.0)

    def body(pair, _):
        ys = (2 * pair, 2 * pair + 1, jnp.minimum(2 * pair + 2, 31))
        U = [[W[c, y] for c in range(5)] for y in ys]
        S = [[Q[k, y] for k in range(PRIMS)] for y in ys]
        before = [FY[c] for c in range(5)]
        results = []
        for n in range(2):
            scale = COURANT if n == 0 else jnp.where(jnp.broadcast_to(pair, shape) < 15, COURANT, 0.0)
            F = face_flux(U[n], S[n], U[n + 1], S[n + 1], 1, scale)
            total = [F[c] - before[c] for c in range(5)]
            before = F
            F = face_flux(
                U[n], S[n], [roll(a, -1, 1) for a in U[n]], [roll(a, -1, 1) for a in S[n]], 2, scale_z
            )
            total = [total[c] + (F[c] - roll(F[c], 1, 1)) for c in range(5)]
            F = face_flux(
                U[n], S[n], [next_x(a) for a in U[n]], [next_x(a) for a in S[n]], 0, scale_x
            )
            results.append([U[n][c] - (total[c] + (F[c] - last_x(F[c]))) for c in range(5)])
        for c in range(5):
            W[c, ys[0]] = results[0][c]
            W[c, ys[1]] = results[1][c]
            FY[c] = before[c]
        return 0

    lax.fori_loop(first // 2, last // 2, body, 0)


def fine_shells(got, sources, S, T16, mix=None):
    zeros = jnp.zeros((16, 128), F32)
    twice = lanes((16, 128)) // 2
    for g in range(4):
        blocks = []
        for s in range(4):
            at = pl.ds(16 * g, 16)
            block = got[sources[s], at, :]
            if mix is not None:
                block = 0.5 * (block + mix[sources[s], at, :])
            blocks.append(block)
        pieces = block_transpose(blocks + [zeros] * 4, 16)
        for k in range(8):
            q = 8 * g + k
            if q < 30:
                e, c = q // 5, q % 5
                out = pick(pieces[k], twice)
                if e in (2, 3):
                    S[e, c, pl.ds(0, 16, 2), :] = out
                    S[e, c, pl.ds(1, 16, 2), :] = out
                else:
                    T16[q] = out
                    even, odd = T16[q, pl.ds(0, 8, 2), :], T16[q, pl.ds(1, 8, 2), :]
                    S[e, c] = jnp.concatenate([even, even, odd, odd], axis=0)


def fine_boundary(B, Q, S, FB, FS, first):
    for n in range(3):
        for face in (2 * n, 2 * n + 1):
            inner = [B[face, c] for c in range(5)]
            outer = [S[face, c] for c in range(5)]
            qo = primitives(outer)
            if n == 0:
                qi = primitives(inner)
            elif n == 1:
                qi = [Q[k, :, 31 * (face % 2), :] for k in range(PRIMS)]
            else:
                qi = [Q[k, 31 * (face % 2)] for k in range(PRIMS)]
            if face % 2 == 0:
                F = face_flux(outer, qo, inner, qi, NORMAL[face])
            else:
                F = face_flux(inner, qi, outer, qo, NORMAL[face])
            for c in range(5):
                FB[face, c] = F[c]
                FS[face, c] = F[c] if first else FS[face, c] + F[c]


def add_boundary(W, FB):
    for c in range(5):
        FB[1, c] = roll(FB[1, c], 31, 1)
        W[c, :, 0, :] = W[c, :, 0, :] + FB[2, c]
        W[c, :, 31, :] = W[c, :, 31, :] - FB[3, c]
        W[c, 0] = W[c, 0] + FB[4, c]
        W[c, 31] = W[c, 31] - FB[5, c]


def z_boundary(value, FB, c, y, lane):
    upper = jnp.where((lane + 1) % 32 == y, -FB[1, c], 0.0)
    return value + pltpu.roll(jnp.where(lane == y, FB[0, c], upper), 128 - y, 1)


def fine_again(W, FB, Q, B):
    lane = lanes((32, 128)) % 32

    def body(pair, _):
        for y in (2 * pair, 2 * pair + 1):
            U = []
            for c in range(5):
                U.append(z_boundary(W[c, y], FB, c, y, lane))
                W[c, y] = U[c]
            collect(U, y, lane, B)
            for k, q in enumerate(primitives(U)):
                Q[k, y] = q
        return 0

    lax.fori_loop(0, 16, body, 0)


def fine_store(W, FB, patch, count, out, T):
    lane = lanes((32, 128)) % 32

    def body(yg, _):
        at = pl.ds(pl.multiple_of(yg * 128, 128), 128)
        for c in range(5):
            for j in range(4):
                y = 4 * yg + j
                value = z_boundary(W[c, y], FB, c, y, lane)
                for v in range(4):
                    T[c, j, pl.ds(v, 8, 4), :] = value[8 * v : 8 * v + 8]
        for c in range(5):
            vs = block_transpose([T[c, j] for j in range(4)], 32)
            for s in range(4):
                out[s, c, :, at] = jnp.where(s < count, vs[s], patch[s, c, :, at])
        return 0

    lax.fori_loop(0, 8, body, 0)


def fine_pack(FS, PS, T16):
    half = (lanes((16, 128)) * 2) % 128
    for g in range(4):
        pieces = []
        for k in range(8):
            q = 8 * g + k
            if q >= 30:
                pieces.append(jnp.zeros((16, 128), F32))
                continue
            e, c = q // 5, q % 5
            if e in (2, 3):
                m = FS[e, c, pl.ds(0, 16, 2), :] + FS[e, c, pl.ds(1, 16, 2), :]
            else:
                T16[q, pl.ds(0, 8, 2), :] = FS[e, c, 0:8] + FS[e, c, 8:16]
                T16[q, pl.ds(1, 8, 2), :] = FS[e, c, 16:24] + FS[e, c, 24:32]
                m = T16[q]
            pieces.append(pick(m + roll(m, -1, 1), half))
        outs = block_transpose(pieces, 16)
        for s in range(4):
            PS[s, pl.ds(16 * g, 16), :] = outs[s]


def build_shells(field, sides, planes, PZ):
    shape = (16, 128)
    lane = lanes(shape)
    zeros = jnp.zeros(shape, F32)
    T = [zeros] * 10
    for x in range(16):
        here = lane % 16 == x
        for c in range(5):
            U = field[c, x, 0:16, :]
            T[c] = jnp.where(here, roll(U, x + 1, 1), T[c])
            T[5 + c] = jnp.where(here, roll(U, x - 16, 1), T[5 + c])
    z0 = jnp.concatenate(T[:8], axis=0).T
    z1 = jnp.concatenate(T[8:] + [zeros] * 6, axis=0).T
    for zb in range(8):
        PZ[zb, 0:16] = z0[16 * zb : 16 * zb + 16]
    for g in range(1, 4):
        vs = []
        for k in range(8):
            q = 8 * g + k
            vs.append(zeros if q < 10 or q >= 30 else sides[q // 5 - 2][q % 5])
        vs = block_transpose(vs, 16)
        for zb in range(8):
            value = vs[zb]
            if g == 1:
                value = jnp.where(lane < 32, z1[16 * zb : 16 * zb + 16], value)
            PZ[zb, 16 * g : 16 * g + 16] = value


def coarse_step(field, xlo, xhi, ylo, yhi, adv, FP, C, Q, FX):
    for c in range(5):
        for x in range(16):
            C[c, x, 0:16] = field[c, x]
            C[c, x, 16:24] = jnp.broadcast_to(yhi[c, x : x + 1], (8, 128))
        C[c, 16, 0:16] = xhi[c]
        C[c, 16, 16:24] = xhi[c, 8:16]

    def cells(x4, _):
        for x in range(4):
            for k, q in enumerate(primitives([C[c, 4 * x4 + x] for c in range(5)])):
                Q[k, 4 * x4 + x] = q
        return 0

    lax.fori_loop(0, 4, cells, 0)
    for k, q in enumerate(primitives([C[c, 16] for c in range(5)])):
        Q[k, 16] = q
    R = [field[c, 0] for c in range(5)]
    L = [xlo[c] for c in range(5)]
    F = face_flux(L, primitives(L), R, primitives(R), 0)
    for c in range(5):
        FP[2, c] = F[c]
        FX[c] = F[c]
    R = [field[c, :, 0, :] for c in range(5)]
    L = [ylo[c] for c in range(5)]
    F = face_flux(L, primitives(L), R, primitives(R), 1)
    for c in range(5):
        FP[4, c] = F[c]
        FP[0, c] = jnp.zeros((16, 128), F32)
    lane = lanes((16, 128)) % 16
    row = lax.broadcasted_iota(jnp.int32, (16, 128), 0)

    def body(pair, _):
        xs = (2 * pair, 2 * pair + 1, 2 * pair + 2)
        U24 = [[C[c, x] for c in range(5)] for x in xs]
        S24 = [[Q[k, x] for k in range(PRIMS)] for x in xs]
        U = [[a[0:16] for a in As] for As in U24]
        S = [[a[0:16] for a in As] for As in S24]
        below = [FX[c] for c in range(5)]
        corner = [[FP[4, c, pl.ds(x, 1), :] for c in range(5)] for x in xs[:2]]
        zs = [FP[0, c] for c in range(5)]
        results, tops = [], []
        for n in range(2):
            F = face_flux(U[n], S[n], U[n + 1], S[n + 1], 0)
            total = [F[c] - below[c] for c in range(5)]
            below = F
            F = face_flux(
                U[n], S[n], [roll(a, -1, 1) for a in U[n]], [roll(a, -1, 1) for a in S[n]], 2
            )
            for c in range(5):
                zs[c] = jnp.where(lane == xs[n], pltpu.roll(F[c], xs[n] + 1, 1), zs[c])
                total[c] = total[c] + (F[c] - roll(F[c], 1, 1))
            up = [[roll(a, -1, 0)[0:16] for a in As] for As in (U24[n], S24[n])]
            F = face_flux(U[n], S[n], up[0], up[1], 1)
            tops.append([a[15:16] for a in F])
            for c in range(5):
                before = jnp.where(row == 0, corner[n][c], roll(F[c], 1, 0))
                total[c] = total[c] + (F[c] - before)
            results.append([U[n][c] - total[c] for c in range(5)])
        for c in range(5):
            for n in range(2):
                adv[c, xs[n]] = results[n][c]
                FP[5, c, pl.ds(xs[n], 1), :] = tops[n][c]
            FP[0, c] = zs[c]
            FX[c] = below[c]
        return 0

    lax.fori_loop(0, 8, body, 0)
    for c in range(5):
        FP[3, c] = FX[c]
        FP[1, c] = roll(FP[0, c], -16, 1)


def owned_blocks(anchors, counts, me, owners):
    blocks = []
    for o in range(owners):
        block = jnp.int32(-1)
        for s in range(4):
            mine = jnp.logical_and(s < counts[o], anchors[0, s, o] == 16 * me)
            block = jnp.where(mine, anchors[2, s, o] // 16, block)
        blocks.append(block)
    return blocks


def pack_shells(blocks, field, sides, PZ, dense):
    build_shells(field, sides, None, PZ)
    for o, block in enumerate(blocks):
        dense[o] = PZ[jnp.maximum(block, 0)]


class Place:
    def __init__(self):
        self.i, self.j = lax.axis_index("gx"), lax.axis_index("gy")
        self.ni, self.nj = lax.axis_size("gx"), lax.axis_size("gy")

    def along_x(self, d):
        return (lax.rem(self.i + (d + self.ni), self.ni), self.j)

    def along_y(self, d):
        return (self.i, lax.rem(self.j + (d + self.nj), self.nj))

    def greet(self):
        barrier = pltpu.get_barrier_semaphore()
        for d in range(1, self.ni):
            pl.semaphore_signal(barrier, inc=1, device_id=self.along_x(d), device_id_type=MESH)
        for d in (1, -1):
            pl.semaphore_signal(barrier, inc=1, device_id=self.along_y(d), device_id_type=MESH)

    def greeted(self):
        pl.semaphore_wait(pltpu.get_barrier_semaphore(), self.ni + 1)

    def send(self, src, dst, send_sem, recv_sem, to):
        copy = pltpu.make_async_remote_copy(
            src_ref=src,
            dst_ref=dst,
            send_sem=send_sem,
            recv_sem=recv_sem,
            device_id=to,
            device_id_type=MESH,
        )
        copy.start()
        return copy

    def neighbours(self, planes, sides, sems):
        to = (self.along_x(1), self.along_x(-1), self.along_y(1), self.along_y(-1))
        return [
            self.send(planes[k], sides[k], sems.at[0, k], sems.at[1, k], to[k]) for k in range(4)
        ]

    def exchange(self, dense, got, sems):
        got[self.i] = dense[self.i]
        copies = []
        for d in range(1, self.ni):
            to = self.along_x(d)
            copies.append(
                self.send(dense.at[to[0]], got.at[self.i], sems.at[0, d], sems.at[1, d], to)
            )
        return copies


def wait(copies):
    for copy in copies:
        copy.wait()


def edge_planes(field, edges):
    for c in range(5):
        edges[0, c] = field[c, :, 15, :]
        edges[1, c] = field[c, :, 0, :]
    return (field.at[:, 15], field.at[:, 0], edges.at[0], edges.at[1])


def step_kernel(
    anchors_hbm, counts_hbm, patch_hbm, field_hbm, out_field, out, anchors, counts, patch, field, load_sems,
    W, Q, B, S1, S2, FB, FS, FY, PS, C, CQ, FX, adv, FP, PZ,
    dense_old, dense_new, dense_back, got_old, got_new, got_back, edges, D, sides, near_sems, far_sems, T, T16,
):
    place = Place()
    me = place.i

    def chunk(yg):
        at = pl.ds(pl.multiple_of(yg * 128, 128), 128)
        return pltpu.make_async_copy(
            patch_hbm.at[:, :, :, at], patch.at[:, :, :, at], load_sems.at[yg]
        )

    small = [
        pltpu.make_async_copy(field_hbm, field, load_sems.at[8]),
        pltpu.make_async_copy(anchors_hbm, anchors, load_sems.at[9]),
        pltpu.make_async_copy(counts_hbm, counts, load_sems.at[10]),
    ]
    chunk(0).start()
    for copy in small:
        copy.start()
    for yg in range(1, 8):
        chunk(yg).start()
    old, new, rims = ([sides.at[n, k] for k in range(4)] for n in range(3))
    place.greet()
    fine_load(patch, W, Q, B, T, lambda yg: chunk(yg).wait())
    wait(small)
    planes = edge_planes(field, edges.at[0])
    count = counts[me]
    sources = [anchors[0, s, me] // 16 for s in range(4)]
    blocks = owned_blocks(anchors, counts, me, place.ni)
    fine_edges(W, FY, B)
    place.greeted()
    near = place.neighbours(planes, old, near_sems.at[0])
    fine_interior(W, Q, FY, 0, 4)
    wait(near)
    pack_shells(blocks, field, old, PZ, dense_old)
    far_old = place.exchange(dense_old, got_old, far_sems.at[0])
    coarse_step(field, *old, adv, FP, C, CQ, FX)
    planes = edge_planes(adv, edges.at[1])
    near = place.neighbours(planes, new, near_sems.at[1])
    fine_interior(W, Q, FY, 4, 10)
    wait(near)
    pack_shells(blocks, adv, new, PZ, dense_new)
    far_new = place.exchange(dense_new, got_new, far_sems.at[1])
    fine_interior(W, Q, FY, 10, 32)
    wait(far_old)
    fine_shells(got_old, sources, S1, T16)
    fine_boundary(B, Q, S1, FB, FS, True)
    add_boundary(W, FB)
    fine_again(W, FB, Q, B)
    fine_edges(W, FY, B)
    wait(far_new)
    fine_shells(got_old, sources, S2, T16, got_new)
    fine_boundary(B, Q, S2, FB, FS, False)
    fine_pack(FS, PS, T16)
    for i in range(place.ni):
        slot = jnp.int32(0)
        for s in range(1, 4):
            slot = jnp.where(jnp.logical_and(s < count, sources[s] == i), s, slot)
        dense_back[i] = PS[slot]
    back = place.exchange(dense_back, got_back, far_sems.at[2])
    fine_interior(W, Q, FY, 0, 28)
    wait(back)
    reflux(blocks, adv, FP, got_back, out_field, D)
    near = place.neighbours([D.at[1], D.at[0], D.at[3], D.at[2]], rims, near_sems.at[2])
    fine_interior(W, Q, FY, 28, 32)
    add_boundary(W, FB)
    fine_store(W, FB, patch, count, out, T)
    wait(near)
    for c in range(5):
        out_field[c, 0] = out_field[c, 0] + sides[2, 0, c]
        out_field[c, 15] = out_field[c, 15] + sides[2, 1, c]
        out_field[c, :, 0, :] = out_field[c, :, 0, :] + sides[2, 2, c]
        out_field[c, :, 15, :] = out_field[c, :, 15, :] + sides[2, 3, c]


def reflux(blocks, adv, FP, got, out, D):
    shape = (16, 128)
    lane = lanes(shape)
    owner = [jnp.int32(0)] * 8
    present = [jnp.int32(0)] * 8
    for o, block in enumerate(blocks):
        for zb in range(8):
            owner[zb] = jnp.where(block == zb, o, owner[zb])
            present[zb] = jnp.where(block == zb, 1, present[zb])
    live = jnp.zeros(shape, jnp.int32)
    for zb in range(8):
        live = jnp.where(lane // 16 == zb, present[zb], live)
    live = live > 0
    delta = {}
    for g in range(4):
        vs = [got[owner[zb], pl.ds(16 * g, 16), :] for zb in range(8)]
        if g < 2:
            turned = jnp.concatenate(vs, axis=0).T
        if g > 0:
            vs = block_transpose(vs, 16)
        for k in range(8):
            q = 8 * g + k
            if q < 30:
                e, c = q // 5, q % 5
                mean = 0.125 * (turned[16 * k : 16 * k + 16] if q < 10 else vs[k])
                value = FP[e, c] - mean if e % 2 == 0 else mean - FP[e, c]
                value = jnp.where(live, value, 0.0)
                if e < 2:
                    delta[e, c] = value
                else:
                    D[e - 2, c] = value
    for c in range(5):
        for x in range(16):
            value = adv[c, x]
            value = value + jnp.where(lane % 16 == 15, roll(delta[0, c], -(x + 1), 1), 0.0)
            value = value + jnp.where(lane % 16 == 0, roll(delta[1, c], 16 - x, 1), 0.0)
            out[c, x] = value


def call(kernel, outs, n_in, scratch=(), collective=None):
    more = {}
    if collective is not None:
        more = {"collective_id": collective, "has_side_effects": True}
    return pl.pallas_call(
        kernel,
        out_shape=[jax.ShapeDtypeStruct(shape, F32) for shape in outs],
        in_specs=[pl.BlockSpec(memory_space=pltpu.HBM)] * n_in,
        out_specs=[pl.BlockSpec(memory_space=pltpu.VMEM)] * len(outs),
        scratch_shapes=[pltpu.VMEM(s, F32) if isinstance(s, tuple) else s for s in scratch],
        compiler_params=pltpu.CompilerParams(vmem_limit_bytes=VMEM_LIMIT, **more),
        cost_estimate=pl.CostEstimate(flops=10000000, bytes_accessed=4000000, transcendentals=0),
    )


def shards(coarse_state, patch_state, patch_anchor, patch_count):
    owners = lax.axis_size("gx")
    anchors = jnp.transpose(patch_anchor[:, 0], (2, 1, 0))
    counts = patch_count.reshape(-1)
    patch = patch_state.reshape(4, 5, 32, 1024)
    cube = (5, 32, 32, 128)
    prim = (PRIMS, 32, 32, 128)
    planes = (6, 5, 32, 128)
    field = (5, 16, 16, 128)
    side = (5, 16, 128)
    dense = (owners, 64, 128)
    dma = pltpu.SemaphoreType.DMA

    coarse_next, out = call(
        step_kernel,
        [field, (4, 5, 32, 1024)],
        4,
        [pltpu.SMEM((3, 4, owners), jnp.int32), pltpu.SMEM((owners,), jnp.int32)]
        + [(4, 5, 32, 1024), field, dma((11,)), cube, prim] + [planes] * 5 + [(5, 32, 128), (4, 64, 128)]
        + [(5, 17, 24, 128), (PRIMS, 17, 24, 128), side, field, (6,) + side, (8, 64, 128)]
        + [dense] * 6
        + [(2, 2) + side, (4,) + side, (3, 4) + side, dma((3, 2, 4)), dma((3, 2, owners)), (5, 4, 32, 128), (30, 16, 128)],
        0,
    )(*(pltpu.with_memory_space_constraint(a, pltpu.HBM) for a in (anchors, counts, patch, coarse_state)))
    return (coarse_next, out.reshape(patch_state.shape))


def solution(mesh):
    in_specs = (
        P(None, "gx", "gy", None),
        P("gx", "gy", None, None, None, None),
        P(None, "gy", None, None),
        P(None, "gy"),
    )
    out_specs = (P(None, "gx", "gy", None), P("gx", "gy", None, None, None, None))
    return jax.shard_map(shards, mesh=mesh, in_specs=in_specs, out_specs=out_specs, check_vma=False)
```

```python
import jax
import jax.numpy as jnp
from jax import lax
from jax.experimental import pallas as pl
from jax.experimental.pallas import tpu as pltpu
from jax.sharding import PartitionSpec as P

COURANT = 0.12
VMEM_LIMIT = 50 * 1024 * 1024
F32 = jnp.float32
BF16 = jnp.bfloat16
MESH = pl.DeviceIdType.MESH


def rcp(x):
    return pl.reciprocal(x, approx=True)


def root(x):
    return x * lax.rsqrt(x)


def primitives(U):
    r = rcp(U[0])
    u, v, w = U[1] * r, U[2] * r, U[3] * r
    p = 0.4 * (U[4] - 0.5 * (U[1] * u + U[2] * v + U[3] * w))
    cc = 1.4 * (p * r)
    c5 = 5.0 * root(cc)
    cg5 = c5 * jnp.exp2(jnp.log2(p) * (-1.0 / 7.0))
    return [u, v, w, p, c5, cg5, 1.2 * U[0], p * (1.0 / 6.0), cc, 1.2 * r]


PRIMS = 10


def newton(s, z, L, R, du):
    value, slope = du, None
    scaled = (2.0 / 7.0) * rcp(s)
    for p, c5, cg5, r12, p6 in (L, R):
        d = s - p
        rt = lax.rsqrt((s + p6) * r12)
        shock = d * rt
        shock_slope = rt * (2.0 - (shock * rt) * r12)
        power = cg5 * z
        rare = power - c5
        rare_slope = power * scaled
        up = d > 0.0
        value = value + jnp.where(up, shock, rare)
        term = jnp.where(up, shock_slope, rare_slope)
        slope = term if slope is None else slope + term
    return s - (value + value) * rcp(slope)


def first_star(L, R, du):
    z = (L[1] + R[1] - du) * rcp(L[2] + R[2])
    z2 = z * z
    z3 = z2 * z
    return newton(z3 * z3 * z, z, L, R, du)


def face_flux(UL, QL, UR, QR, n, scale=COURANT):
    uL, pL, uR, pR = QL[n], QL[3], QR[n], QR[3]
    du = uR - uL
    s = first_star([q.astype(BF16) for q in QL[3:8]], [q.astype(BF16) for q in QR[3:8]], du.astype(BF16))
    s = s.astype(F32)
    z = jnp.exp2(jnp.log2(s) * (1.0 / 7.0))
    s = newton(s, z, QL[3:8], QR[3:8], du)
    low, high = (root(jnp.maximum(q[8], (s + q[7]) * q[9])) for q in (QL, QR))
    low = jnp.minimum(uL - low, 0.0)
    high = jnp.maximum(uR + high, 0.0)
    inv = rcp(high - low) * scale
    wL, wR = high * inv, low * inv
    a, b = wL * (uL - low), wR * (high - uR)
    eL, eR = wL * pL, wR * pR
    F = [a * UL[i] + b * UR[i] for i in range(5)]
    F[1 + n] = F[1 + n] + (eL - eR)
    F[4] = F[4] + (eL * uL - eR * uR)
    return F


def roll(x, by, axis):
    by = by % x.shape[axis]
    return x if by == 0 else pltpu.roll(x, by, axis)


def lanes(shape):
    return lax.broadcasted_iota(jnp.int32, shape, len(shape) - 1)


def block_transpose(vs, width):
    n = len(vs)
    block = lanes(vs[0].shape) // width
    vs = list(vs)
    d = n // 2
    while d:
        low = (block & d) == 0
        for i in range(n):
            if i & d == 0:
                a, b = vs[i], vs[i + d]
                vs[i] = jnp.where(low, a, roll(b, d * width, 1))
                vs[i + d] = jnp.where(low, roll(a, -d * width, 1), b)
        d //= 2
    return vs


def pick(x, index):
    return jnp.take_along_axis(x, index, axis=1)


NORMAL = (2, 2, 0, 0, 1, 1)


def next_x(a):
    return jnp.concatenate([a[8:32], roll(a[0:8], -1, 0)], axis=0)


def last_x(a):
    return jnp.concatenate([roll(a[24:32], 1, 0), a[0:24]], axis=0)


def collect(U, y, lane, planes):
    lower, upper = lane == y, (lane + 1) % 32 == y
    for c in range(5):
        turned = pltpu.roll(U[c], y, 1)
        planes[0][c] = jnp.where(lower, turned, planes[0][c])
        planes[1][c] = jnp.where(upper, turned, planes[1][c])


def z_planes(B):
    return [[B[side, c] for c in range(5)] for side in range(2)]


def put_planes(B, planes):
    for side in range(2):
        for c in range(5):
            B[side, c] = planes[side][c]


def fine_load(patch, W, Q, B, T, arrived):
    lane = lanes((32, 128)) % 32
    for c in range(5):
        B[0, c] = jnp.zeros((32, 128), F32)
        B[1, c] = jnp.zeros((32, 128), F32)

    def body(yg, _):
        at = pl.ds(pl.multiple_of(yg * 128, 128), 128)
        arrived(yg)
        U = [[None] * 5 for _ in range(4)]
        for c in range(5):
            vs = block_transpose([patch[s, c, :, at] for s in range(4)], 32)
            for j in range(4):
                T[c, j] = vs[j]
        for c in range(5):
            for j in range(4):
                U[j][c] = jnp.concatenate([T[c, j, pl.ds(v, 8, 4), :] for v in range(4)], axis=0)
                W[c, 4 * yg + j] = U[j][c]
        planes = z_planes(B)
        for j in range(4):
            collect(U[j], 4 * yg + j, lane, planes)
        put_planes(B, planes)
        for j in range(4):
            for k, q in enumerate(primitives(U[j])):
                Q[k, 4 * yg + j] = q
        return 0

    lax.fori_loop(0, 8, body, 0)


def fine_edges(W, FY, B):
    for c in range(5):
        FY[c] = jnp.zeros((32, 128), F32)
        B[1, c] = roll(B[1, c], -31, 1)
        B[2, c] = W[c, :, 0, :]
        B[3, c] = W[c, :, 31, :]
        B[4, c] = W[c, 0]
        B[5, c] = W[c, 31]


def fine_interior(W, Q, FY, first, last):
    shape = (32, 128)
    row = lax.broadcasted_iota(jnp.int32, shape, 0)
    scale_x = jnp.where(row < 31, COURANT, 0.0)
    scale_z = jnp.where(lanes(shape) % 32 < 31, COURANT, 0.0)

    def body(pair, _):
        ys = (2 * pair, 2 * pair + 1, jnp.minimum(2 * pair + 2, 31))
        U = [[W[c, y] for c in range(5)] for y in ys]
        S = [[Q[k, y] for k in range(PRIMS)] for y in ys]
        before = [FY[c] for c in range(5)]
        results = []
        for n in range(2):
            scale = COURANT if n == 0 else jnp.where(jnp.broadcast_to(pair, shape) < 15, COURANT, 0.0)
            F = face_flux(U[n], S[n], U[n + 1], S[n + 1], 1, scale)
            total = [F[c] - before[c] for c in range(5)]
            before = F
            F = face_flux(
                U[n], S[n], [roll(a, -1, 1) for a in U[n]], [roll(a, -1, 1) for a in S[n]], 2, scale_z
            )
            total = [total[c] + (F[c] - roll(F[c], 1, 1)) for c in range(5)]
            F = face_flux(
                U[n], S[n], [next_x(a) for a in U[n]], [next_x(a) for a in S[n]], 0, scale_x
            )
            results.append([U[n][c] - (total[c] + (F[c] - last_x(F[c]))) for c in range(5)])
        for c in range(5):
            W[c, ys[0]] = results[0][c]
            W[c, ys[1]] = results[1][c]
            FY[c] = before[c]
        return 0

    lax.fori_loop(first // 2, last // 2, body, 0)


def fine_shells(got, sources, S, T16, mix=None):
    zeros = jnp.zeros((16, 128), F32)
    twice = lanes((16, 128)) // 2
    for g in range(4):
        blocks = []
        for s in range(4):
            at = pl.ds(16 * g, 16)
            block = got[sources[s], at, :]
            if mix is not None:
                block = 0.5 * (block + mix[sources[s], at, :])
            blocks.append(block)
        pieces = block_transpose(blocks + [zeros] * 4, 16)
        for k in range(8):
            q = 8 * g + k
            if q < 30:
                e, c = q // 5, q % 5
                out = pick(pieces[k], twice)
                if e in (2, 3):
                    S[e, c, pl.ds(0, 16, 2), :] = out
                    S[e, c, pl.ds(1, 16, 2), :] = out
                else:
                    T16[q] = out
                    even, odd = T16[q, pl.ds(0, 8, 2), :], T16[q, pl.ds(1, 8, 2), :]
                    S[e, c] = jnp.concatenate([even, even, odd, odd], axis=0)


def fine_boundary(B, Q, S, FB, FS, first):
    for n in range(3):
        for face in (2 * n, 2 * n + 1):
            inner = [B[face, c] for c in range(5)]
            outer = [S[face, c] for c in range(5)]
            qo = primitives(outer)
            if n == 0:
                qi = primitives(inner)
            elif n == 1:
                qi = [Q[k, :, 31 * (face % 2), :] for k in range(PRIMS)]
            else:
                qi = [Q[k, 31 * (face % 2)] for k in range(PRIMS)]
            if face % 2 == 0:
                F = face_flux(outer, qo, inner, qi, NORMAL[face])
            else:
                F = face_flux(inner, qi, outer, qo, NORMAL[face])
            for c in range(5):
                FB[face, c] = F[c]
                FS[face, c] = F[c] if first else FS[face, c] + F[c]


def add_boundary(W, FB):
    for c in range(5):
        FB[1, c] = roll(FB[1, c], 31, 1)
        W[c, :, 0, :] = W[c, :, 0, :] + FB[2, c]
        W[c, :, 31, :] = W[c, :, 31, :] - FB[3, c]
        W[c, 0] = W[c, 0] + FB[4, c]
        W[c, 31] = W[c, 31] - FB[5, c]


def z_boundary(value, FB, c, y, lane):
    upper = jnp.where((lane + 1) % 32 == y, -FB[1, c], 0.0)
    return value + pltpu.roll(jnp.where(lane == y, FB[0, c], upper), 128 - y, 1)


def fine_again(W, FB, Q, B):
    lane = lanes((32, 128)) % 32

    def body(yg, _):
        planes = z_planes(B)
        for j in range(4):
            y = 4 * yg + j
            U = [z_boundary(W[c, y], FB, c, y, lane) for c in range(5)]
            for c in range(5):
                W[c, y] = U[c]
            collect(U, y, lane, planes)
            for k, q in enumerate(primitives(U)):
                Q[k, y] = q
        put_planes(B, planes)
        return 0

    lax.fori_loop(0, 8, body, 0)


def fine_store(W, FB, patch, count, out, T):
    lane = lanes((32, 128)) % 32

    def body(yg, _):
        at = pl.ds(pl.multiple_of(yg * 128, 128), 128)
        for c in range(5):
            for j in range(4):
                y = 4 * yg + j
                value = z_boundary(W[c, y], FB, c, y, lane)
                for v in range(4):
                    T[c, j, pl.ds(v, 8, 4), :] = value[8 * v : 8 * v + 8]
        for c in range(5):
            vs = block_transpose([T[c, j] for j in range(4)], 32)
            for s in range(4):
                out[s, c, :, at] = jnp.where(s < count, vs[s], patch[s, c, :, at])
        return 0

    lax.fori_loop(0, 8, body, 0)


def fine_pack(FS, PS, T16):
    half = (lanes((16, 128)) * 2) % 128
    for g in range(4):
        pieces = []
        for k in range(8):
            q = 8 * g + k
            if q >= 30:
                pieces.append(jnp.zeros((16, 128), F32))
                continue
            e, c = q // 5, q % 5
            if e in (2, 3):
                m = FS[e, c, pl.ds(0, 16, 2), :] + FS[e, c, pl.ds(1, 16, 2), :]
            else:
                T16[q, pl.ds(0, 8, 2), :] = FS[e, c, 0:8] + FS[e, c, 8:16]
                T16[q, pl.ds(1, 8, 2), :] = FS[e, c, 16:24] + FS[e, c, 24:32]
                m = T16[q]
            pieces.append(pick(m + roll(m, -1, 1), half))
        outs = block_transpose(pieces, 16)
        for s in range(4):
            PS[s, pl.ds(16 * g, 16), :] = outs[s]


def build_shells(field, sides, planes, PZ):
    shape = (16, 128)
    lane = lanes(shape)
    zeros = jnp.zeros(shape, F32)
    T = [zeros] * 10
    for x in range(16):
        here = lane % 16 == x
        for c in range(5):
            U = field[c, x, 0:16, :]
            turned = roll(U, x, 1)
            T[c] = jnp.where((lane + 1) % 16 == x, turned, T[c])
            T[5 + c] = jnp.where(here, turned, T[5 + c])
    T = [roll(a, 1, 1) for a in T[:5]] + [roll(a, -16, 1) for a in T[5:]]
    z0 = jnp.concatenate(T[:8], axis=0).T
    z1 = jnp.concatenate(T[8:] + [zeros] * 6, axis=0).T
    for zb in range(8):
        PZ[zb, 0:16] = z0[16 * zb : 16 * zb + 16]
    for g in range(1, 4):
        vs = []
        for k in range(8):
            q = 8 * g + k
            vs.append(zeros if q < 10 or q >= 30 else sides[q // 5 - 2][q % 5])
        vs = block_transpose(vs, 16)
        for zb in range(8):
            value = vs[zb]
            if g == 1:
                value = jnp.where(lane < 32, z1[16 * zb : 16 * zb + 16], value)
            PZ[zb, 16 * g : 16 * g + 16] = value


def coarse_step(field, xlo, xhi, ylo, yhi, adv, FP, C, Q, FX):
    for c in range(5):
        for x in range(16):
            C[c, x, 0:16] = field[c, x]
            C[c, x, 16:24] = jnp.broadcast_to(yhi[c, x : x + 1], (8, 128))
        C[c, 16, 0:16] = xhi[c]
        C[c, 16, 16:24] = xhi[c, 8:16]

    def cells(x4, _):
        for x in range(4):
            for k, q in enumerate(primitives([C[c, 4 * x4 + x] for c in range(5)])):
                Q[k, 4 * x4 + x] = q
        return 0

    lax.fori_loop(0, 4, cells, 0)
    for k, q in enumerate(primitives([C[c, 16] for c in range(5)])):
        Q[k, 16] = q
    R = [field[c, 0] for c in range(5)]
    L = [xlo[c] for c in range(5)]
    F = face_flux(L, primitives(L), R, primitives(R), 0)
    for c in range(5):
        FP[2, c] = F[c]
        FX[c] = F[c]
    R = [field[c, :, 0, :] for c in range(5)]
    L = [ylo[c] for c in range(5)]
    F = face_flux(L, primitives(L), R, primitives(R), 1)
    for c in range(5):
        FP[4, c] = F[c]
        FP[0, c] = jnp.zeros((16, 128), F32)
    lane = lanes((16, 128)) % 16
    row = lax.broadcasted_iota(jnp.int32, (16, 128), 0)

    def body(pair, _):
        xs = (2 * pair, 2 * pair + 1, 2 * pair + 2)
        U24 = [[C[c, x] for c in range(5)] for x in xs]
        S24 = [[Q[k, x] for k in range(PRIMS)] for x in xs]
        U = [[a[0:16] for a in As] for As in U24]
        S = [[a[0:16] for a in As] for As in S24]
        below = [FX[c] for c in range(5)]
        corner = [[FP[4, c, pl.ds(x, 1), :] for c in range(5)] for x in xs[:2]]
        zs = [FP[0, c] for c in range(5)]
        results, tops = [], []
        for n in range(2):
            F = face_flux(U[n], S[n], U[n + 1], S[n + 1], 0)
            total = [F[c] - below[c] for c in range(5)]
            below = F
            F = face_flux(
                U[n], S[n], [roll(a, -1, 1) for a in U[n]], [roll(a, -1, 1) for a in S[n]], 2
            )
            for c in range(5):
                zs[c] = jnp.where(lane == xs[n], pltpu.roll(F[c], xs[n] + 1, 1), zs[c])
                total[c] = total[c] + (F[c] - roll(F[c], 1, 1))
            up = [[roll(a, -1, 0)[0:16] for a in As] for As in (U24[n], S24[n])]
            F = face_flux(U[n], S[n], up[0], up[1], 1)
            tops.append([a[15:16] for a in F])
            for c in range(5):
                before = jnp.where(row == 0, corner[n][c], roll(F[c], 1, 0))
                total[c] = total[c] + (F[c] - before)
            results.append([U[n][c] - total[c] for c in range(5)])
        for c in range(5):
            for n in range(2):
                adv[c, xs[n]] = results[n][c]
                FP[5, c, pl.ds(xs[n], 1), :] = tops[n][c]
            FP[0, c] = zs[c]
            FX[c] = below[c]
        return 0

    lax.fori_loop(0, 8, body, 0)
    for c in range(5):
        FP[3, c] = FX[c]
        FP[1, c] = roll(FP[0, c], -16, 1)


def owned_blocks(anchors, counts, me, owners):
    blocks = []
    for o in range(owners):
        block = jnp.int32(-1)
        for s in range(4):
            mine = jnp.logical_and(s < counts[o], anchors[0, s, o] == 16 * me)
            block = jnp.where(mine, anchors[2, s, o] // 16, block)
        blocks.append(block)
    return blocks


def pack_shells(blocks, field, sides, PZ, dense):
    build_shells(field, sides, None, PZ)
    for o, block in enumerate(blocks):
        dense[o] = PZ[jnp.maximum(block, 0)]


class Place:
    def __init__(self):
        self.i, self.j = lax.axis_index("gx"), lax.axis_index("gy")
        self.ni, self.nj = lax.axis_size("gx"), lax.axis_size("gy")

    def along_x(self, d):
        return (lax.rem(self.i + (d + self.ni), self.ni), self.j)

    def along_y(self, d):
        return (self.i, lax.rem(self.j + (d + self.nj), self.nj))

    def greet(self):
        barrier = pltpu.get_barrier_semaphore()
        for d in range(1, self.ni):
            pl.semaphore_signal(barrier, inc=1, device_id=self.along_x(d), device_id_type=MESH)
        for d in (1, -1):
            pl.semaphore_signal(barrier, inc=1, device_id=self.along_y(d), device_id_type=MESH)

    def greeted(self):
        pl.semaphore_wait(pltpu.get_barrier_semaphore(), self.ni + 1)

    def send(self, src, dst, send_sem, recv_sem, to):
        copy = pltpu.make_async_remote_copy(
            src_ref=src,
            dst_ref=dst,
            send_sem=send_sem,
            recv_sem=recv_sem,
            device_id=to,
            device_id_type=MESH,
        )
        copy.start()
        return copy

    def neighbours(self, planes, sides, sems):
        to = (self.along_x(1), self.along_x(-1), self.along_y(1), self.along_y(-1))
        return [
            self.send(planes[k], sides[k], sems.at[0, k], sems.at[1, k], to[k]) for k in range(4)
        ]

    def exchange(self, dense, got, sems):
        got[self.i] = dense[self.i]
        copies = []
        for d in range(1, self.ni):
            to = self.along_x(d)
            copies.append(
                self.send(dense.at[to[0]], got.at[self.i], sems.at[0, d], sems.at[1, d], to)
            )
        return copies


def wait(copies):
    for copy in copies:
        copy.wait()


def edge_planes(field, edges):
    for c in range(5):
        edges[0, c] = field[c, :, 15, :]
        edges[1, c] = field[c, :, 0, :]
    return (field.at[:, 15], field.at[:, 0], edges.at[0], edges.at[1])


def step_kernel(
    anchors_hbm, counts_hbm, patch_hbm, field_hbm, out_field, out, anchors, counts, patch, field, load_sems,
    W, Q, B, S1, S2, FB, FS, FY, PS, C, CQ, FX, adv, FP, PZ,
    dense_old, dense_new, dense_back, got_old, got_new, got_back, edges, D, sides, near_sems, far_sems, T, T16,
):
    place = Place()
    me = place.i

    def chunk(yg):
        at = pl.ds(pl.multiple_of(yg * 128, 128), 128)
        return pltpu.make_async_copy(
            patch_hbm.at[:, :, :, at], patch.at[:, :, :, at], load_sems.at[yg]
        )

    small = [
        pltpu.make_async_copy(field_hbm, field, load_sems.at[8]),
        pltpu.make_async_copy(anchors_hbm, anchors, load_sems.at[9]),
        pltpu.make_async_copy(counts_hbm, counts, load_sems.at[10]),
    ]
    chunk(0).start()
    for copy in small:
        copy.start()
    for yg in range(1, 8):
        chunk(yg).start()
    old, new, rims = ([sides.at[n, k] for k in range(4)] for n in range(3))
    place.greet()
    fine_load(patch, W, Q, B, T, lambda yg: chunk(yg).wait())
    wait(small)
    planes = edge_planes(field, edges.at[0])
    count = counts[me]
    sources = [anchors[0, s, me] // 16 for s in range(4)]
    blocks = owned_blocks(anchors, counts, me, place.ni)
    fine_edges(W, FY, B)
    place.greeted()
    near = place.neighbours(planes, old, near_sems.at[0])
    fine_interior(W, Q, FY, 0, 4)
    wait(near)
    pack_shells(blocks, field, old, PZ, dense_old)
    far_old = place.exchange(dense_old, got_old, far_sems.at[0])
    coarse_step(field, *old, adv, FP, C, CQ, FX)
    planes = edge_planes(adv, edges.at[1])
    near = place.neighbours(planes, new, near_sems.at[1])
    fine_interior(W, Q, FY, 4, 10)
    wait(near)
    pack_shells(blocks, adv, new, PZ, dense_new)
    far_new = place.exchange(dense_new, got_new, far_sems.at[1])
    fine_interior(W, Q, FY, 10, 32)
    wait(far_old)
    fine_shells(got_old, sources, S1, T16)
    fine_boundary(B, Q, S1, FB, FS, True)
    add_boundary(W, FB)
    fine_again(W, FB, Q, B)
    fine_edges(W, FY, B)
    wait(far_new)
    fine_shells(got_old, sources, S2, T16, got_new)
    fine_boundary(B, Q, S2, FB, FS, False)
    fine_pack(FS, PS, T16)
    for i in range(place.ni):
        slot = jnp.int32(0)
        for s in range(1, 4):
            slot = jnp.where(jnp.logical_and(s < count, sources[s] == i), s, slot)
        dense_back[i] = PS[slot]
    back = place.exchange(dense_back, got_back, far_sems.at[2])
    fine_interior(W, Q, FY, 0, 28)
    wait(back)
    reflux(blocks, adv, FP, got_back, out_field, D)
    near = place.neighbours([D.at[1], D.at[0], D.at[3], D.at[2]], rims, near_sems.at[2])
    fine_interior(W, Q, FY, 28, 32)
    add_boundary(W, FB)
    fine_store(W, FB, patch, count, out, T)
    wait(near)
    for c in range(5):
        out_field[c, 0] = out_field[c, 0] + sides[2, 0, c]
        out_field[c, 15] = out_field[c, 15] + sides[2, 1, c]
        out_field[c, :, 0, :] = out_field[c, :, 0, :] + sides[2, 2, c]
        out_field[c, :, 15, :] = out_field[c, :, 15, :] + sides[2, 3, c]


def write_kernel(field, patch, out_field, out, sems):
    copies = [
        pltpu.make_async_copy(patch, out, sems.at[0]),
        pltpu.make_async_copy(field, out_field, sems.at[1]),
    ]
    for copy in copies:
        copy.start()
    wait(copies)


def reflux(blocks, adv, FP, got, out, D):
    shape = (16, 128)
    lane = lanes(shape)
    owner = [jnp.int32(0)] * 8
    present = [jnp.int32(0)] * 8
    for o, block in enumerate(blocks):
        for zb in range(8):
            owner[zb] = jnp.where(block == zb, o, owner[zb])
            present[zb] = jnp.where(block == zb, 1, present[zb])
    live = jnp.zeros(shape, jnp.int32)
    for zb in range(8):
        live = jnp.where(lane // 16 == zb, present[zb], live)
    live = live > 0
    delta = {}
    for g in range(4):
        vs = [got[owner[zb], pl.ds(16 * g, 16), :] for zb in range(8)]
        if g < 2:
            turned = jnp.concatenate(vs, axis=0).T
        if g > 0:
            vs = block_transpose(vs, 16)
        for k in range(8):
            q = 8 * g + k
            if q < 30:
                e, c = q // 5, q % 5
                mean = 0.125 * (turned[16 * k : 16 * k + 16] if q < 10 else vs[k])
                value = FP[e, c] - mean if e % 2 == 0 else mean - FP[e, c]
                value = jnp.where(live, value, 0.0)
                if e < 2:
                    delta[e, c] = value
                else:
                    D[e - 2, c] = value
    column = lane % 16
    for c in range(5):
        lower, upper = roll(delta[0, c], -1, 1), roll(delta[1, c], 16, 1)
        for x in range(16):
            both = jnp.where((column + 1) % 16 == x, lower, 0.0)
            out[c, x] = adv[c, x] + roll(jnp.where(column == x, upper, both), -x, 1)


def call(kernel, outs, n_in, spaces, scratch=(), collective=None):
    more = {}
    if collective is not None:
        more = {"collective_id": collective, "has_side_effects": True}
    return pl.pallas_call(
        kernel,
        out_shape=[jax.ShapeDtypeStruct(shape, F32) for shape in outs],
        in_specs=[pl.BlockSpec(memory_space=spaces[0])] * n_in,
        out_specs=[pl.BlockSpec(memory_space=spaces[1])] * len(outs),
        scratch_shapes=[pltpu.VMEM(s, F32) if isinstance(s, tuple) else s for s in scratch],
        compiler_params=pltpu.CompilerParams(vmem_limit_bytes=VMEM_LIMIT, **more),
        cost_estimate=pl.CostEstimate(flops=10000000, bytes_accessed=4000000, transcendentals=0),
    )


def shards(coarse_state, patch_state, patch_anchor, patch_count):
    owners = lax.axis_size("gx")
    anchors = jnp.transpose(patch_anchor[:, 0], (2, 1, 0))
    counts = patch_count.reshape(-1)
    patch = patch_state.reshape(4, 5, 32, 1024)
    cube = (5, 32, 32, 128)
    prim = (PRIMS, 32, 32, 128)
    planes = (6, 5, 32, 128)
    field = (5, 16, 16, 128)
    side = (5, 16, 128)
    dense = (owners, 64, 128)
    dma = pltpu.SemaphoreType.DMA

    results = [field, (4, 5, 32, 1024)]
    made = call(
        step_kernel,
        results,
        4,
        (pltpu.HBM, pltpu.VMEM),
        [pltpu.SMEM((3, 4, owners), jnp.int32), pltpu.SMEM((owners,), jnp.int32)]
        + [(4, 5, 32, 1024), field, dma((11,)), cube, prim] + [planes] * 5 + [(5, 32, 128), (4, 64, 128)]
        + [(5, 17, 24, 128), (PRIMS, 17, 24, 128), side, field, (6,) + side, (8, 64, 128)]
        + [dense] * 6
        + [(2, 2) + side, (4,) + side, (3, 4) + side, dma((3, 2, 4)), dma((3, 2, owners)), (5, 4, 32, 128), (30, 16, 128)],
        0,
    )(*(pltpu.with_memory_space_constraint(a, pltpu.HBM) for a in (anchors, counts, patch, coarse_state)))
    made = (pltpu.with_memory_space_constraint(a, pltpu.VMEM) for a in made)
    coarse_next, out = call(write_kernel, results, 2, (pltpu.VMEM, pltpu.HBM), [dma((2,))])(*made)
    return (coarse_next, out.reshape(patch_state.shape))


def solution(mesh):
    in_specs = (
        P(None, "gx", "gy", None),
        P("gx", "gy", None, None, None, None),
        P(None, "gy", None, None),
        P(None, "gy"),
    )
    out_specs = (P(None, "gx", "gy", None), P("gx", "gy", None, None, None, None))
    return jax.shard_map(shards, mesh=mesh, in_specs=in_specs, out_specs=out_specs, check_vma=False)
```

```python
import jax
import jax.numpy as jnp
from jax import lax
from jax.experimental import pallas as pl
from jax.experimental.pallas import tpu as pltpu
from jax.sharding import PartitionSpec as P

COURANT = 0.12
VMEM_LIMIT = 50 * 1024 * 1024
F32 = jnp.float32
BF16 = jnp.bfloat16
MESH = pl.DeviceIdType.MESH


def rcp(x):
    return pl.reciprocal(x, approx=True)


def root(x):
    return x * lax.rsqrt(x)


def primitives(U):
    r = rcp(U[0])
    u, v, w = U[1] * r, U[2] * r, U[3] * r
    p = 0.4 * (U[4] - 0.5 * (U[1] * u + U[2] * v + U[3] * w))
    cc = 1.4 * (p * r)
    c5 = 5.0 * root(cc)
    cg5 = c5 * jnp.exp2(jnp.log2(p) * (-1.0 / 7.0))
    return [u, v, w, p, c5, cg5, 1.2 * U[0], p * (1.0 / 6.0), cc, 1.2 * r]


PRIMS = 10


def newton(s, z, L, R, du):
    value, slope = du, None
    scaled = (2.0 / 7.0) * rcp(s)
    for p, c5, cg5, r12, p6 in (L, R):
        d = s - p
        rt = lax.rsqrt((s + p6) * r12)
        shock = d * rt
        shock_slope = rt * (2.0 - (shock * rt) * r12)
        power = cg5 * z
        rare = power - c5
        rare_slope = power * scaled
        up = d > 0.0
        value = value + jnp.where(up, shock, rare)
        term = jnp.where(up, shock_slope, rare_slope)
        slope = term if slope is None else slope + term
    return s - (value + value) * rcp(slope)


def first_star(L, R, du):
    z = (L[1] + R[1] - du) * rcp(L[2] + R[2])
    z2 = z * z
    z3 = z2 * z
    return newton(z3 * z3 * z, z, L, R, du)


def face_flux(UL, QL, UR, QR, n, scale=COURANT):
    uL, pL, uR, pR = QL[n], QL[3], QR[n], QR[3]
    du = uR - uL
    s = first_star([q.astype(BF16) for q in QL[3:8]], [q.astype(BF16) for q in QR[3:8]], du.astype(BF16))
    s = s.astype(F32)
    z = jnp.exp2(jnp.log2(s) * (1.0 / 7.0))
    s = newton(s, z, QL[3:8], QR[3:8], du)
    low, high = (root(jnp.maximum(q[8], (s + q[7]) * q[9])) for q in (QL, QR))
    low = jnp.minimum(uL - low, 0.0)
    high = jnp.maximum(uR + high, 0.0)
    inv = rcp(high - low) * scale
    wL, wR = high * inv, low * inv
    a, b = wL * (uL - low), wR * (high - uR)
    eL, eR = wL * pL, wR * pR
    F = [a * UL[i] + b * UR[i] for i in range(5)]
    F[1 + n] = F[1 + n] + (eL - eR)
    F[4] = F[4] + (eL * uL - eR * uR)
    return F


def roll(x, by, axis):
    by = by % x.shape[axis]
    return x if by == 0 else pltpu.roll(x, by, axis)


def lanes(shape):
    return lax.broadcasted_iota(jnp.int32, shape, len(shape) - 1)


def block_transpose(vs, width):
    n = len(vs)
    block = lanes(vs[0].shape) // width
    vs = list(vs)
    d = n // 2
    while d:
        low = (block & d) == 0
        for i in range(n):
            if i & d == 0:
                a, b = vs[i], vs[i + d]
                vs[i] = jnp.where(low, a, roll(b, d * width, 1))
                vs[i + d] = jnp.where(low, roll(a, -d * width, 1), b)
        d //= 2
    return vs


def pick(x, index):
    return jnp.take_along_axis(x, index, axis=1)


def next_x(a):
    return jnp.concatenate([a[8:32], roll(a[0:8], -1, 0)], axis=0)


def last_x(a):
    return jnp.concatenate([roll(a[24:32], 1, 0), a[0:24]], axis=0)


def collect(U, y, lane, planes):
    lower, upper = lane == y, (lane + 1) % 32 == y
    for c in range(5):
        turned = pltpu.roll(U[c], y, 1)
        planes[0][c] = jnp.where(lower, turned, planes[0][c])
        planes[1][c] = jnp.where(upper, turned, planes[1][c])


def z_planes(B):
    return [[B[side, c] for c in range(5)] for side in range(2)]


def put_planes(B, planes):
    for side in range(2):
        for c in range(5):
            B[side, c] = planes[side][c]


def fine_load(patch, W, Q, B, T, arrived):
    lane = lanes((32, 128)) % 32
    for c in range(5):
        B[0, c] = jnp.zeros((32, 128), F32)
        B[1, c] = jnp.zeros((32, 128), F32)

    def body(yg, _):
        at = pl.ds(pl.multiple_of(yg * 128, 128), 128)
        arrived(yg)
        U = [[None] * 5 for _ in range(4)]
        for c in range(5):
            vs = block_transpose([patch[s, c, :, at] for s in range(4)], 32)
            for j in range(4):
                T[c, j] = vs[j]
        for c in range(5):
            for j in range(4):
                U[j][c] = jnp.concatenate([T[c, j, pl.ds(v, 8, 4), :] for v in range(4)], axis=0)
                W[c, 4 * yg + j] = U[j][c]
        planes = z_planes(B)
        for j in range(4):
            collect(U[j], 4 * yg + j, lane, planes)
        put_planes(B, planes)
        for j in range(4):
            for k, q in enumerate(primitives(U[j])):
                Q[k, 4 * yg + j] = q
        return 0

    lax.fori_loop(0, 8, body, 0)


def fine_edges(W, FY, B):
    for c in range(5):
        FY[c] = jnp.zeros((32, 128), F32)
        B[1, c] = roll(B[1, c], -31, 1)
        B[2, c] = W[c, :, 0, :]
        B[3, c] = W[c, :, 31, :]
        B[4, c] = W[c, 0]
        B[5, c] = W[c, 31]


def fine_interior(W, Q, FY, first, last):
    shape = (32, 128)
    row = lax.broadcasted_iota(jnp.int32, shape, 0)
    scale_x = jnp.where(row < 31, COURANT, 0.0)
    scale_z = jnp.where(lanes(shape) % 32 < 31, COURANT, 0.0)

    def body(pair, _):
        ys = (2 * pair, 2 * pair + 1, jnp.minimum(2 * pair + 2, 31))
        U = [[W[c, y] for c in range(5)] for y in ys]
        S = [[Q[k, y] for k in range(PRIMS)] for y in ys]
        before = [FY[c] for c in range(5)]
        results = []
        for n in range(2):
            scale = COURANT if n == 0 else jnp.where(jnp.broadcast_to(pair, shape) < 15, COURANT, 0.0)
            F = face_flux(U[n], S[n], U[n + 1], S[n + 1], 1, scale)
            total = [F[c] - before[c] for c in range(5)]
            before = F
            F = face_flux(
                U[n], S[n], [roll(a, -1, 1) for a in U[n]], [roll(a, -1, 1) for a in S[n]], 2, scale_z
            )
            total = [total[c] + (F[c] - roll(F[c], 1, 1)) for c in range(5)]
            F = face_flux(
                U[n], S[n], [next_x(a) for a in U[n]], [next_x(a) for a in S[n]], 0, scale_x
            )
            results.append([U[n][c] - (total[c] + (F[c] - last_x(F[c]))) for c in range(5)])
        for c in range(5):
            W[c, ys[0]] = results[0][c]
            W[c, ys[1]] = results[1][c]
            FY[c] = before[c]
        return 0

    lax.fori_loop(first // 2, last // 2, body, 0)


def fine_shells(got, sources, S, T16, mix=None):
    zeros = jnp.zeros((16, 128), F32)
    twice = lanes((16, 128)) // 2
    for g in range(4):
        blocks = []
        for s in range(4):
            at = pl.ds(16 * g, 16)
            block = got[sources[s], at, :]
            if mix is not None:
                block = 0.5 * (block + mix[sources[s], at, :])
            blocks.append(block)
        pieces = block_transpose(blocks + [zeros] * 4, 16)
        for k in range(8):
            q = 8 * g + k
            if q < 30:
                e, c = q // 5, q % 5
                out = pick(pieces[k], twice)
                if e in (2, 3):
                    S[e, c, pl.ds(0, 16, 2), :] = out
                    S[e, c, pl.ds(1, 16, 2), :] = out
                else:
                    T16[q] = out
                    even, odd = T16[q, pl.ds(0, 8, 2), :], T16[q, pl.ds(1, 8, 2), :]
                    S[e, c] = jnp.concatenate([even, even, odd, odd], axis=0)


def fine_boundary(B, S, FB, FS, first):
    def body(n, _):
        axis = lax.rem(n + 2, 3)
        order = (0, 1 + axis, 1 + lax.rem(axis + 1, 3), 1 + lax.rem(axis + 2, 3), 4)
        for side in range(2):
            face = 2 * n + side
            inner = [B[face, c] for c in order]
            outer = [S[face, c] for c in order]
            qi, qo = primitives(inner), primitives(outer)
            if side == 0:
                F = face_flux(outer, qo, inner, qi, 0)
            else:
                F = face_flux(inner, qi, outer, qo, 0)
            for k, c in enumerate(order):
                FB[face, c] = F[k]
                FS[face, c] = F[k] if first else FS[face, c] + F[k]
        return 0

    lax.fori_loop(0, 3, body, 0)


def add_boundary(W, FB):
    for c in range(5):
        FB[1, c] = roll(FB[1, c], 31, 1)
        W[c, :, 0, :] = W[c, :, 0, :] + FB[2, c]
        W[c, :, 31, :] = W[c, :, 31, :] - FB[3, c]
        W[c, 0] = W[c, 0] + FB[4, c]
        W[c, 31] = W[c, 31] - FB[5, c]


def z_boundary(value, FB, c, y, lane):
    upper = jnp.where((lane + 1) % 32 == y, -FB[1, c], 0.0)
    return value + pltpu.roll(jnp.where(lane == y, FB[0, c], upper), 128 - y, 1)


def fine_again(W, FB, Q, B):
    lane = lanes((32, 128)) % 32

    def body(yg, _):
        planes = z_planes(B)
        for j in range(4):
            y = 4 * yg + j
            U = [z_boundary(W[c, y], FB, c, y, lane) for c in range(5)]
            for c in range(5):
                W[c, y] = U[c]
            collect(U, y, lane, planes)
            for k, q in enumerate(primitives(U)):
                Q[k, y] = q
        put_planes(B, planes)
        return 0

    lax.fori_loop(0, 8, body, 0)


def fine_store(W, FB, patch, count, out, T):
    lane = lanes((32, 128)) % 32

    def body(yg, _):
        at = pl.ds(pl.multiple_of(yg * 128, 128), 128)
        for c in range(5):
            for j in range(4):
                y = 4 * yg + j
                value = z_boundary(W[c, y], FB, c, y, lane)
                for v in range(4):
                    T[c, j, pl.ds(v, 8, 4), :] = value[8 * v : 8 * v + 8]
        for c in range(5):
            vs = block_transpose([T[c, j] for j in range(4)], 32)
            for s in range(4):
                out[s, c, :, at] = jnp.where(s < count, vs[s], patch[s, c, :, at])
        return 0

    lax.fori_loop(0, 8, body, 0)


def fine_pack(FS, PS, T16):
    half = (lanes((16, 128)) * 2) % 128
    for g in range(4):
        pieces = []
        for k in range(8):
            q = 8 * g + k
            if q >= 30:
                pieces.append(jnp.zeros((16, 128), F32))
                continue
            e, c = q // 5, q % 5
            if e in (2, 3):
                m = FS[e, c, pl.ds(0, 16, 2), :] + FS[e, c, pl.ds(1, 16, 2), :]
            else:
                T16[q, pl.ds(0, 8, 2), :] = FS[e, c, 0:8] + FS[e, c, 8:16]
                T16[q, pl.ds(1, 8, 2), :] = FS[e, c, 16:24] + FS[e, c, 24:32]
                m = T16[q]
            pieces.append(pick(m + roll(m, -1, 1), half))
        outs = block_transpose(pieces, 16)
        for s in range(4):
            PS[s, pl.ds(16 * g, 16), :] = outs[s]


def build_shells(field, sides, planes, PZ):
    shape = (16, 128)
    lane = lanes(shape)
    zeros = jnp.zeros(shape, F32)

    def collected(x, T):
        lower, upper = (lane + 1) % 16 == x, lane % 16 == x
        out = list(T)
        for c in range(5):
            turned = pltpu.roll(field[c, x], x, 1)
            out[c] = jnp.where(lower, turned, T[c])
            out[5 + c] = jnp.where(upper, turned, T[5 + c])
        return tuple(out)

    T = lax.fori_loop(0, 16, collected, (zeros,) * 10)
    T = [roll(a, 1, 1) for a in T[:5]] + [roll(a, -16, 1) for a in T[5:]]
    z0 = jnp.concatenate(T[:8], axis=0).T
    z1 = jnp.concatenate(T[8:] + [zeros] * 6, axis=0).T
    for zb in range(8):
        PZ[zb, 0:16] = z0[16 * zb : 16 * zb + 16]
    for g in range(1, 4):
        vs = []
        for k in range(8):
            q = 8 * g + k
            vs.append(zeros if q < 10 or q >= 30 else sides[q // 5 - 2][q % 5])
        vs = block_transpose(vs, 16)
        for zb in range(8):
            value = vs[zb]
            if g == 1:
                value = jnp.where(lane < 32, z1[16 * zb : 16 * zb + 16], value)
            PZ[zb, 16 * g : 16 * g + 16] = value


def coarse_step(field, xlo, xhi, ylo, yhi, adv, FP, C, Q, FX):
    def fill(x, _):
        for c in range(5):
            C[c, x, 0:16] = field[c, x]
            C[c, x, 16:24] = jnp.broadcast_to(yhi[c, pl.ds(x, 1), :], (8, 128))
        return 0

    lax.fori_loop(0, 16, fill, 0)
    for c in range(5):
        C[c, 16, 0:16] = xhi[c]
        C[c, 16, 16:24] = xhi[c, 8:16]

    def cells(x4, _):
        for x in range(4):
            for k, q in enumerate(primitives([C[c, 4 * x4 + x] for c in range(5)])):
                Q[k, 4 * x4 + x] = q
        return 0

    lax.fori_loop(0, 4, cells, 0)
    for k, q in enumerate(primitives([C[c, 16] for c in range(5)])):
        Q[k, 16] = q
    R = [field[c, 0] for c in range(5)]
    L = [xlo[c] for c in range(5)]
    F = face_flux(L, primitives(L), R, primitives(R), 0)
    for c in range(5):
        FP[2, c] = F[c]
        FX[c] = F[c]
    R = [field[c, :, 0, :] for c in range(5)]
    L = [ylo[c] for c in range(5)]
    F = face_flux(L, primitives(L), R, primitives(R), 1)
    for c in range(5):
        FP[4, c] = F[c]
        FP[0, c] = jnp.zeros((16, 128), F32)
    lane = lanes((16, 128)) % 16
    row = lax.broadcasted_iota(jnp.int32, (16, 128), 0)

    def body(pair, _):
        xs = (2 * pair, 2 * pair + 1, 2 * pair + 2)
        U24 = [[C[c, x] for c in range(5)] for x in xs]
        S24 = [[Q[k, x] for k in range(PRIMS)] for x in xs]
        U = [[a[0:16] for a in As] for As in U24]
        S = [[a[0:16] for a in As] for As in S24]
        below = [FX[c] for c in range(5)]
        corner = [[FP[4, c, pl.ds(x, 1), :] for c in range(5)] for x in xs[:2]]
        zs = [FP[0, c] for c in range(5)]
        results, tops = [], []
        for n in range(2):
            F = face_flux(U[n], S[n], U[n + 1], S[n + 1], 0)
            total = [F[c] - below[c] for c in range(5)]
            below = F
            F = face_flux(
                U[n], S[n], [roll(a, -1, 1) for a in U[n]], [roll(a, -1, 1) for a in S[n]], 2
            )
            for c in range(5):
                zs[c] = jnp.where(lane == xs[n], pltpu.roll(F[c], xs[n] + 1, 1), zs[c])
                total[c] = total[c] + (F[c] - roll(F[c], 1, 1))
            up = [[roll(a, -1, 0)[0:16] for a in As] for As in (U24[n], S24[n])]
            F = face_flux(U[n], S[n], up[0], up[1], 1)
            tops.append([a[15:16] for a in F])
            for c in range(5):
                before = jnp.where(row == 0, corner[n][c], roll(F[c], 1, 0))
                total[c] = total[c] + (F[c] - before)
            results.append([U[n][c] - total[c] for c in range(5)])
        for c in range(5):
            for n in range(2):
                adv[c, xs[n]] = results[n][c]
                FP[5, c, pl.ds(xs[n], 1), :] = tops[n][c]
            FP[0, c] = zs[c]
            FX[c] = below[c]
        return 0

    lax.fori_loop(0, 8, body, 0)
    for c in range(5):
        FP[3, c] = FX[c]
        FP[1, c] = roll(FP[0, c], -16, 1)


def owned_blocks(anchors, counts, me, owners):
    blocks = []
    for o in range(owners):
        block = jnp.int32(-1)
        for s in range(4):
            mine = jnp.logical_and(s < counts[o], anchors[0, s, o] == 16 * me)
            block = jnp.where(mine, anchors[2, s, o] // 16, block)
        blocks.append(block)
    return blocks


def pack_shells(blocks, field, sides, PZ, dense):
    build_shells(field, sides, None, PZ)
    for o, block in enumerate(blocks):
        dense[o] = PZ[jnp.maximum(block, 0)]


class Place:
    def __init__(self):
        self.i, self.j = lax.axis_index("gx"), lax.axis_index("gy")
        self.ni, self.nj = lax.axis_size("gx"), lax.axis_size("gy")

    def along_x(self, d):
        return (lax.rem(self.i + (d + self.ni), self.ni), self.j)

    def along_y(self, d):
        return (self.i, lax.rem(self.j + (d + self.nj), self.nj))

    def greet(self):
        barrier = pltpu.get_barrier_semaphore()
        for d in range(1, self.ni):
            pl.semaphore_signal(barrier, inc=1, device_id=self.along_x(d), device_id_type=MESH)
        for d in (1, -1):
            pl.semaphore_signal(barrier, inc=1, device_id=self.along_y(d), device_id_type=MESH)

    def greeted(self):
        pl.semaphore_wait(pltpu.get_barrier_semaphore(), self.ni + 1)

    def send(self, src, dst, send_sem, recv_sem, to):
        copy = pltpu.make_async_remote_copy(
            src_ref=src,
            dst_ref=dst,
            send_sem=send_sem,
            recv_sem=recv_sem,
            device_id=to,
            device_id_type=MESH,
        )
        copy.start()
        return copy

    def neighbours(self, planes, sides, sems):
        to = (self.along_x(1), self.along_x(-1), self.along_y(1), self.along_y(-1))
        return [
            self.send(planes[k], sides[k], sems.at[0, k], sems.at[1, k], to[k]) for k in range(4)
        ]

    def exchange(self, dense, got, sems):
        got[self.i] = dense[self.i]
        copies = []
        for d in range(1, self.ni):
            to = self.along_x(d)
            copies.append(
                self.send(dense.at[to[0]], got.at[self.i], sems.at[0, d], sems.at[1, d], to)
            )
        return copies


def wait(copies):
    for copy in copies:
        copy.wait()


def edge_planes(field, edges):
    for c in range(5):
        edges[0, c] = field[c, :, 15, :]
        edges[1, c] = field[c, :, 0, :]
    return (field.at[:, 15], field.at[:, 0], edges.at[0], edges.at[1])


def step_kernel(
    anchors_hbm, counts_hbm, patch_hbm, field_hbm, out_field, out, anchors, counts, patch, field, load_sems,
    W, Q, B, S1, S2, FB, FS, FY, PS, C, CQ, FX, adv, FP, PZ,
    dense_old, dense_new, dense_back, got_old, got_new, got_back, edges, D, sides, near_sems, far_sems, T, T16,
):
    place = Place()
    me = place.i

    def chunk(yg):
        at = pl.ds(pl.multiple_of(yg * 128, 128), 128)
        return pltpu.make_async_copy(
            patch_hbm.at[:, :, :, at], patch.at[:, :, :, at], load_sems.at[yg]
        )

    small = [
        pltpu.make_async_copy(field_hbm, field, load_sems.at[8]),
        pltpu.make_async_copy(anchors_hbm, anchors, load_sems.at[9]),
        pltpu.make_async_copy(counts_hbm, counts, load_sems.at[10]),
    ]
    chunk(0).start()
    for copy in small:
        copy.start()
    for yg in range(1, 8):
        chunk(yg).start()
    old, new, rims = ([sides.at[n, k] for k in range(4)] for n in range(3))
    place.greet()
    fine_load(patch, W, Q, B, T, lambda yg: chunk(yg).wait())
    wait(small)
    planes = edge_planes(field, edges.at[0])
    count = counts[me]
    sources = [anchors[0, s, me] // 16 for s in range(4)]
    blocks = owned_blocks(anchors, counts, me, place.ni)
    fine_edges(W, FY, B)
    place.greeted()
    near = place.neighbours(planes, old, near_sems.at[0])
    fine_interior(W, Q, FY, 0, 10)
    wait(near)
    pack_shells(blocks, field, old, PZ, dense_old)
    far_old = place.exchange(dense_old, got_old, far_sems.at[0])
    coarse_step(field, *old, adv, FP, C, CQ, FX)
    planes = edge_planes(adv, edges.at[1])
    near = place.neighbours(planes, new, near_sems.at[1])
    fine_interior(W, Q, FY, 10, 14)
    wait(near)
    pack_shells(blocks, adv, new, PZ, dense_new)
    far_new = place.exchange(dense_new, got_new, far_sems.at[1])
    fine_interior(W, Q, FY, 14, 32)
    wait(far_old)
    fine_shells(got_old, sources, S1, T16)
    fine_boundary(B, S1, FB, FS, True)
    add_boundary(W, FB)
    fine_again(W, FB, Q, B)
    fine_edges(W, FY, B)
    wait(far_new)
    fine_shells(got_old, sources, S2, T16, got_new)
    fine_boundary(B, S2, FB, FS, False)
    fine_pack(FS, PS, T16)
    for i in range(place.ni):
        slot = jnp.int32(0)
        for s in range(1, 4):
            slot = jnp.where(jnp.logical_and(s < count, sources[s] == i), s, slot)
        dense_back[i] = PS[slot]
    back = place.exchange(dense_back, got_back, far_sems.at[2])
    fine_interior(W, Q, FY, 0, 28)
    wait(back)
    reflux(blocks, adv, FP, got_back, out_field, D)
    near = place.neighbours([D.at[1], D.at[0], D.at[3], D.at[2]], rims, near_sems.at[2])
    fine_interior(W, Q, FY, 28, 32)
    add_boundary(W, FB)
    fine_store(W, FB, patch, count, out, T)
    wait(near)
    for c in range(5):
        out_field[c, 0] = out_field[c, 0] + sides[2, 0, c]
        out_field[c, 15] = out_field[c, 15] + sides[2, 1, c]
        out_field[c, :, 0, :] = out_field[c, :, 0, :] + sides[2, 2, c]
        out_field[c, :, 15, :] = out_field[c, :, 15, :] + sides[2, 3, c]


def write_kernel(field, patch, out_field, out, sems):
    copies = [pltpu.make_async_copy(patch.at[s], out.at[s], sems.at[s]) for s in range(4)]
    copies.append(pltpu.make_async_copy(field, out_field, sems.at[4]))
    for copy in copies:
        copy.start()
    wait(copies)


def reflux(blocks, adv, FP, got, out, D):
    shape = (16, 128)
    lane = lanes(shape)
    owner = [jnp.int32(0)] * 8
    present = [jnp.int32(0)] * 8
    for o, block in enumerate(blocks):
        for zb in range(8):
            owner[zb] = jnp.where(block == zb, o, owner[zb])
            present[zb] = jnp.where(block == zb, 1, present[zb])
    live = jnp.zeros(shape, jnp.int32)
    for zb in range(8):
        live = jnp.where(lane // 16 == zb, present[zb], live)
    live = live > 0
    delta = {}
    for g in range(4):
        vs = [got[owner[zb], pl.ds(16 * g, 16), :] for zb in range(8)]
        if g < 2:
            turned = jnp.concatenate(vs, axis=0).T
        if g > 0:
            vs = block_transpose(vs, 16)
        for k in range(8):
            q = 8 * g + k
            if q < 30:
                e, c = q // 5, q % 5
                mean = 0.125 * (turned[16 * k : 16 * k + 16] if q < 10 else vs[k])
                value = FP[e, c] - mean if e % 2 == 0 else mean - FP[e, c]
                value = jnp.where(live, value, 0.0)
                if e < 2:
                    delta[e, c] = value
                else:
                    D[e - 2, c] = value
    column = lane % 16
    lower = [roll(delta[0, c], -1, 1) for c in range(5)]
    upper = [roll(delta[1, c], 16, 1) for c in range(5)]

    def put(x, _):
        for c in range(5):
            both = jnp.where((column + 1) % 16 == x, lower[c], 0.0)
            out[c, x] = adv[c, x] + pltpu.roll(jnp.where(column == x, upper[c], both), 128 - x, 1)
        return 0

    lax.fori_loop(0, 16, put, 0)


def call(kernel, outs, n_in, spaces, scratch=(), collective=None):
    more = {}
    if collective is not None:
        more = {"collective_id": collective, "has_side_effects": True}
    return pl.pallas_call(
        kernel,
        out_shape=[jax.ShapeDtypeStruct(shape, F32) for shape in outs],
        in_specs=[pl.BlockSpec(memory_space=spaces[0])] * n_in,
        out_specs=[pl.BlockSpec(memory_space=spaces[1])] * len(outs),
        scratch_shapes=[pltpu.VMEM(s, F32) if isinstance(s, tuple) else s for s in scratch],
        compiler_params=pltpu.CompilerParams(vmem_limit_bytes=VMEM_LIMIT, **more),
        cost_estimate=pl.CostEstimate(flops=10000000, bytes_accessed=4000000, transcendentals=0),
    )


def shards(coarse_state, patch_state, patch_anchor, patch_count):
    owners = lax.axis_size("gx")
    anchors = jnp.transpose(patch_anchor[:, 0], (2, 1, 0))
    counts = patch_count.reshape(-1)
    patch = patch_state.reshape(4, 5, 32, 1024)
    cube = (5, 32, 32, 128)
    prim = (PRIMS, 32, 32, 128)
    planes = (6, 5, 32, 128)
    field = (5, 16, 16, 128)
    side = (5, 16, 128)
    dense = (owners, 64, 128)
    dma = pltpu.SemaphoreType.DMA

    results = [field, (4, 5, 32, 1024)]
    made = call(
        step_kernel,
        results,
        4,
        (pltpu.HBM, pltpu.VMEM),
        [pltpu.SMEM((3, 4, owners), jnp.int32), pltpu.SMEM((owners,), jnp.int32)]
        + [(4, 5, 32, 1024), field, dma((11,)), cube, prim] + [planes] * 5 + [(5, 32, 128), (4, 64, 128)]
        + [(5, 17, 24, 128), (PRIMS, 17, 24, 128), side, field, (6,) + side, (8, 64, 128)]
        + [dense] * 6
        + [(2, 2) + side, (4,) + side, (3, 4) + side, dma((3, 2, 4)), dma((3, 2, owners)), (5, 4, 32, 128), (30, 16, 128)],
        0,
    )(*(pltpu.with_memory_space_constraint(a, pltpu.HBM) for a in (anchors, counts, patch, coarse_state)))
    made = (pltpu.with_memory_space_constraint(a, pltpu.VMEM) for a in made)
    coarse_next, out = call(write_kernel, results, 2, (pltpu.VMEM, pltpu.HBM), [dma((5,))])(*made)
    return (coarse_next, out.reshape(patch_state.shape))


def solution(mesh):
    in_specs = (
        P(None, "gx", "gy", None),
        P("gx", "gy", None, None, None, None),
        P(None, "gy", None, None),
        P(None, "gy"),
    )
    out_specs = (P(None, "gx", "gy", None), P("gx", "gy", None, None, None, None))
    return jax.shard_map(shards, mesh=mesh, in_specs=in_specs, out_specs=out_specs, check_vma=False)
```

```python
import jax
import jax.numpy as jnp
from jax import lax
from jax.experimental import pallas as pl
from jax.experimental.pallas import tpu as pltpu
from jax.sharding import PartitionSpec as P

COURANT = 0.12
VMEM_LIMIT = 50 * 1024 * 1024
F32 = jnp.float32
BF16 = jnp.bfloat16
MESH = pl.DeviceIdType.MESH


def rcp(x):
    return pl.reciprocal(x, approx=True)


def root(x):
    return x * lax.rsqrt(x)


def primitives(U):
    r = rcp(U[0])
    u, v, w = U[1] * r, U[2] * r, U[3] * r
    p = 0.4 * (U[4] - 0.5 * (U[1] * u + U[2] * v + U[3] * w))
    cc = 1.4 * (p * r)
    c5 = 5.0 * root(cc)
    cg5 = c5 * jnp.exp2(jnp.log2(p) * (-1.0 / 7.0))
    return [u, v, w, p, c5, cg5, 1.2 * U[0], p * (1.0 / 6.0), cc, 1.2 * r]


PRIMS = 10


def newton(s, z, L, R, du):
    value, slope = du, None
    scaled = (2.0 / 7.0) * rcp(s)
    for p, c5, cg5, r12, p6 in (L, R):
        d = s - p
        rt = lax.rsqrt((s + p6) * r12)
        shock = d * rt
        shock_slope = rt * (2.0 - (shock * rt) * r12)
        power = cg5 * z
        rare = power - c5
        rare_slope = power * scaled
        up = d > 0.0
        value = value + jnp.where(up, shock, rare)
        term = jnp.where(up, shock_slope, rare_slope)
        slope = term if slope is None else slope + term
    return s - (value + value) * rcp(slope)


def first_star(L, R, du):
    z = (L[1] + R[1] - du) * rcp(L[2] + R[2])
    z2 = z * z
    z3 = z2 * z
    return newton(z3 * z3 * z, z, L, R, du)


def face_flux(UL, QL, UR, QR, n, scale=COURANT):
    uL, pL, uR, pR = QL[n], QL[3], QR[n], QR[3]
    du = uR - uL
    s = first_star([q.astype(BF16) for q in QL[3:8]], [q.astype(BF16) for q in QR[3:8]], du.astype(BF16))
    s = s.astype(F32)
    z = jnp.exp2(jnp.log2(s) * (1.0 / 7.0))
    s = newton(s, z, QL[3:8], QR[3:8], du)
    low, high = (root(jnp.maximum(q[8], (s + q[7]) * q[9])) for q in (QL, QR))
    low = jnp.minimum(uL - low, 0.0)
    high = jnp.maximum(uR + high, 0.0)
    inv = rcp(high - low) * scale
    wL, wR = high * inv, low * inv
    a, b = wL * (uL - low), wR * (high - uR)
    eL, eR = wL * pL, wR * pR
    F = [a * UL[i] + b * UR[i] for i in range(5)]
    F[1 + n] = F[1 + n] + (eL - eR)
    F[4] = F[4] + (eL * uL - eR * uR)
    return F


def roll(x, by, axis):
    by = by % x.shape[axis]
    return x if by == 0 else pltpu.roll(x, by, axis)


def lanes(shape):
    return lax.broadcasted_iota(jnp.int32, shape, len(shape) - 1)


def block_transpose(vs, width):
    n = len(vs)
    block = lanes(vs[0].shape) // width
    vs = list(vs)
    d = n // 2
    while d:
        low = (block & d) == 0
        for i in range(n):
            if i & d == 0:
                a, b = vs[i], vs[i + d]
                vs[i] = jnp.where(low, a, roll(b, d * width, 1))
                vs[i + d] = jnp.where(low, roll(a, -d * width, 1), b)
        d //= 2
    return vs


def pick(x, index):
    return jnp.take_along_axis(x, index, axis=1)


NORMAL = (2, 2, 0, 0, 1, 1)


def next_x(a):
    return jnp.concatenate([a[8:32], roll(a[0:8], -1, 0)], axis=0)


def last_x(a):
    return jnp.concatenate([roll(a[24:32], 1, 0), a[0:24]], axis=0)


def collect(U, y, lane, planes):
    lower, upper = lane == y, (lane + 1) % 32 == y
    for c in range(5):
        turned = pltpu.roll(U[c], y, 1)
        planes[0][c] = jnp.where(lower, turned, planes[0][c])
        planes[1][c] = jnp.where(upper, turned, planes[1][c])


def z_planes(B):
    return [[B[side, c] for c in range(5)] for side in range(2)]


def put_planes(B, planes):
    for side in range(2):
        for c in range(5):
            B[side, c] = planes[side][c]


def fine_load(patch, W, Q, B, T, arrived):
    lane = lanes((32, 128)) % 32
    for c in range(5):
        B[0, c] = jnp.zeros((32, 128), F32)
        B[1, c] = jnp.zeros((32, 128), F32)

    def body(yg, _):
        at = pl.ds(pl.multiple_of(yg * 128, 128), 128)
        arrived(yg)
        U = [[None] * 5 for _ in range(4)]
        for c in range(5):
            vs = block_transpose([patch[s, c, :, at] for s in range(4)], 32)
            for j in range(4):
                T[c, j] = vs[j]
        for c in range(5):
            for j in range(4):
                U[j][c] = jnp.concatenate([T[c, j, pl.ds(v, 8, 4), :] for v in range(4)], axis=0)
                W[c, 4 * yg + j] = U[j][c]
        planes = z_planes(B)
        for j in range(4):
            collect(U[j], 4 * yg + j, lane, planes)
        put_planes(B, planes)
        for j in range(4):
            for k, q in enumerate(primitives(U[j])):
                Q[k, 4 * yg + j] = q
        return 0

    lax.fori_loop(0, 8, body, 0)


def fine_edges(W, FY, B):
    for c in range(5):
        FY[c] = jnp.zeros((32, 128), F32)
        B[1, c] = roll(B[1, c], -31, 1)
        B[2, c] = W[c, :, 0, :]
        B[3, c] = W[c, :, 31, :]
        B[4, c] = W[c, 0]
        B[5, c] = W[c, 31]


def fine_interior(W, Q, FY, first, last):
    shape = (32, 128)
    row = lax.broadcasted_iota(jnp.int32, shape, 0)
    scale_x = jnp.where(row < 31, COURANT, 0.0)
    scale_z = jnp.where(lanes(shape) % 32 < 31, COURANT, 0.0)

    def body(pair, _):
        ys = (2 * pair, 2 * pair + 1, jnp.minimum(2 * pair + 2, 31))
        U = [[W[c, y] for c in range(5)] for y in ys]
        S = [[Q[k, y] for k in range(PRIMS)] for y in ys]
        before = [FY[c] for c in range(5)]
        results = []
        for n in range(2):
            scale = COURANT if n == 0 else jnp.where(jnp.broadcast_to(pair, shape) < 15, COURANT, 0.0)
            F = face_flux(U[n], S[n], U[n + 1], S[n + 1], 1, scale)
            total = [F[c] - before[c] for c in range(5)]
            before = F
            F = face_flux(
                U[n], S[n], [roll(a, -1, 1) for a in U[n]], [roll(a, -1, 1) for a in S[n]], 2, scale_z
            )
            total = [total[c] + (F[c] - roll(F[c], 1, 1)) for c in range(5)]
            F = face_flux(
                U[n], S[n], [next_x(a) for a in U[n]], [next_x(a) for a in S[n]], 0, scale_x
            )
            results.append([U[n][c] - (total[c] + (F[c] - last_x(F[c]))) for c in range(5)])
        for c in range(5):
            W[c, ys[0]] = results[0][c]
            W[c, ys[1]] = results[1][c]
            FY[c] = before[c]
        return 0

    lax.fori_loop(first // 2, last // 2, body, 0)


def fine_shells(got, sources, S, T16, mix=None):
    zeros = jnp.zeros((16, 128), F32)
    twice = lanes((16, 128)) // 2
    for g in range(4):
        blocks = []
        for s in range(4):
            at = pl.ds(16 * g, 16)
            block = got[sources[s], at, :]
            if mix is not None:
                block = 0.5 * (block + mix[sources[s], at, :])
            blocks.append(block)
        pieces = block_transpose(blocks + [zeros] * 4, 16)
        for k in range(8):
            q = 8 * g + k
            if q < 30:
                e, c = q // 5, q % 5
                out = pick(pieces[k], twice)
                if e in (2, 3):
                    S[e, c, pl.ds(0, 16, 2), :] = out
                    S[e, c, pl.ds(1, 16, 2), :] = out
                else:
                    T16[q] = out
                    even, odd = T16[q, pl.ds(0, 8, 2), :], T16[q, pl.ds(1, 8, 2), :]
                    S[e, c] = jnp.concatenate([even, even, odd, odd], axis=0)


def fine_boundary(B, Q, S, FB, FS, first):
    for n in range(3):
        for face in (2 * n, 2 * n + 1):
            inner = [B[face, c] for c in range(5)]
            outer = [S[face, c] for c in range(5)]
            qo = primitives(outer)
            if n == 0:
                qi = primitives(inner)
            elif n == 1:
                qi = [Q[k, :, 31 * (face % 2), :] for k in range(PRIMS)]
            else:
                qi = [Q[k, 31 * (face % 2)] for k in range(PRIMS)]
            if face % 2 == 0:
                F = face_flux(outer, qo, inner, qi, NORMAL[face])
            else:
                F = face_flux(inner, qi, outer, qo, NORMAL[face])
            for c in range(5):
                FB[face, c] = F[c]
                FS[face, c] = F[c] if first else FS[face, c] + F[c]


def add_boundary(W, FB):
    for c in range(5):
        FB[1, c] = roll(FB[1, c], 31, 1)
        W[c, :, 0, :] = W[c, :, 0, :] + FB[2, c]
        W[c, :, 31, :] = W[c, :, 31, :] - FB[3, c]
        W[c, 0] = W[c, 0] + FB[4, c]
        W[c, 31] = W[c, 31] - FB[5, c]


def z_boundary(value, FB, c, y, lane):
    upper = jnp.where((lane + 1) % 32 == y, -FB[1, c], 0.0)
    return value + pltpu.roll(jnp.where(lane == y, FB[0, c], upper), 128 - y, 1)


def fine_again(W, FB, Q, B):
    lane = lanes((32, 128)) % 32

    def body(yg, _):
        planes = z_planes(B)
        for j in range(4):
            y = 4 * yg + j
            U = [z_boundary(W[c, y], FB, c, y, lane) for c in range(5)]
            for c in range(5):
                W[c, y] = U[c]
            collect(U, y, lane, planes)
            for k, q in enumerate(primitives(U)):
                Q[k, y] = q
        put_planes(B, planes)
        return 0

    lax.fori_loop(0, 8, body, 0)


def fine_store(W, FB, patch, count, out, T):
    lane = lanes((32, 128)) % 32

    def body(yg, _):
        at = pl.ds(pl.multiple_of(yg * 128, 128), 128)
        for c in range(5):
            for j in range(4):
                y = 4 * yg + j
                value = z_boundary(W[c, y], FB, c, y, lane)
                for v in range(4):
                    T[c, j, pl.ds(v, 8, 4), :] = value[8 * v : 8 * v + 8]
        for c in range(5):
            vs = block_transpose([T[c, j] for j in range(4)], 32)
            for s in range(4):
                out[s, c, :, at] = jnp.where(s < count, vs[s], patch[s, c, :, at])
        return 0

    lax.fori_loop(0, 8, body, 0)


def fine_pack(FS, PS, T16):
    half = (lanes((16, 128)) * 2) % 128
    for g in range(4):
        pieces = []
        for k in range(8):
            q = 8 * g + k
            if q >= 30:
                pieces.append(jnp.zeros((16, 128), F32))
                continue
            e, c = q // 5, q % 5
            if e in (2, 3):
                m = FS[e, c, pl.ds(0, 16, 2), :] + FS[e, c, pl.ds(1, 16, 2), :]
            else:
                T16[q, pl.ds(0, 8, 2), :] = FS[e, c, 0:8] + FS[e, c, 8:16]
                T16[q, pl.ds(1, 8, 2), :] = FS[e, c, 16:24] + FS[e, c, 24:32]
                m = T16[q]
            pieces.append(pick(m + roll(m, -1, 1), half))
        outs = block_transpose(pieces, 16)
        for s in range(4):
            PS[s, pl.ds(16 * g, 16), :] = outs[s]


def build_shells(field, sides, planes, PZ):
    shape = (16, 128)
    lane = lanes(shape)
    zeros = jnp.zeros(shape, F32)
    T = [zeros] * 10
    for x in range(16):
        here = lane % 16 == x
        for c in range(5):
            U = field[c, x, 0:16, :]
            turned = roll(U, x, 1)
            T[c] = jnp.where((lane + 1) % 16 == x, turned, T[c])
            T[5 + c] = jnp.where(here, turned, T[5 + c])
    T = [roll(a, 1, 1) for a in T[:5]] + [roll(a, -16, 1) for a in T[5:]]
    z0 = jnp.concatenate(T[:8], axis=0).T
    z1 = jnp.concatenate(T[8:] + [zeros] * 6, axis=0).T
    for zb in range(8):
        PZ[zb, 0:16] = z0[16 * zb : 16 * zb + 16]
    for g in range(1, 4):
        vs = []
        for k in range(8):
            q = 8 * g + k
            vs.append(zeros if q < 10 or q >= 30 else sides[q // 5 - 2][q % 5])
        vs = block_transpose(vs, 16)
        for zb in range(8):
            value = vs[zb]
            if g == 1:
                value = jnp.where(lane < 32, z1[16 * zb : 16 * zb + 16], value)
            PZ[zb, 16 * g : 16 * g + 16] = value


def coarse_step(field, xlo, xhi, ylo, yhi, adv, FP, C, Q, FX):
    for c in range(5):
        for x in range(16):
            C[c, x, 0:16] = field[c, x]
            C[c, x, 16:24] = jnp.broadcast_to(yhi[c, x : x + 1], (8, 128))
        C[c, 16, 0:16] = xhi[c]
        C[c, 16, 16:24] = xhi[c, 8:16]

    def cells(x4, _):
        for x in range(4):
            for k, q in enumerate(primitives([C[c, 4 * x4 + x] for c in range(5)])):
                Q[k, 4 * x4 + x] = q
        return 0

    lax.fori_loop(0, 4, cells, 0)
    for k, q in enumerate(primitives([C[c, 16] for c in range(5)])):
        Q[k, 16] = q
    R = [field[c, 0] for c in range(5)]
    L = [xlo[c] for c in range(5)]
    F = face_flux(L, primitives(L), R, primitives(R), 0)
    for c in range(5):
        FP[2, c] = F[c]
        FX[c] = F[c]
    R = [field[c, :, 0, :] for c in range(5)]
    L = [ylo[c] for c in range(5)]
    F = face_flux(L, primitives(L), R, primitives(R), 1)
    for c in range(5):
        FP[4, c] = F[c]
        FP[0, c] = jnp.zeros((16, 128), F32)
    lane = lanes((16, 128)) % 16
    row = lax.broadcasted_iota(jnp.int32, (16, 128), 0)

    def body(pair, _):
        xs = (2 * pair, 2 * pair + 1, 2 * pair + 2)
        U24 = [[C[c, x] for c in range(5)] for x in xs]
        S24 = [[Q[k, x] for k in range(PRIMS)] for x in xs]
        U = [[a[0:16] for a in As] for As in U24]
        S = [[a[0:16] for a in As] for As in S24]
        below = [FX[c] for c in range(5)]
        corner = [[FP[4, c, pl.ds(x, 1), :] for c in range(5)] for x in xs[:2]]
        zs = [FP[0, c] for c in range(5)]
        results, tops = [], []
        for n in range(2):
            F = face_flux(U[n], S[n], U[n + 1], S[n + 1], 0)
            total = [F[c] - below[c] for c in range(5)]
            below = F
            F = face_flux(
                U[n], S[n], [roll(a, -1, 1) for a in U[n]], [roll(a, -1, 1) for a in S[n]], 2
            )
            for c in range(5):
                zs[c] = jnp.where(lane == xs[n], pltpu.roll(F[c], xs[n] + 1, 1), zs[c])
                total[c] = total[c] + (F[c] - roll(F[c], 1, 1))
            up = [[roll(a, -1, 0)[0:16] for a in As] for As in (U24[n], S24[n])]
            F = face_flux(U[n], S[n], up[0], up[1], 1)
            tops.append([a[15:16] for a in F])
            for c in range(5):
                before = jnp.where(row == 0, corner[n][c], roll(F[c], 1, 0))
                total[c] = total[c] + (F[c] - before)
            results.append([U[n][c] - total[c] for c in range(5)])
        for c in range(5):
            for n in range(2):
                adv[c, xs[n]] = results[n][c]
                FP[5, c, pl.ds(xs[n], 1), :] = tops[n][c]
            FP[0, c] = zs[c]
            FX[c] = below[c]
        return 0

    lax.fori_loop(0, 8, body, 0)
    for c in range(5):
        FP[3, c] = FX[c]
        FP[1, c] = roll(FP[0, c], -16, 1)


def owned_blocks(anchors, counts, me, owners):
    blocks = []
    for o in range(owners):
        block = jnp.int32(-1)
        for s in range(4):
            mine = jnp.logical_and(s < counts[o], anchors[0, s, o] == 16 * me)
            block = jnp.where(mine, anchors[2, s, o] // 16, block)
        blocks.append(block)
    return blocks


def pack_shells(blocks, field, sides, PZ, dense):
    build_shells(field, sides, None, PZ)
    for o, block in enumerate(blocks):
        dense[o] = PZ[jnp.maximum(block, 0)]


class Place:
    def __init__(self):
        self.i, self.j = lax.axis_index("gx"), lax.axis_index("gy")
        self.ni, self.nj = lax.axis_size("gx"), lax.axis_size("gy")

    def along_x(self, d):
        return (lax.rem(self.i + (d + self.ni), self.ni), self.j)

    def along_y(self, d):
        return (self.i, lax.rem(self.j + (d + self.nj), self.nj))

    def greet(self):
        barrier = pltpu.get_barrier_semaphore()
        for d in range(1, self.ni):
            pl.semaphore_signal(barrier, inc=1, device_id=self.along_x(d), device_id_type=MESH)
        for d in (1, -1):
            pl.semaphore_signal(barrier, inc=1, device_id=self.along_y(d), device_id_type=MESH)

    def greeted(self):
        pl.semaphore_wait(pltpu.get_barrier_semaphore(), self.ni + 1)

    def send(self, src, dst, send_sem, recv_sem, to):
        copy = pltpu.make_async_remote_copy(
            src_ref=src,
            dst_ref=dst,
            send_sem=send_sem,
            recv_sem=recv_sem,
            device_id=to,
            device_id_type=MESH,
        )
        copy.start()
        return copy

    def neighbours(self, planes, sides, sems):
        to = (self.along_x(1), self.along_x(-1), self.along_y(1), self.along_y(-1))
        return [
            self.send(planes[k], sides[k], sems.at[0, k], sems.at[1, k], to[k]) for k in range(4)
        ]

    def exchange(self, dense, got, sems):
        got[self.i] = dense[self.i]
        copies = []
        for d in range(1, self.ni):
            to = self.along_x(d)
            copies.append(
                self.send(dense.at[to[0]], got.at[self.i], sems.at[0, d], sems.at[1, d], to)
            )
        return copies


def wait(copies):
    for copy in copies:
        copy.wait()


def edge_planes(field, edges):
    for c in range(5):
        edges[0, c] = field[c, :, 15, :]
        edges[1, c] = field[c, :, 0, :]
    return (field.at[:, 15], field.at[:, 0], edges.at[0], edges.at[1])


def step_kernel(
    anchors_hbm, counts_hbm, patch_hbm, field_hbm, out_field, out, anchors, counts, patch, field, load_sems,
    W, Q, B, S1, S2, FB, FS, FY, PS, C, CQ, FX, adv, FP, PZ,
    dense_old, dense_new, dense_back, got_old, got_new, got_back, edges, D, sides, near_sems, far_sems, T, T16,
):
    place = Place()
    me = place.i

    def chunk(yg):
        at = pl.ds(pl.multiple_of(yg * 128, 128), 128)
        return pltpu.make_async_copy(
            patch_hbm.at[:, :, :, at], patch.at[:, :, :, at], load_sems.at[yg]
        )

    small = [
        pltpu.make_async_copy(field_hbm, field, load_sems.at[8]),
        pltpu.make_async_copy(anchors_hbm, anchors, load_sems.at[9]),
        pltpu.make_async_copy(counts_hbm, counts, load_sems.at[10]),
    ]
    for copy in small:
        copy.start()
    for yg in range(8):
        chunk(yg).start()
    old, new, rims = ([sides.at[n, k] for k in range(4)] for n in range(3))
    place.greet()
    wait(small)
    planes = edge_planes(field, edges.at[0])
    place.greeted()
    near = place.neighbours(planes, old, near_sems.at[0])
    fine_load(patch, W, Q, B, T, lambda yg: chunk(yg).wait())
    count = counts[me]
    sources = [anchors[0, s, me] // 16 for s in range(4)]
    blocks = owned_blocks(anchors, counts, me, place.ni)
    fine_edges(W, FY, B)
    wait(near)
    pack_shells(blocks, field, old, PZ, dense_old)
    far_old = place.exchange(dense_old, got_old, far_sems.at[0])
    coarse_step(field, *old, adv, FP, C, CQ, FX)
    planes = edge_planes(adv, edges.at[1])
    near = place.neighbours(planes, new, near_sems.at[1])
    fine_interior(W, Q, FY, 0, 4)
    wait(near)
    pack_shells(blocks, adv, new, PZ, dense_new)
    far_new = place.exchange(dense_new, got_new, far_sems.at[1])
    fine_interior(W, Q, FY, 4, 32)
    wait(far_old)
    fine_shells(got_old, sources, S1, T16)
    fine_boundary(B, Q, S1, FB, FS, True)
    add_boundary(W, FB)
    fine_again(W, FB, Q, B)
    fine_edges(W, FY, B)
    wait(far_new)
    fine_shells(got_old, sources, S2, T16, got_new)
    fine_boundary(B, Q, S2, FB, FS, False)
    fine_pack(FS, PS, T16)
    for i in range(place.ni):
        slot = jnp.int32(0)
        for s in range(1, 4):
            slot = jnp.where(jnp.logical_and(s < count, sources[s] == i), s, slot)
        dense_back[i] = PS[slot]
    back = place.exchange(dense_back, got_back, far_sems.at[2])
    fine_interior(W, Q, FY, 0, 28)
    wait(back)
    reflux(blocks, adv, FP, got_back, out_field, D)
    near = place.neighbours([D.at[1], D.at[0], D.at[3], D.at[2]], rims, near_sems.at[2])
    fine_interior(W, Q, FY, 28, 32)
    add_boundary(W, FB)
    fine_store(W, FB, patch, count, out, T)
    wait(near)
    for c in range(5):
        out_field[c, 0] = out_field[c, 0] + sides[2, 0, c]
        out_field[c, 15] = out_field[c, 15] + sides[2, 1, c]
        out_field[c, :, 0, :] = out_field[c, :, 0, :] + sides[2, 2, c]
        out_field[c, :, 15, :] = out_field[c, :, 15, :] + sides[2, 3, c]


def write_kernel(field, patch, out_field, out, sems):
    copies = [
        pltpu.make_async_copy(patch, out, sems.at[0]),
        pltpu.make_async_copy(field, out_field, sems.at[1]),
    ]
    for copy in copies:
        copy.start()
    wait(copies)


def reflux(blocks, adv, FP, got, out, D):
    shape = (16, 128)
    lane = lanes(shape)
    owner = [jnp.int32(0)] * 8
    present = [jnp.int32(0)] * 8
    for o, block in enumerate(blocks):
        for zb in range(8):
            owner[zb] = jnp.where(block == zb, o, owner[zb])
            present[zb] = jnp.where(block == zb, 1, present[zb])
    live = jnp.zeros(shape, jnp.int32)
    for zb in range(8):
        live = jnp.where(lane // 16 == zb, present[zb], live)
    live = live > 0
    delta = {}
    for g in range(4):
        vs = [got[owner[zb], pl.ds(16 * g, 16), :] for zb in range(8)]
        if g < 2:
            turned = jnp.concatenate(vs, axis=0).T
        if g > 0:
            vs = block_transpose(vs, 16)
        for k in range(8):
            q = 8 * g + k
            if q < 30:
                e, c = q // 5, q % 5
                mean = 0.125 * (turned[16 * k : 16 * k + 16] if q < 10 else vs[k])
                value = FP[e, c] - mean if e % 2 == 0 else mean - FP[e, c]
                value = jnp.where(live, value, 0.0)
                if e < 2:
                    delta[e, c] = value
                else:
                    D[e - 2, c] = value
    column = lane % 16
    for c in range(5):
        lower, upper = roll(delta[0, c], -1, 1), roll(delta[1, c], 16, 1)
        for x in range(16):
            both = jnp.where((column + 1) % 16 == x, lower, 0.0)
            out[c, x] = adv[c, x] + roll(jnp.where(column == x, upper, both), -x, 1)


def call(kernel, outs, n_in, spaces, scratch=(), collective=None):
    more = {}
    if collective is not None:
        more = {"collective_id": collective, "has_side_effects": True}
    return pl.pallas_call(
        kernel,
        out_shape=[jax.ShapeDtypeStruct(shape, F32) for shape in outs],
        in_specs=[pl.BlockSpec(memory_space=spaces[0])] * n_in,
        out_specs=[pl.BlockSpec(memory_space=spaces[1])] * len(outs),
        scratch_shapes=[pltpu.VMEM(s, F32) if isinstance(s, tuple) else s for s in scratch],
        compiler_params=pltpu.CompilerParams(vmem_limit_bytes=VMEM_LIMIT, **more),
        cost_estimate=pl.CostEstimate(flops=10000000, bytes_accessed=4000000, transcendentals=0),
    )


def shards(coarse_state, patch_state, patch_anchor, patch_count):
    owners = lax.axis_size("gx")
    anchors = jnp.transpose(patch_anchor[:, 0], (2, 1, 0))
    counts = patch_count.reshape(-1)
    patch = patch_state.reshape(4, 5, 32, 1024)
    cube = (5, 32, 32, 128)
    prim = (PRIMS, 32, 32, 128)
    planes = (6, 5, 32, 128)
    field = (5, 16, 16, 128)
    side = (5, 16, 128)
    dense = (owners, 64, 128)
    dma = pltpu.SemaphoreType.DMA

    results = [field, (4, 5, 32, 1024)]
    made = call(
        step_kernel,
        results,
        4,
        (pltpu.HBM, pltpu.VMEM),
        [pltpu.SMEM((3, 4, owners), jnp.int32), pltpu.SMEM((owners,), jnp.int32)]
        + [(4, 5, 32, 1024), field, dma((11,)), cube, prim] + [planes] * 5 + [(5, 32, 128), (4, 64, 128)]
        + [(5, 17, 24, 128), (PRIMS, 17, 24, 128), side, field, (6,) + side, (8, 64, 128)]
        + [dense] * 6
        + [(2, 2) + side, (4,) + side, (3, 4) + side, dma((3, 2, 4)), dma((3, 2, owners)), (5, 4, 32, 128), (30, 16, 128)],
        0,
    )(*(pltpu.with_memory_space_constraint(a, pltpu.HBM) for a in (anchors, counts, patch, coarse_state)))
    made = (pltpu.with_memory_space_constraint(a, pltpu.VMEM) for a in made)
    coarse_next, out = call(write_kernel, results, 2, (pltpu.VMEM, pltpu.HBM), [dma((2,))])(*made)
    return (coarse_next, out.reshape(patch_state.shape))


def solution(mesh):
    in_specs = (
        P(None, "gx", "gy", None),
        P("gx", "gy", None, None, None, None),
        P(None, "gy", None, None),
        P(None, "gy"),
    )
    out_specs = (P(None, "gx", "gy", None), P("gx", "gy", None, None, None, None))
    return jax.shard_map(shards, mesh=mesh, in_specs=in_specs, out_specs=out_specs, check_vma=False)
```

```python
import jax
import jax.numpy as jnp
from jax import lax
from jax.experimental import pallas as pl
from jax.experimental.pallas import tpu as pltpu
from jax.sharding import PartitionSpec as P

COURANT = 0.12
VMEM_LIMIT = 50 * 1024 * 1024
F32 = jnp.float32
BF16 = jnp.bfloat16
MESH = pl.DeviceIdType.MESH


def rcp(x):
    return pl.reciprocal(x, approx=True)


def root(x):
    return x * lax.rsqrt(x)


def primitives(U):
    r = rcp(U[0])
    u, v, w = U[1] * r, U[2] * r, U[3] * r
    p = 0.4 * (U[4] - 0.5 * (U[1] * u + U[2] * v + U[3] * w))
    cc = 1.4 * (p * r)
    c5 = 5.0 * root(cc)
    cg5 = c5 * jnp.exp2(jnp.log2(p) * (-1.0 / 7.0))
    return [u, v, w, p, c5, cg5, 1.2 * U[0], p * (1.0 / 6.0), cc, 1.2 * r]


PRIMS = 10


def newton(s, z, L, R, du):
    value, slope = du, None
    scaled = (2.0 / 7.0) * rcp(s)
    for p, c5, cg5, r12, p6 in (L, R):
        d = s - p
        rt = lax.rsqrt((s + p6) * r12)
        shock = d * rt
        shock_slope = rt * (2.0 - (shock * rt) * r12)
        power = cg5 * z
        rare = power - c5
        rare_slope = power * scaled
        up = d > 0.0
        value = value + jnp.where(up, shock, rare)
        term = jnp.where(up, shock_slope, rare_slope)
        slope = term if slope is None else slope + term
    return s - (value + value) * rcp(slope)


def first_star(L, R, du):
    z = (L[1] + R[1] - du) * rcp(L[2] + R[2])
    z2 = z * z
    z3 = z2 * z
    return newton(z3 * z3 * z, z, L, R, du)


def face_flux(UL, QL, UR, QR, n, scale=COURANT):
    uL, pL, uR, pR = QL[n], QL[3], QR[n], QR[3]
    du = uR - uL
    s = first_star([q.astype(BF16) for q in QL[3:8]], [q.astype(BF16) for q in QR[3:8]], du.astype(BF16))
    s = s.astype(F32)
    z = jnp.exp2(jnp.log2(s) * (1.0 / 7.0))
    s = newton(s, z, QL[3:8], QR[3:8], du)
    low, high = (root(jnp.maximum(q[8], (s + q[7]) * q[9])) for q in (QL, QR))
    low = jnp.minimum(uL - low, 0.0)
    high = jnp.maximum(uR + high, 0.0)
    inv = rcp(high - low) * scale
    wL, wR = high * inv, low * inv
    a, b = wL * (uL - low), wR * (high - uR)
    eL, eR = wL * pL, wR * pR
    F = [a * UL[i] + b * UR[i] for i in range(5)]
    F[1 + n] = F[1 + n] + (eL - eR)
    F[4] = F[4] + (eL * uL - eR * uR)
    return F


def roll(x, by, axis):
    by = by % x.shape[axis]
    return x if by == 0 else pltpu.roll(x, by, axis)


def lanes(shape):
    return lax.broadcasted_iota(jnp.int32, shape, len(shape) - 1)


def block_transpose(vs, width):
    n = len(vs)
    block = lanes(vs[0].shape) // width
    vs = list(vs)
    d = n // 2
    while d:
        low = (block & d) == 0
        for i in range(n):
            if i & d == 0:
                a, b = vs[i], vs[i + d]
                vs[i] = jnp.where(low, a, roll(b, d * width, 1))
                vs[i + d] = jnp.where(low, roll(a, -d * width, 1), b)
        d //= 2
    return vs


def pick(x, index):
    return jnp.take_along_axis(x, index, axis=1)


NORMAL = (2, 2, 0, 0, 1, 1)


def next_x(a):
    return jnp.concatenate([a[8:32], roll(a[0:8], -1, 0)], axis=0)


def last_x(a):
    return jnp.concatenate([roll(a[24:32], 1, 0), a[0:24]], axis=0)


def collect(U, y, lane, planes):
    lower, upper = lane == y, (lane + 1) % 32 == y
    for c in range(5):
        turned = pltpu.roll(U[c], y, 1)
        planes[0][c] = jnp.where(lower, turned, planes[0][c])
        planes[1][c] = jnp.where(upper, turned, planes[1][c])


def z_planes(B):
    return [[B[side, c] for c in range(5)] for side in range(2)]


def put_planes(B, planes):
    for side in range(2):
        for c in range(5):
            B[side, c] = planes[side][c]


def fine_load(patch, W, Q, B, T, arrived):
    lane = lanes((32, 128)) % 32
    for c in range(5):
        B[0, c] = jnp.zeros((32, 128), F32)
        B[1, c] = jnp.zeros((32, 128), F32)

    def body(yg, _):
        at = pl.ds(pl.multiple_of(yg * 128, 128), 128)
        arrived(yg)
        U = [[None] * 5 for _ in range(4)]
        for c in range(5):
            vs = block_transpose([patch[s, c, :, at] for s in range(4)], 32)
            for j in range(4):
                T[c, j] = vs[j]
        for c in range(5):
            for j in range(4):
                U[j][c] = jnp.concatenate([T[c, j, pl.ds(v, 8, 4), :] for v in range(4)], axis=0)
                W[c, 4 * yg + j] = U[j][c]
        planes = z_planes(B)
        for j in range(4):
            collect(U[j], 4 * yg + j, lane, planes)
        put_planes(B, planes)
        for j in range(4):
            for k, q in enumerate(primitives(U[j])):
                Q[k, 4 * yg + j] = q
        return 0

    lax.fori_loop(0, 8, body, 0)


def fine_edges(W, FY, B):
    for c in range(5):
        FY[c] = jnp.zeros((32, 128), F32)
        B[1, c] = roll(B[1, c], -31, 1)
        B[2, c] = W[c, :, 0, :]
        B[3, c] = W[c, :, 31, :]
        B[4, c] = W[c, 0]
        B[5, c] = W[c, 31]


def fine_interior(W, Q, FY, first, last):
    shape = (32, 128)
    row = lax.broadcasted_iota(jnp.int32, shape, 0)
    scale_x = jnp.where(row < 31, COURANT, 0.0)
    scale_z = jnp.where(lanes(shape) % 32 < 31, COURANT, 0.0)

    def body(pair, _):
        ys = (2 * pair, 2 * pair + 1, jnp.minimum(2 * pair + 2, 31))
        U = [[W[c, y] for c in range(5)] for y in ys]
        S = [[Q[k, y] for k in range(PRIMS)] for y in ys]
        before = [FY[c] for c in range(5)]
        results = []
        for n in range(2):
            scale = COURANT if n == 0 else jnp.where(jnp.broadcast_to(pair, shape) < 15, COURANT, 0.0)
            F = face_flux(U[n], S[n], U[n + 1], S[n + 1], 1, scale)
            total = [F[c] - before[c] for c in range(5)]
            before = F
            F = face_flux(
                U[n], S[n], [roll(a, -1, 1) for a in U[n]], [roll(a, -1, 1) for a in S[n]], 2, scale_z
            )
            total = [total[c] + (F[c] - roll(F[c], 1, 1)) for c in range(5)]
            F = face_flux(
                U[n], S[n], [next_x(a) for a in U[n]], [next_x(a) for a in S[n]], 0, scale_x
            )
            results.append([U[n][c] - (total[c] + (F[c] - last_x(F[c]))) for c in range(5)])
        for c in range(5):
            W[c, ys[0]] = results[0][c]
            W[c, ys[1]] = results[1][c]
            FY[c] = before[c]
        return 0

    lax.fori_loop(first // 2, last // 2, body, 0)


def fine_shells(got, sources, S, T16, mix=None):
    zeros = jnp.zeros((16, 128), F32)
    twice = lanes((16, 128)) // 2
    for g in range(4):
        blocks = []
        for s in range(4):
            at = pl.ds(16 * g, 16)
            block = got[sources[s], at, :]
            if mix is not None:
                block = 0.5 * (block + mix[sources[s], at, :])
            blocks.append(block)
        pieces = block_transpose(blocks + [zeros] * 4, 16)
        for k in range(8):
            q = 8 * g + k
            if q < 30:
                e, c = q // 5, q % 5
                out = pick(pieces[k], twice)
                if e in (2, 3):
                    S[e, c, pl.ds(0, 16, 2), :] = out
                    S[e, c, pl.ds(1, 16, 2), :] = out
                else:
                    T16[q] = out
                    even, odd = T16[q, pl.ds(0, 8, 2), :], T16[q, pl.ds(1, 8, 2), :]
                    S[e, c] = jnp.concatenate([even, even, odd, odd], axis=0)


def fine_boundary(B, Q, S, FB, FS, first):
    for n in range(3):
        for face in (2 * n, 2 * n + 1):
            inner = [B[face, c] for c in range(5)]
            outer = [S[face, c] for c in range(5)]
            qo = primitives(outer)
            if n == 0:
                qi = primitives(inner)
            elif n == 1:
                qi = [Q[k, :, 31 * (face % 2), :] for k in range(PRIMS)]
            else:
                qi = [Q[k, 31 * (face % 2)] for k in range(PRIMS)]
            if face % 2 == 0:
                F = face_flux(outer, qo, inner, qi, NORMAL[face])
            else:
                F = face_flux(inner, qi, outer, qo, NORMAL[face])
            for c in range(5):
                FB[face, c] = F[c]
                FS[face, c] = F[c] if first else FS[face, c] + F[c]


def add_boundary(W, FB):
    for c in range(5):
        FB[1, c] = roll(FB[1, c], 31, 1)
        W[c, :, 0, :] = W[c, :, 0, :] + FB[2, c]
        W[c, :, 31, :] = W[c, :, 31, :] - FB[3, c]
        W[c, 0] = W[c, 0] + FB[4, c]
        W[c, 31] = W[c, 31] - FB[5, c]


def z_boundary(value, FB, c, y, lane):
    upper = jnp.where((lane + 1) % 32 == y, -FB[1, c], 0.0)
    return value + pltpu.roll(jnp.where(lane == y, FB[0, c], upper), 128 - y, 1)


def fine_again(W, FB, Q, B):
    lane = lanes((32, 128)) % 32

    def body(yg, _):
        planes = z_planes(B)
        for j in range(4):
            y = 4 * yg + j
            U = [z_boundary(W[c, y], FB, c, y, lane) for c in range(5)]
            for c in range(5):
                W[c, y] = U[c]
            collect(U, y, lane, planes)
            for k, q in enumerate(primitives(U)):
                Q[k, y] = q
        put_planes(B, planes)
        return 0

    lax.fori_loop(0, 8, body, 0)


def fine_store(W, FB, patch, count, out, T):
    lane = lanes((32, 128)) % 32

    def body(yg, _):
        at = pl.ds(pl.multiple_of(yg * 128, 128), 128)
        for c in range(5):
            for j in range(4):
                y = 4 * yg + j
                value = z_boundary(W[c, y], FB, c, y, lane)
                for v in range(4):
                    T[c, j, pl.ds(v, 8, 4), :] = value[8 * v : 8 * v + 8]
        for c in range(5):
            vs = block_transpose([T[c, j] for j in range(4)], 32)
            for s in range(4):
                out[s, c, :, at] = jnp.where(s < count, vs[s], patch[s, c, :, at])
        return 0

    lax.fori_loop(0, 8, body, 0)


def fine_pack(FS, PS, T16):
    half = (lanes((16, 128)) * 2) % 128
    for g in range(4):
        pieces = []
        for k in range(8):
            q = 8 * g + k
            if q >= 30:
                pieces.append(jnp.zeros((16, 128), F32))
                continue
            e, c = q // 5, q % 5
            if e in (2, 3):
                m = FS[e, c, pl.ds(0, 16, 2), :] + FS[e, c, pl.ds(1, 16, 2), :]
            else:
                T16[q, pl.ds(0, 8, 2), :] = FS[e, c, 0:8] + FS[e, c, 8:16]
                T16[q, pl.ds(1, 8, 2), :] = FS[e, c, 16:24] + FS[e, c, 24:32]
                m = T16[q]
            pieces.append(pick(m + roll(m, -1, 1), half))
        outs = block_transpose(pieces, 16)
        for s in range(4):
            PS[s, pl.ds(16 * g, 16), :] = outs[s]


def build_shells(field, sides, planes, PZ):
    shape = (16, 128)
    lane = lanes(shape)
    zeros = jnp.zeros(shape, F32)
    T = [zeros] * 10
    for x in range(16):
        here = lane % 16 == x
        for c in range(5):
            U = field[c, x, 0:16, :]
            turned = roll(U, x, 1)
            T[c] = jnp.where((lane + 1) % 16 == x, turned, T[c])
            T[5 + c] = jnp.where(here, turned, T[5 + c])
    T = [roll(a, 1, 1) for a in T[:5]] + [roll(a, -16, 1) for a in T[5:]]
    z0 = jnp.concatenate(T[:8], axis=0).T
    z1 = jnp.concatenate(T[8:] + [zeros] * 6, axis=0).T
    for zb in range(8):
        PZ[zb, 0:16] = z0[16 * zb : 16 * zb + 16]
    for g in range(1, 4):
        vs = []
        for k in range(8):
            q = 8 * g + k
            vs.append(zeros if q < 10 or q >= 30 else sides[q // 5 - 2][q % 5])
        vs = block_transpose(vs, 16)
        for zb in range(8):
            value = vs[zb]
            if g == 1:
                value = jnp.where(lane < 32, z1[16 * zb : 16 * zb + 16], value)
            PZ[zb, 16 * g : 16 * g + 16] = value


def coarse_step(field, xlo, xhi, ylo, yhi, adv, FP, C, Q, FX):
    for c in range(5):
        for x in range(16):
            C[c, x, 0:16] = field[c, x]
            C[c, x, 16:24] = jnp.broadcast_to(yhi[c, x : x + 1], (8, 128))
        C[c, 16, 0:16] = xhi[c]
        C[c, 16, 16:24] = xhi[c, 8:16]

    def cells(x4, _):
        for x in range(4):
            for k, q in enumerate(primitives([C[c, 4 * x4 + x] for c in range(5)])):
                Q[k, 4 * x4 + x] = q
        return 0

    lax.fori_loop(0, 4, cells, 0)
    for k, q in enumerate(primitives([C[c, 16] for c in range(5)])):
        Q[k, 16] = q
    R = [field[c, 0] for c in range(5)]
    L = [xlo[c] for c in range(5)]
    F = face_flux(L, primitives(L), R, primitives(R), 0)
    for c in range(5):
        FP[2, c] = F[c]
        FX[c] = F[c]
    R = [field[c, :, 0, :] for c in range(5)]
    L = [ylo[c] for c in range(5)]
    F = face_flux(L, primitives(L), R, primitives(R), 1)
    for c in range(5):
        FP[4, c] = F[c]
        FP[0, c] = jnp.zeros((16, 128), F32)
    lane = lanes((16, 128)) % 16
    row = lax.broadcasted_iota(jnp.int32, (16, 128), 0)

    def body(pair, _):
        xs = (2 * pair, 2 * pair + 1, 2 * pair + 2)
        U24 = [[C[c, x] for c in range(5)] for x in xs]
        S24 = [[Q[k, x] for k in range(PRIMS)] for x in xs]
        U = [[a[0:16] for a in As] for As in U24]
        S = [[a[0:16] for a in As] for As in S24]
        below = [FX[c] for c in range(5)]
        corner = [[FP[4, c, pl.ds(x, 1), :] for c in range(5)] for x in xs[:2]]
        zs = [FP[0, c] for c in range(5)]
        results, tops = [], []
        for n in range(2):
            F = face_flux(U[n], S[n], U[n + 1], S[n + 1], 0)
            total = [F[c] - below[c] for c in range(5)]
            below = F
            F = face_flux(
                U[n], S[n], [roll(a, -1, 1) for a in U[n]], [roll(a, -1, 1) for a in S[n]], 2
            )
            for c in range(5):
                zs[c] = jnp.where(lane == xs[n], pltpu.roll(F[c], xs[n] + 1, 1), zs[c])
                total[c] = total[c] + (F[c] - roll(F[c], 1, 1))
            up = [[roll(a, -1, 0)[0:16] for a in As] for As in (U24[n], S24[n])]
            F = face_flux(U[n], S[n], up[0], up[1], 1)
            tops.append([a[15:16] for a in F])
            for c in range(5):
                before = jnp.where(row == 0, corner[n][c], roll(F[c], 1, 0))
                total[c] = total[c] + (F[c] - before)
            results.append([U[n][c] - total[c] for c in range(5)])
        for c in range(5):
            for n in range(2):
                adv[c, xs[n]] = results[n][c]
                FP[5, c, pl.ds(xs[n], 1), :] = tops[n][c]
            FP[0, c] = zs[c]
            FX[c] = below[c]
        return 0

    lax.fori_loop(0, 8, body, 0)
    for c in range(5):
        FP[3, c] = FX[c]
        FP[1, c] = roll(FP[0, c], -16, 1)


def owned_blocks(anchors, counts, me, owners):
    blocks = []
    for o in range(owners):
        block = jnp.int32(-1)
        for s in range(4):
            mine = jnp.logical_and(s < counts[o], anchors[0, s, o] == 16 * me)
            block = jnp.where(mine, anchors[2, s, o] // 16, block)
        blocks.append(block)
    return blocks


def pack_shells(blocks, field, sides, PZ, dense):
    build_shells(field, sides, None, PZ)
    for o, block in enumerate(blocks):
        dense[o] = PZ[jnp.maximum(block, 0)]


class Place:
    def __init__(self):
        self.i, self.j = lax.axis_index("gx"), lax.axis_index("gy")
        self.ni, self.nj = lax.axis_size("gx"), lax.axis_size("gy")

    def along_x(self, d):
        return (lax.rem(self.i + (d + self.ni), self.ni), self.j)

    def along_y(self, d):
        return (self.i, lax.rem(self.j + (d + self.nj), self.nj))

    def greet(self):
        barrier = pltpu.get_barrier_semaphore()
        for d in range(1, self.ni):
            pl.semaphore_signal(barrier, inc=1, device_id=self.along_x(d), device_id_type=MESH)
        for d in (1, -1):
            pl.semaphore_signal(barrier, inc=1, device_id=self.along_y(d), device_id_type=MESH)

    def greeted(self):
        pl.semaphore_wait(pltpu.get_barrier_semaphore(), self.ni + 1)

    def send(self, src, dst, send_sem, recv_sem, to):
        copy = pltpu.make_async_remote_copy(
            src_ref=src,
            dst_ref=dst,
            send_sem=send_sem,
            recv_sem=recv_sem,
            device_id=to,
            device_id_type=MESH,
        )
        copy.start()
        return copy

    def neighbours(self, planes, sides, sems):
        to = (self.along_x(1), self.along_x(-1), self.along_y(1), self.along_y(-1))
        return [
            self.send(planes[k], sides[k], sems.at[0, k], sems.at[1, k], to[k]) for k in range(4)
        ]

    def exchange(self, dense, got, sems):
        got[self.i] = dense[self.i]
        copies = []
        for d in range(1, self.ni):
            to = self.along_x(d)
            copies.append(
                self.send(dense.at[to[0]], got.at[self.i], sems.at[0, d], sems.at[1, d], to)
            )
        return copies


def wait(copies):
    for copy in copies:
        copy.wait()


def edge_planes(field, edges):
    for c in range(5):
        edges[0, c] = field[c, :, 15, :]
        edges[1, c] = field[c, :, 0, :]
    return (field.at[:, 15], field.at[:, 0], edges.at[0], edges.at[1])


def step_kernel(
    anchors_hbm, counts_hbm, patch_hbm, field_hbm, out_field, out, anchors, counts, patch, field, load_sems,
    W, Q, B, S1, S2, FB, FS, FY, PS, C, CQ, FX, adv, FP, PZ,
    dense_old, dense_new, dense_back, got_old, got_new, got_back, edges, D, sides, near_sems, far_sems, T, T16,
):
    place = Place()
    me = place.i

    def chunk(yg):
        at = pl.ds(pl.multiple_of(yg * 128, 128), 128)
        return pltpu.make_async_copy(
            patch_hbm.at[:, :, :, at], patch.at[:, :, :, at], load_sems.at[yg]
        )

    small = [
        pltpu.make_async_copy(field_hbm, field, load_sems.at[8]),
        pltpu.make_async_copy(anchors_hbm, anchors, load_sems.at[9]),
        pltpu.make_async_copy(counts_hbm, counts, load_sems.at[10]),
    ]
    for copy in small:
        copy.start()
    for yg in range(8):
        chunk(yg).start()
    old, new, rims = ([sides.at[n, k] for k in range(4)] for n in range(3))
    place.greet()
    wait(small)
    planes = edge_planes(field, edges.at[0])
    place.greeted()
    near = place.neighbours(planes, old, near_sems.at[0])
    fine_load(patch, W, Q, B, T, lambda yg: chunk(yg).wait())
    count = counts[me]
    sources = [anchors[0, s, me] // 16 for s in range(4)]
    blocks = owned_blocks(anchors, counts, me, place.ni)
    fine_edges(W, FY, B)
    wait(near)
    coarse_step(field, *old, adv, FP, C, CQ, FX)
    planes = edge_planes(adv, edges.at[1])
    near = place.neighbours(planes, new, near_sems.at[1])
    pack_shells(blocks, field, old, PZ, dense_old)
    far_old = place.exchange(dense_old, got_old, far_sems.at[0])
    wait(near)
    pack_shells(blocks, adv, new, PZ, dense_new)
    far_new = place.exchange(dense_new, got_new, far_sems.at[1])
    fine_interior(W, Q, FY, 0, 32)
    wait(far_old)
    fine_shells(got_old, sources, S1, T16)
    fine_boundary(B, Q, S1, FB, FS, True)
    add_boundary(W, FB)
    fine_again(W, FB, Q, B)
    fine_edges(W, FY, B)
    wait(far_new)
    fine_shells(got_old, sources, S2, T16, got_new)
    fine_boundary(B, Q, S2, FB, FS, False)
    fine_pack(FS, PS, T16)
    for i in range(place.ni):
        slot = jnp.int32(0)
        for s in range(1, 4):
            slot = jnp.where(jnp.logical_and(s < count, sources[s] == i), s, slot)
        dense_back[i] = PS[slot]
    back = place.exchange(dense_back, got_back, far_sems.at[2])
    fine_interior(W, Q, FY, 0, 28)
    wait(back)
    reflux(blocks, adv, FP, got_back, out_field, D)
    near = place.neighbours([D.at[1], D.at[0], D.at[3], D.at[2]], rims, near_sems.at[2])
    fine_interior(W, Q, FY, 28, 32)
    add_boundary(W, FB)
    fine_store(W, FB, patch, count, out, T)
    wait(near)
    for c in range(5):
        out_field[c, 0] = out_field[c, 0] + sides[2, 0, c]
        out_field[c, 15] = out_field[c, 15] + sides[2, 1, c]
        out_field[c, :, 0, :] = out_field[c, :, 0, :] + sides[2, 2, c]
        out_field[c, :, 15, :] = out_field[c, :, 15, :] + sides[2, 3, c]


def write_kernel(field, patch, out_field, out, sems):
    copies = [
        pltpu.make_async_copy(patch, out, sems.at[0]),
        pltpu.make_async_copy(field, out_field, sems.at[1]),
    ]
    for copy in copies:
        copy.start()
    wait(copies)


def reflux(blocks, adv, FP, got, out, D):
    shape = (16, 128)
    lane = lanes(shape)
    owner = [jnp.int32(0)] * 8
    present = [jnp.int32(0)] * 8
    for o, block in enumerate(blocks):
        for zb in range(8):
            owner[zb] = jnp.where(block == zb, o, owner[zb])
            present[zb] = jnp.where(block == zb, 1, present[zb])
    live = jnp.zeros(shape, jnp.int32)
    for zb in range(8):
        live = jnp.where(lane // 16 == zb, present[zb], live)
    live = live > 0
    delta = {}
    for g in range(4):
        vs = [got[owner[zb], pl.ds(16 * g, 16), :] for zb in range(8)]
        if g < 2:
            turned = jnp.concatenate(vs, axis=0).T
        if g > 0:
            vs = block_transpose(vs, 16)
        for k in range(8):
            q = 8 * g + k
            if q < 30:
                e, c = q // 5, q % 5
                mean = 0.125 * (turned[16 * k : 16 * k + 16] if q < 10 else vs[k])
                value = FP[e, c] - mean if e % 2 == 0 else mean - FP[e, c]
                value = jnp.where(live, value, 0.0)
                if e < 2:
                    delta[e, c] = value
                else:
                    D[e - 2, c] = value
    column = lane % 16
    for c in range(5):
        lower, upper = roll(delta[0, c], -1, 1), roll(delta[1, c], 16, 1)
        for x in range(16):
            both = jnp.where((column + 1) % 16 == x, lower, 0.0)
            out[c, x] = adv[c, x] + roll(jnp.where(column == x, upper, both), -x, 1)


def call(kernel, outs, n_in, spaces, scratch=(), collective=None):
    more = {}
    if collective is not None:
        more = {"collective_id": collective, "has_side_effects": True}
    return pl.pallas_call(
        kernel,
        out_shape=[jax.ShapeDtypeStruct(shape, F32) for shape in outs],
        in_specs=[pl.BlockSpec(memory_space=spaces[0])] * n_in,
        out_specs=[pl.BlockSpec(memory_space=spaces[1])] * len(outs),
        scratch_shapes=[pltpu.VMEM(s, F32) if isinstance(s, tuple) else s for s in scratch],
        compiler_params=pltpu.CompilerParams(vmem_limit_bytes=VMEM_LIMIT, **more),
        cost_estimate=pl.CostEstimate(flops=10000000, bytes_accessed=4000000, transcendentals=0),
    )


def shards(coarse_state, patch_state, patch_anchor, patch_count):
    owners = lax.axis_size("gx")
    anchors = jnp.transpose(patch_anchor[:, 0], (2, 1, 0))
    counts = patch_count.reshape(-1)
    patch = patch_state.reshape(4, 5, 32, 1024)
    cube = (5, 32, 32, 128)
    prim = (PRIMS, 32, 32, 128)
    planes = (6, 5, 32, 128)
    field = (5, 16, 16, 128)
    side = (5, 16, 128)
    dense = (owners, 64, 128)
    dma = pltpu.SemaphoreType.DMA

    results = [field, (4, 5, 32, 1024)]
    made = call(
        step_kernel,
        results,
        4,
        (pltpu.HBM, pltpu.VMEM),
        [pltpu.SMEM((3, 4, owners), jnp.int32), pltpu.SMEM((owners,), jnp.int32)]
        + [(4, 5, 32, 1024), field, dma((11,)), cube, prim] + [planes] * 5 + [(5, 32, 128), (4, 64, 128)]
        + [(5, 17, 24, 128), (PRIMS, 17, 24, 128), side, field, (6,) + side, (8, 64, 128)]
        + [dense] * 6
        + [(2, 2) + side, (4,) + side, (3, 4) + side, dma((3, 2, 4)), dma((3, 2, owners)), (5, 4, 32, 128), (30, 16, 128)],
        0,
    )(*(pltpu.with_memory_space_constraint(a, pltpu.HBM) for a in (anchors, counts, patch, coarse_state)))
    made = (pltpu.with_memory_space_constraint(a, pltpu.VMEM) for a in made)
    coarse_next, out = call(write_kernel, results, 2, (pltpu.VMEM, pltpu.HBM), [dma((2,))])(*made)
    return (coarse_next, out.reshape(patch_state.shape))


def solution(mesh):
    in_specs = (
        P(None, "gx", "gy", None),
        P("gx", "gy", None, None, None, None),
        P(None, "gy", None, None),
        P(None, "gy"),
    )
    out_specs = (P(None, "gx", "gy", None), P("gx", "gy", None, None, None, None))
    return jax.shard_map(shards, mesh=mesh, in_specs=in_specs, out_specs=out_specs, check_vma=False)
```
